32 devices in a mesh: lat: 8 (over z, x), azim: 4 (over y, core).
Axes of the slice: x: 2, y: 2, z: 4, core: 2. Of those that a mesh axis runs over, the one named last changes fastest.
Arguments:
- magnetic: float32 [3, 32, 256, 2048], P(None, None, 'lat', 'azim'), may hold values from -6 to 6
- kept_modes: int32 [256], replicated, may hold values from 1 to 1024, as said below
Outputs:
- current_density: float32 [3, 32, 256, 2048], P(None, None, 'lat', 'azim')
The draws below stay inside these ranges and needn't reach their ends.
Inputs may be any that keep to these rules, and one draw needn't show every extreme that they name: `kept_modes`: at latitude 256 // 2 all 1024 modes are kept.
All inputs are finite; a program needn't handle non-finite values.
Results may differ from the reference program's by a relative error of at most 0.000068.
Values sent between devices are 32-bit elements; how exact they have to be, the bound alone decides.
No kernel may reach another device: no remote copies, remote signals or barrier semaphores. Data moves between devices by JAX's collectives and lax.ppermute only.
A program may use at most 64 MiB of HBM per device.

```python
import math
import jax
import jax.numpy as jnp
from jax import lax

LONGITUDE_COUNT = 2048
RADII = 32
NTH = 256


def draw_kept_modes(key, part):
    lat_ids = jnp.arange(NTH, dtype=jnp.int32)
    nearest = jnp.minimum(lat_ids, NTH - 1 - lat_ids)
    base_count = jnp.maximum(1, LONGITUDE_COUNT // 2 * 2 * nearest // NTH)
    jitter = jax.random.randint(jax.random.fold_in(key, 1), (NTH,), 0, 1 << 20, dtype=jnp.int32) % (base_count // 2 + 1)
    tally_counts = jnp.maximum(1, base_count - jitter)
    half_places = max(1, NTH // 512)
    polar_reach = max(1, NTH // 8)
    north = jax.random.randint(jax.random.fold_in(key, 2), (half_places,), 0, polar_reach, dtype=jnp.int32)
    south = NTH - 1 - jax.random.randint(jax.random.fold_in(key, 3), (half_places,), 0, polar_reach, dtype=jnp.int32)
    spots = jnp.concatenate([north, south])
    flurry_counts = jax.random.randint(jax.random.fold_in(key, 4), (2 * half_places,), LONGITUDE_COUNT // 4, LONGITUDE_COUNT // 2 + 1, dtype=jnp.int32)
    matched_flag = lat_ids[:, None] == spots[None, :]
    flurry_local = jnp.max(jnp.where(matched_flag, flurry_counts[None, :], 0), axis=1)
    tally_counts = jnp.where(flurry_local > 0, flurry_local, tally_counts)
    return jnp.where(lat_ids == NTH // 2, LONGITUDE_COUNT // 2, tally_counts).astype(jnp.int32)


def levels(own_key, dims, split, low, high):
    level = 1.0
    for position, shards_of in split:
        steps = jax.random.uniform(jax.random.fold_in(jax.random.fold_in(own_key, 6), position), (shards_of,), jnp.float32, low / len(split), high / len(split))
        level = level * jnp.repeat(jnp.exp(steps), dims[position] // shards_of).reshape((-1,) + (1,) * (len(dims) - 1 - position))
    return level


def scatter_about(key, dims, scale, most, split=(), held_as=jnp.bfloat16):
    gain = levels(key, dims, split, -0.22, 0.18) if split else 1.0
    drawn = jax.random.normal(key, dims, jnp.float32) * scale * gain
    return jnp.minimum(jnp.maximum(drawn, -most), most).astype(held_as)


def setup_inputs(seed: int = 0) -> dict:
    arg_keys = jax.random.split(jax.random.key(seed), 3)
    return {
        "magnetic": scatter_about(arg_keys[0], (3, RADII, NTH, LONGITUDE_COUNT), 1.0, 6.0, ((2, 8), (3, 4)), jnp.float32),
        "kept_modes": draw_kept_modes(jax.random.fold_in(arg_keys[2], 71), 0),
    }


inner_radius = 0.7
stencil_coeffs = (-1.0 / 60.0, 3.0 / 20.0, -3.0 / 4.0, 0.0, 3.0 / 4.0, -3.0 / 20.0, 1.0 / 60.0)


def central_diff(values, split_axis):
    length = values.shape[split_axis]
    widths = [(0, 0)] * values.ndim
    widths[split_axis] = (3, 3)
    padded = jnp.pad(values, widths)
    total = jnp.zeros_like(values)
    for offset in range(-3, 4):
        if offset != 0:
            total = total + stencil_coeffs[offset + 3] * lax.slice_in_dim(padded, 3 + offset, 3 + offset + length, axis=split_axis)
    return total


def reference(magnetic, kept_modes):
    spacing = math.pi / NTH
    colatitude = (jnp.arange(NTH, dtype=jnp.float32) + 0.5) * spacing
    radius = inner_radius + (jnp.arange(RADII, dtype=jnp.float32) + 0.5) * spacing
    radius = radius[:, None, None]
    inv_sin = (1.0 / jnp.sin(colatitude))[None, :, None]
    cotangent = (jnp.cos(colatitude) / jnp.sin(colatitude))[None, :, None]
    b_radial = magnetic[0]
    b_polar = magnetic[1]
    b_azim = magnetic[2]
    spectrum = jnp.fft.rfft(magnetic[:2], axis=-1)
    mode_ids = jnp.arange(LONGITUDE_COUNT // 2 + 1, dtype=jnp.int32)
    keep = mode_ids[None, :] < kept_modes[:, None]
    factor = jnp.where(keep, mode_ids[None, :], 0).astype(jnp.float32)
    azimuthal = jnp.fft.irfft(1j * factor[None, None, :, :] * spectrum, n=LONGITUDE_COUNT, axis=-1).astype(jnp.float32)
    j_radial = (central_diff(b_azim, 1) + spacing * cotangent * b_azim - spacing * inv_sin * azimuthal[1]) / radius
    j_polar = (spacing * inv_sin * azimuthal[0] - central_diff(radius * b_azim, 0)) / radius
    j_azim = (central_diff(radius * b_polar, 0) - central_diff(b_radial, 1)) / radius
    return jnp.stack([j_radial, j_polar, j_azim])
```

```python
import functools
import math

import jax
import jax.numpy as jnp
import numpy as np
from jax import lax
from jax.experimental import pallas as pl
from jax.experimental.pallas import tpu as pltpu
from jax.sharding import PartitionSpec as P

MB = 128


inner_radius = 0.7
stencil_coeffs = (-1.0 / 60.0, 3.0 / 20.0, -3.0 / 4.0, 0.0, 3.0 / 4.0, -3.0 / 20.0, 1.0 / 60.0)


def extended(value, sides, width):
    for axis, dim in sides:
        size, length = (lax.axis_size(axis), value.shape[dim])
        up = [(i, (i + 1) % size) for i in range(size - 1)]
        down = [(j, i) for i, j in up]
        last = lax.slice_in_dim(value, length - width, length, axis=dim)
        first = lax.slice_in_dim(value, 0, width, axis=dim)
        before = lax.ppermute(last, axis, up)
        after = lax.ppermute(first, axis, down)
        value = jnp.concatenate([before, value, after], axis=dim)
    return value


def stencil_sum(padded, split_axis, length):
    total = jnp.zeros(lax.slice_in_dim(padded, 3, 3 + length, axis=split_axis).shape, jnp.float32)
    for offset in range(-3, 4):
        if offset != 0:
            total = total + stencil_coeffs[offset + 3] * lax.slice_in_dim(
                padded, 3 + offset, 3 + offset + length, axis=split_axis
            )
    return total


def radial_diff(values):
    widths = [(0, 0)] * values.ndim
    widths[0] = (3, 3)
    return stencil_sum(jnp.pad(values, widths), 0, values.shape[0])


def row_counts(band_counts, row_lat):
    lat_ids = jnp.arange(band_counts.shape[0], dtype=jnp.int32)
    match = row_lat[:, None] == lat_ids[None, :]
    return jnp.sum(jnp.where(match, band_counts[None, :], 0), axis=1)


def base_tables(lon_total):
    columns = jnp.arange(lon_total, dtype=jnp.int32)
    mode_ids = jnp.arange(MB, dtype=jnp.int32)
    phase = (mode_ids[:, None] * columns[None, :] % lon_total).astype(jnp.float32) * (
        2.0 * math.pi / lon_total
    )
    return (jnp.cos(phase), jnp.sin(phase))


def spectral(row_data, row_kept, base_cos, base_sin):
    lon_total = row_data.shape[1]
    block_count = (jnp.max(row_kept) + MB - 1) // MB
    columns = jnp.arange(lon_total, dtype=jnp.int32)

    def block_step(block, total):
        mode_ids = block * MB + jnp.arange(MB, dtype=jnp.int32)
        offset_phase = (block * MB * columns % lon_total).astype(jnp.float32) * (
            2.0 * math.pi / lon_total
        )
        offset_cos = jnp.cos(offset_phase)[None, :]
        offset_sin = jnp.sin(offset_phase)[None, :]
        cos_rows = base_cos * offset_cos - base_sin * offset_sin
        sin_rows = base_sin * offset_cos + base_cos * offset_sin
        table = jnp.concatenate([cos_rows, sin_rows], axis=0)
        spectrum = lax.dot_general(
            row_data,
            table,
            (((1,), (1,)), ((), ())),
            precision=lax.Precision.HIGHEST,
            preferred_element_type=jnp.float32,
        )
        weight = jnp.where(mode_ids[None, :] < row_kept[:, None], mode_ids[None, :], 0).astype(
            jnp.float32
        ) * (2.0 / lon_total)
        scaled = jnp.concatenate([spectrum[:, MB:] * weight, -spectrum[:, :MB] * weight], axis=1)
        return total + jnp.dot(
            scaled, table, precision=lax.Precision.HIGHEST, preferred_element_type=jnp.float32
        )

    return lax.fori_loop(0, block_count, block_step, jnp.zeros_like(row_data))


def band_geometry(th_dev):
    lat_total = th_dev * lax.axis_size("lat")
    spacing = math.pi / lat_total
    band_start = lax.axis_index("lat") * th_dev
    colatitude = (
        (band_start + jnp.arange(th_dev, dtype=jnp.int32)).astype(jnp.float32) + 0.5
    ) * spacing
    return spacing, band_start, colatitude


def on_device(magnetic, kept_modes):
    radii_count, th_dev, ph_dev = (magnetic.shape[1], magnetic.shape[2], magnetic.shape[3])
    spacing, band_start, colatitude = band_geometry(th_dev)
    radius = (inner_radius + (jnp.arange(radii_count, dtype=jnp.float32) + 0.5) * spacing)[
        :, None, None
    ]
    inv_sin = (1.0 / jnp.sin(colatitude))[None, :, None]
    cotangent = (jnp.cos(colatitude) / jnp.sin(colatitude))[None, :, None]
    band_counts = lax.dynamic_slice_in_dim(kept_modes, band_start, th_dev)
    theta_pair = jnp.stack([magnetic[0], magnetic[2]])
    padded = extended(theta_pair, (("lat", 2),), 3)
    theta_diff = stencil_sum(padded, 2, th_dev)
    row_data = magnetic[:2].reshape(2 * radii_count * th_dev, ph_dev)
    lined = lax.all_to_all(row_data, "azim", split_axis=0, concat_axis=1, tiled=True)
    base_cos, base_sin = base_tables(lined.shape[1])
    rows_here = lined.shape[0]
    row_start = lax.axis_index("azim") * rows_here
    row_lat = (row_start + jnp.arange(rows_here, dtype=jnp.int32)) % th_dev
    row_kept = row_counts(band_counts, row_lat)
    azimuthal = spectral(lined, row_kept, base_cos, base_sin)
    flat_rows = lax.all_to_all(azimuthal, "azim", split_axis=1, concat_axis=0, tiled=True)
    azim_diff = flat_rows.reshape(2, radii_count, th_dev, ph_dev)
    b_polar = magnetic[1]
    b_azim = magnetic[2]
    j_radial = (
        theta_diff[1] + spacing * cotangent * b_azim - spacing * inv_sin * azim_diff[1]
    ) / radius
    j_polar = (spacing * inv_sin * azim_diff[0] - radial_diff(radius * b_azim)) / radius
    j_azim = (radial_diff(radius * b_polar) - theta_diff[0]) / radius
    return jnp.stack([j_radial, j_polar, j_azim])


CHUNKS = 2
TO_Y = [(0, 2), (2, 0), (1, 3), (3, 1)]
TO_C = [(0, 1), (1, 0), (2, 3), (3, 2)]
TO_YC = [(0, 3), (3, 0), (1, 2), (2, 1)]
VMEM = 60 * 1024 * 1024


def halves(table):
    high = table.astype(jnp.bfloat16)
    low = (table - high.astype(np.float64)).astype(jnp.bfloat16)
    return np.stack([high, low])


def mode_tables(lon_total):
    quarter = lon_total // 4

    def pair(modes, length):
        phase = (np.arange(length)[:, None] * modes[None, :] % lon_total) * (2.0 * np.pi / lon_total)
        forward = np.concatenate([np.cos(phase), np.sin(phase)], axis=1)
        inverse = np.concatenate([-np.sin(phase), np.cos(phase)], axis=1).T
        return halves(forward), halves(inverse)

    zero = 4 * np.arange(quarter // 2)
    two = zero + 2
    odd = 2 * np.arange(quarter) + 1
    mode_ids = np.concatenate([zero, zero, two, two, odd, odd]).astype(np.float32)[None, :]
    return pair(zero, quarter), pair(two, quarter), pair(odd, 2 * quarter), mode_ids


def triple_dot(value, table):
    high = value.astype(jnp.bfloat16)
    low = (value - high.astype(jnp.float32)).astype(jnp.bfloat16)
    dot = functools.partial(jnp.dot, preferred_element_type=jnp.float32)
    return dot(high, table[0]) + dot(high, table[1]) + dot(low, table[0])


def transform_kernel(
    place, own, across, beside, diagonal, kept, modes, f0, f2, f1, i0, i2, i1, out_own, out_across, out_beside, out_diagonal
):
    quarter = own.shape[-1]
    rows = own.shape[-2] * own.shape[-3]
    sign_y = (1 - 2 * place[0]).astype(jnp.float32)
    sign_c = (1 - 2 * place[1]).astype(jnp.float32)
    first = place[1] == 0
    a, b, c, d = (ref[...].reshape(rows, quarter) for ref in (own, across, beside, diagonal))
    near, far = a + b, c + d
    near_odd, far_odd = sign_y * (a - b), sign_y * (c - d)
    odd = jnp.concatenate([jnp.where(first, near_odd, far_odd), jnp.where(first, far_odd, near_odd)], axis=1)
    limit = kept[...]
    ids = modes[...]
    weight = jnp.where(ids < limit, ids, 0.0) * (0.5 / quarter)

    def filtered(value, forward, inverse, start):
        spectrum = triple_dot(value, forward)
        return triple_dot(spectrum * weight[:, start : start + spectrum.shape[1]], inverse)

    even0 = filtered(near + far, f0, i0, 0)
    even2 = sign_c * filtered(sign_c * (near - far), f2, i2, quarter)
    odd_out = sign_y * filtered(odd, f1, i1, 2 * quarter)
    left, right = odd_out[:, :quarter], odd_out[:, quarter:]
    odd_near, odd_far = jnp.where(first, left, right), jnp.where(first, right, left)
    even_near, even_far = even0 + even2, even0 - even2
    shape = out_own.shape
    out_own[...] = (even_near + odd_near).reshape(shape)
    out_across[...] = (even_near - odd_near).reshape(shape)
    out_beside[...] = (even_far + odd_far).reshape(shape)
    out_diagonal[...] = (even_far - odd_far).reshape(shape)


def transform(place, magnetic, start, across, beside, beside_start, diagonal, kept_rows, tables):
    depth, th_dev, quarter = across.shape
    zero, two, odd, mode_ids = tables
    whole = pl.BlockSpec(memory_space=pltpu.VMEM)
    rows = depth * th_dev
    half = magnetic.shape[1] // 2
    grid_spec = pltpu.PrefetchScalarGridSpec(
        num_scalar_prefetch=1,
        grid=(1,),
        in_specs=[
            pl.BlockSpec((None, depth, th_dev, quarter), lambda i, p: (p[1], p[0] * (half // depth) + start // depth, 0, 0)),
            whole,
            pl.BlockSpec((depth, th_dev, quarter), lambda i, p: (beside_start // depth, 0, 0)),
            whole,
        ]
        + [whole] * 8,
        out_specs=[whole] * 4,
    )
    flops = 2 * 3 * 2 * rows * 6 * quarter * quarter
    return pl.pallas_call(
        transform_kernel,
        grid_spec=grid_spec,
        out_shape=[jax.ShapeDtypeStruct((depth, th_dev, quarter), jnp.float32)] * 4,
        compiler_params=pltpu.CompilerParams(vmem_limit_bytes=VMEM),
        cost_estimate=pl.CostEstimate(flops=flops, bytes_accessed=48 * quarter * quarter, transcendentals=0),
    )(place, magnetic, across, beside, diagonal, kept_rows, mode_ids, zero[0], two[0], odd[0], zero[1], two[1], odd[1])


def diff_along(padded, axis, length):
    total = None
    for offset in range(-3, 4):
        if offset != 0:
            term = stencil_coeffs[offset + 3] * lax.slice_in_dim(padded, 3 + offset, 3 + offset + length, axis=axis)
            total = term if total is None else total + term
    return total


def local_kernel(field, before, after, radius, inv_radius, cot, out):
    radii, th_dev, width = field.shape[1:]
    rad, inv = radius[...], inv_radius[...]
    edge = jnp.zeros((3, th_dev, width), jnp.float32)

    def theta(value, which):
        return diff_along(jnp.concatenate([before[which], value, after[which]], axis=1), 1, th_dev)

    def radial(value):
        return diff_along(jnp.concatenate([edge, rad * value, edge], axis=0), 0, radii)

    b_azim = field[2]
    out[0] = (theta(b_azim, 1) + cot[...] * b_azim) * inv
    out[1] = -radial(b_azim) * inv
    out[2] = (radial(field[1]) - theta(field[0], 0)) * inv


def local_part(magnetic, before, after, radius, inv_radius, cot):
    width = 128
    radii, th_dev, ph_dev = magnetic.shape[1:]
    fixed = lambda *shape: pl.BlockSpec(shape, lambda i: (0, 0, 0))
    wide = lambda *lead: pl.BlockSpec(lead + (width,), lambda i: (0, 0, 0, i))
    return pl.pallas_call(
        local_kernel,
        grid=(ph_dev // width,),
        in_specs=[
            wide(3, radii, th_dev),
            wide(2, radii, 3),
            wide(2, radii, 3),
            fixed(radii, 1, 1),
            fixed(radii, 1, 1),
            fixed(1, th_dev, 1),
        ],
        out_specs=wide(3, radii, th_dev),
        out_shape=jax.ShapeDtypeStruct(magnetic.shape, jnp.float32),
        compiler_params=pltpu.CompilerParams(vmem_limit_bytes=VMEM),
        cost_estimate=pl.CostEstimate(flops=60 * magnetic.size, bytes_accessed=8 * magnetic.size, transcendentals=0),
    )(magnetic, before, after, radius, inv_radius, cot)


def add_kernel(place, base, azim, scale, out):
    out[...] = base[...] + azim[...] * scale[...]


def add_azim(place, current, azim, part, start, field_of, half_of, scale):
    depth, th_dev, ph_dev = azim.shape
    half = current.shape[1] // 2
    at = lambda i, p: (1 - field_of(p), half_of(p) * (half // depth) + start // depth, 0, 0)
    block = pl.BlockSpec((None, depth, th_dev, ph_dev), at)
    return pl.pallas_call(
        add_kernel,
        grid_spec=pltpu.PrefetchScalarGridSpec(
            num_scalar_prefetch=1,
            grid=(1,),
            in_specs=[
                block,
                pl.BlockSpec((depth, th_dev, ph_dev), lambda i, p: (0, 0, 0)),
                pl.BlockSpec((None, depth, th_dev, 1), lambda i, p: (field_of(p), half_of(p) * (half // depth) + start // depth, 0, 0)),
            ],
            out_specs=block,
        ),
        out_shape=jax.ShapeDtypeStruct(current.shape, jnp.float32),
        input_output_aliases={1: 0},
        compiler_params=pltpu.CompilerParams(vmem_limit_bytes=VMEM),
        cost_estimate=pl.CostEstimate(flops=2 * azim.size, bytes_accessed=12 * azim.size, transcendentals=0),
    )(place, current, azim, scale)


def on_four(magnetic, kept_modes):
    radii, th_dev, ph_dev = (magnetic.shape[1], magnetic.shape[2], magnetic.shape[3])
    half = radii // 2
    depth = half // CHUNKS
    index = lax.axis_index("azim")
    y, c = index // 2, index % 2
    place = jnp.stack([y, c]).astype(jnp.int32)
    send = lambda value, pairs: lax.ppermute(value, "azim", pairs)

    def cut(field, start, length):
        return lax.dynamic_slice(magnetic, (field, start, 0, 0), (1, length, th_dev, ph_dev))[0]

    across, diagonal = [], []
    for k in range(CHUNKS):
        across.append(send(cut(c, (1 - y) * half + k * depth, depth), TO_Y))
        diagonal.append(send(cut(1 - c, (1 - y) * half + k * depth, depth), TO_YC))
        if k == 0:
            beside = send(cut(1 - c, y * half, half), TO_C)

    spacing, band_start, colatitude = band_geometry(th_dev)
    radius = (inner_radius + (jnp.arange(radii, dtype=jnp.float32) + 0.5) * spacing)[:, None, None]
    inv_radius = 1.0 / radius
    inv_sin = (1.0 / jnp.sin(colatitude))[None, :, None]
    cot = spacing * (jnp.cos(colatitude) / jnp.sin(colatitude))[None, :, None]
    scale = spacing * inv_sin * inv_radius
    scale = jnp.stack([scale, -scale])
    band_counts = lax.dynamic_slice_in_dim(kept_modes, band_start, th_dev).astype(jnp.float32)
    kept_rows = jnp.broadcast_to(band_counts[None, :, None], (depth, th_dev, 1)).reshape(depth * th_dev, 1)

    lat_size = lax.axis_size("lat")
    up = [(i, i + 1) for i in range(lat_size - 1)]
    down = [(i + 1, i) for i in range(lat_size - 1)]
    before = lax.ppermute(magnetic[0::2, :, th_dev - 3 :], "lat", up)
    after = lax.ppermute(magnetic[0::2, :, :3], "lat", down)
    current = local_part(magnetic, before, after, radius, inv_radius, cot)

    tables = mode_tables(4 * ph_dev)
    back = []
    for k in range(CHUNKS):
        mine, to_y, to_c, to_yc = transform(
            place, magnetic, k * depth, across[k], beside, k * depth, diagonal[k], kept_rows, tables
        )
        back.append((mine, send(to_y, TO_Y), send(to_yc, TO_YC), send(to_c, TO_C)))
    for k, (mine, from_y, from_yc, from_c) in enumerate(back):
        own_field, other_field = lambda p: p[1], lambda p: 1 - p[1]
        own_half, other_half = lambda p: p[0], lambda p: 1 - p[0]
        for azim, field_of, half_of in (
            (mine, own_field, own_half),
            (from_c, other_field, own_half),
            (from_y, own_field, other_half),
            (from_yc, other_field, other_half),
        ):
            current = add_azim(place, current, azim, k, k * depth, field_of, half_of, scale)
    return current


def solution(mesh):
    placed = (P(None, None, "lat", "azim"), P())

    def run(magnetic, kept_modes):
        radii, ph_dev = magnetic.shape[1], magnetic.shape[3]
        four = lax.axis_size("azim") == 4 and radii % (2 * CHUNKS) == 0 and ph_dev % 256 == 0
        return (on_four if four else on_device)(magnetic, kept_modes)

    return jax.shard_map(
        run,
        mesh=mesh,
        in_specs=placed,
        out_specs=P(None, None, "lat", "azim"),
        check_vma=False,
    )
```

```python
import functools
import math

import jax
import jax.numpy as jnp
import numpy as np
from jax import lax
from jax.experimental import pallas as pl
from jax.experimental.pallas import tpu as pltpu
from jax.sharding import PartitionSpec as P

MB = 128


inner_radius = 0.7
stencil_coeffs = (-1.0 / 60.0, 3.0 / 20.0, -3.0 / 4.0, 0.0, 3.0 / 4.0, -3.0 / 20.0, 1.0 / 60.0)


def extended(value, sides, width):
    for axis, dim in sides:
        size, length = (lax.axis_size(axis), value.shape[dim])
        up = [(i, (i + 1) % size) for i in range(size - 1)]
        down = [(j, i) for i, j in up]
        last = lax.slice_in_dim(value, length - width, length, axis=dim)
        first = lax.slice_in_dim(value, 0, width, axis=dim)
        before = lax.ppermute(last, axis, up)
        after = lax.ppermute(first, axis, down)
        value = jnp.concatenate([before, value, after], axis=dim)
    return value


def stencil_sum(padded, split_axis, length):
    total = jnp.zeros(lax.slice_in_dim(padded, 3, 3 + length, axis=split_axis).shape, jnp.float32)
    for offset in range(-3, 4):
        if offset != 0:
            total = total + stencil_coeffs[offset + 3] * lax.slice_in_dim(
                padded, 3 + offset, 3 + offset + length, axis=split_axis
            )
    return total


def radial_diff(values):
    widths = [(0, 0)] * values.ndim
    widths[0] = (3, 3)
    return stencil_sum(jnp.pad(values, widths), 0, values.shape[0])


def row_counts(band_counts, row_lat):
    lat_ids = jnp.arange(band_counts.shape[0], dtype=jnp.int32)
    match = row_lat[:, None] == lat_ids[None, :]
    return jnp.sum(jnp.where(match, band_counts[None, :], 0), axis=1)


def base_tables(lon_total):
    columns = jnp.arange(lon_total, dtype=jnp.int32)
    mode_ids = jnp.arange(MB, dtype=jnp.int32)
    phase = (mode_ids[:, None] * columns[None, :] % lon_total).astype(jnp.float32) * (
        2.0 * math.pi / lon_total
    )
    return (jnp.cos(phase), jnp.sin(phase))


def spectral(row_data, row_kept, base_cos, base_sin):
    lon_total = row_data.shape[1]
    block_count = (jnp.max(row_kept) + MB - 1) // MB
    columns = jnp.arange(lon_total, dtype=jnp.int32)

    def block_step(block, total):
        mode_ids = block * MB + jnp.arange(MB, dtype=jnp.int32)
        offset_phase = (block * MB * columns % lon_total).astype(jnp.float32) * (
            2.0 * math.pi / lon_total
        )
        offset_cos = jnp.cos(offset_phase)[None, :]
        offset_sin = jnp.sin(offset_phase)[None, :]
        cos_rows = base_cos * offset_cos - base_sin * offset_sin
        sin_rows = base_sin * offset_cos + base_cos * offset_sin
        table = jnp.concatenate([cos_rows, sin_rows], axis=0)
        spectrum = lax.dot_general(
            row_data,
            table,
            (((1,), (1,)), ((), ())),
            precision=lax.Precision.HIGHEST,
            preferred_element_type=jnp.float32,
        )
        weight = jnp.where(mode_ids[None, :] < row_kept[:, None], mode_ids[None, :], 0).astype(
            jnp.float32
        ) * (2.0 / lon_total)
        scaled = jnp.concatenate([spectrum[:, MB:] * weight, -spectrum[:, :MB] * weight], axis=1)
        return total + jnp.dot(
            scaled, table, precision=lax.Precision.HIGHEST, preferred_element_type=jnp.float32
        )

    return lax.fori_loop(0, block_count, block_step, jnp.zeros_like(row_data))


def band_geometry(th_dev):
    lat_total = th_dev * lax.axis_size("lat")
    spacing = math.pi / lat_total
    band_start = lax.axis_index("lat") * th_dev
    colatitude = (
        (band_start + jnp.arange(th_dev, dtype=jnp.int32)).astype(jnp.float32) + 0.5
    ) * spacing
    return spacing, band_start, colatitude


def on_device(magnetic, kept_modes):
    radii_count, th_dev, ph_dev = (magnetic.shape[1], magnetic.shape[2], magnetic.shape[3])
    spacing, band_start, colatitude = band_geometry(th_dev)
    radius = (inner_radius + (jnp.arange(radii_count, dtype=jnp.float32) + 0.5) * spacing)[
        :, None, None
    ]
    inv_sin = (1.0 / jnp.sin(colatitude))[None, :, None]
    cotangent = (jnp.cos(colatitude) / jnp.sin(colatitude))[None, :, None]
    band_counts = lax.dynamic_slice_in_dim(kept_modes, band_start, th_dev)
    theta_pair = jnp.stack([magnetic[0], magnetic[2]])
    padded = extended(theta_pair, (("lat", 2),), 3)
    theta_diff = stencil_sum(padded, 2, th_dev)
    row_data = magnetic[:2].reshape(2 * radii_count * th_dev, ph_dev)
    lined = lax.all_to_all(row_data, "azim", split_axis=0, concat_axis=1, tiled=True)
    base_cos, base_sin = base_tables(lined.shape[1])
    rows_here = lined.shape[0]
    row_start = lax.axis_index("azim") * rows_here
    row_lat = (row_start + jnp.arange(rows_here, dtype=jnp.int32)) % th_dev
    row_kept = row_counts(band_counts, row_lat)
    azimuthal = spectral(lined, row_kept, base_cos, base_sin)
    flat_rows = lax.all_to_all(azimuthal, "azim", split_axis=1, concat_axis=0, tiled=True)
    azim_diff = flat_rows.reshape(2, radii_count, th_dev, ph_dev)
    b_polar = magnetic[1]
    b_azim = magnetic[2]
    j_radial = (
        theta_diff[1] + spacing * cotangent * b_azim - spacing * inv_sin * azim_diff[1]
    ) / radius
    j_polar = (spacing * inv_sin * azim_diff[0] - radial_diff(radius * b_azim)) / radius
    j_azim = (radial_diff(radius * b_polar) - theta_diff[0]) / radius
    return jnp.stack([j_radial, j_polar, j_azim])


CHUNKS = 2
TO_Y = [(0, 2), (2, 0), (1, 3), (3, 1)]
TO_C = [(0, 1), (1, 0), (2, 3), (3, 2)]
TO_YC = [(0, 3), (3, 0), (1, 2), (2, 1)]
VMEM = 60 * 1024 * 1024


def halves(table):
    high = table.astype(jnp.bfloat16)
    low = (table - high.astype(np.float64)).astype(jnp.bfloat16)
    return np.stack([high, low])


def mode_tables(lon_total):
    quarter = lon_total // 4

    def pair(modes, length):
        phase = (np.arange(length)[:, None] * modes[None, :] % lon_total) * (2.0 * np.pi / lon_total)
        forward = np.concatenate([np.cos(phase), np.sin(phase)], axis=1)
        inverse = np.concatenate([-np.sin(phase), np.cos(phase)], axis=1).T
        return halves(forward), halves(inverse)

    zero = 4 * np.arange(quarter // 2)
    two = zero + 2
    odd = 2 * np.arange(quarter) + 1
    mode_ids = np.concatenate([zero, zero, two, two, odd, odd]).astype(np.float32)[None, :]
    return pair(zero, quarter), pair(two, quarter), pair(odd, 2 * quarter), mode_ids


def triple_dot(value, table):
    high = value.astype(jnp.bfloat16)
    low = (value - high.astype(jnp.float32)).astype(jnp.bfloat16)
    dot = functools.partial(jnp.dot, preferred_element_type=jnp.float32)
    return dot(high, table[0]) + dot(high, table[1]) + dot(low, table[0])


def transform_kernel(
    place, own, across, beside, diagonal, kept, gain, modes, f0, f2, f1, i0, i2, i1, out_own, out_across, out_beside, out_diagonal
):
    quarter = own.shape[-1]
    rows = own.shape[-2] * own.shape[-3]
    sign_y = (1 - 2 * place[0]).astype(jnp.float32)
    sign_c = (1 - 2 * place[1]).astype(jnp.float32)
    first = place[1] == 0
    a, b, c, d = (ref[...].reshape(rows, quarter) for ref in (own, across, beside, diagonal))
    near, far = a + b, c + d
    near_odd, far_odd = sign_y * (a - b), sign_y * (c - d)
    odd = jnp.concatenate([jnp.where(first, near_odd, far_odd), jnp.where(first, far_odd, near_odd)], axis=1)
    limit = kept[...]
    ids = modes[...]
    weight = jnp.where(ids < limit, ids, 0.0) * gain[...]

    def filtered(value, forward, inverse, start):
        spectrum = triple_dot(value, forward)
        return triple_dot(spectrum * weight[:, start : start + spectrum.shape[1]], inverse)

    even0 = filtered(near + far, f0, i0, 0)
    even2 = sign_c * filtered(sign_c * (near - far), f2, i2, quarter)
    odd_out = sign_y * filtered(odd, f1, i1, 2 * quarter)
    left, right = odd_out[:, :quarter], odd_out[:, quarter:]
    odd_near, odd_far = jnp.where(first, left, right), jnp.where(first, right, left)
    even_near, even_far = even0 + even2, even0 - even2
    shape = out_own.shape
    out_own[...] = (even_near + odd_near).reshape(shape)
    out_across[...] = (even_near - odd_near).reshape(shape)
    out_beside[...] = (even_far + odd_far).reshape(shape)
    out_diagonal[...] = (even_far - odd_far).reshape(shape)


def transform(place, magnetic, start, across, beside, beside_start, diagonal, kept_rows, gain_rows, tables):
    depth, th_dev, quarter = across.shape
    zero, two, odd, mode_ids = tables
    whole = pl.BlockSpec(memory_space=pltpu.VMEM)
    rows = depth * th_dev
    half = magnetic.shape[1] // 2
    grid_spec = pltpu.PrefetchScalarGridSpec(
        num_scalar_prefetch=1,
        grid=(1,),
        in_specs=[
            pl.BlockSpec((None, depth, th_dev, quarter), lambda i, p: (p[1], p[0] * (half // depth) + start // depth, 0, 0)),
            whole,
            pl.BlockSpec((depth, th_dev, quarter), lambda i, p: (beside_start // depth, 0, 0)),
            whole,
        ]
        + [whole] * 9,
        out_specs=[whole] * 4,
    )
    flops = 2 * 3 * 2 * rows * 6 * quarter * quarter
    return pl.pallas_call(
        transform_kernel,
        grid_spec=grid_spec,
        out_shape=[jax.ShapeDtypeStruct((depth, th_dev, quarter), jnp.float32)] * 4,
        compiler_params=pltpu.CompilerParams(vmem_limit_bytes=VMEM),
        cost_estimate=pl.CostEstimate(flops=flops, bytes_accessed=48 * quarter * quarter, transcendentals=0),
    )(place, magnetic, across, beside, diagonal, kept_rows, gain_rows, mode_ids, zero[0], two[0], odd[0], zero[1], two[1], odd[1])


def diff_along(padded, axis, length):
    total = None
    for offset in range(-3, 4):
        if offset != 0:
            term = stencil_coeffs[offset + 3] * lax.slice_in_dim(padded, 3 + offset, 3 + offset + length, axis=axis)
            total = term if total is None else total + term
    return total


def local_kernel(field, before, after, radius, inv_radius, cot, out):
    radii, th_dev, width = field.shape[1:]
    rad, inv = radius[...], inv_radius[...]
    edge = jnp.zeros((3, th_dev, width), jnp.float32)

    def theta(value, which):
        return diff_along(jnp.concatenate([before[which], value, after[which]], axis=1), 1, th_dev)

    def radial(value):
        return diff_along(jnp.concatenate([edge, rad * value, edge], axis=0), 0, radii)

    b_azim = field[2]
    out[0] = (theta(b_azim, 1) + cot[...] * b_azim) * inv
    out[1] = -radial(b_azim) * inv
    out[2] = (radial(field[1]) - theta(field[0], 0)) * inv


def local_part(magnetic, before, after, radius, inv_radius, cot):
    width = 128
    radii, th_dev, ph_dev = magnetic.shape[1:]
    fixed = lambda *shape: pl.BlockSpec(shape, lambda i: (0, 0, 0))
    wide = lambda *lead: pl.BlockSpec(lead + (width,), lambda i: (0, 0, 0, i))
    return pl.pallas_call(
        local_kernel,
        grid=(ph_dev // width,),
        in_specs=[
            wide(3, radii, th_dev),
            wide(2, radii, 3),
            wide(2, radii, 3),
            fixed(radii, 1, 1),
            fixed(radii, 1, 1),
            fixed(1, th_dev, 1),
        ],
        out_specs=wide(3, radii, th_dev),
        out_shape=jax.ShapeDtypeStruct(magnetic.shape, jnp.float32),
        compiler_params=pltpu.CompilerParams(vmem_limit_bytes=VMEM),
        cost_estimate=pl.CostEstimate(flops=60 * magnetic.size, bytes_accessed=8 * magnetic.size, transcendentals=0),
    )(magnetic, before, after, radius, inv_radius, cot)


def add_azim(place, current, groups, step_radii):
    depth, th_dev, ph_dev = groups[0][0].shape
    steps = depth // step_radii
    half_steps = current.shape[1] // 2 // step_radii

    def radius_block(i, p):
        block = 0
        for g, (_, _, own_half, start) in enumerate(groups):
            half = p[0] if own_half else 1 - p[0]
            here = half * half_steps + start // step_radii + i - g * steps
            block = jnp.where(i // steps == g, here, block)
        return block

    current_block = pl.BlockSpec((2, step_radii, th_dev, ph_dev), lambda i, p: (0, radius_block(i, p), 0, 0))

    def group_block(g):
        at = lambda i, p: (jnp.clip(i - g * steps, 0, steps - 1), 0, 0)
        return pl.BlockSpec((step_radii, th_dev, ph_dev), at)

    def kernel(place, base, *refs):
        out = refs[-1]
        own_part = 1 - place[1]
        for g in range(len(groups)):

            @pl.when(pl.program_id(0) // steps == g)
            def _():
                out[own_part] = base[own_part] + refs[2 * g][...]
                out[1 - own_part] = base[1 - own_part] + refs[2 * g + 1][...]

    azims = [azim for own, other, _, _ in groups for azim in (own, other)]
    size = sum(azim.size for azim in azims)
    return pl.pallas_call(
        kernel,
        grid_spec=pltpu.PrefetchScalarGridSpec(
            num_scalar_prefetch=1,
            grid=(len(groups) * steps,),
            in_specs=[current_block] + [group_block(i // 2) for i in range(len(azims))],
            out_specs=current_block,
        ),
        out_shape=jax.ShapeDtypeStruct(current.shape, jnp.float32),
        input_output_aliases={1: 0},
        compiler_params=pltpu.CompilerParams(vmem_limit_bytes=VMEM),
        cost_estimate=pl.CostEstimate(flops=2 * size, bytes_accessed=12 * size, transcendentals=0),
    )(place, current, *azims)


def after(first, *then):
    return lax.optimization_barrier((first, then))[1]


def on_four(magnetic, kept_modes):
    radii, th_dev, ph_dev = (magnetic.shape[1], magnetic.shape[2], magnetic.shape[3])
    half = radii // 2
    depth = half // CHUNKS
    index = lax.axis_index("azim")
    y, c = index // 2, index % 2
    place = jnp.stack([y, c]).astype(jnp.int32)
    send = lambda value, pairs: lax.ppermute(value, "azim", pairs)

    def cut(source, field, start, length):
        return lax.dynamic_slice(source, (field, start, 0, 0), (1, length, th_dev, ph_dev))[0]

    across, diagonal = [], []
    source = magnetic
    for k in range(CHUNKS):
        to_y = cut(source, c, (1 - y) * half + k * depth, depth)
        (source,) = after(to_y, source)
        to_yc = cut(source, 1 - c, (1 - y) * half + k * depth, depth)
        (source,) = after(to_yc, source)
        across.append(send(to_y, TO_Y))
        diagonal.append(send(to_yc, TO_YC))
        if k == 0:
            to_c = cut(source, 1 - c, y * half, half)
            (source,) = after(to_c, source)
            beside = send(to_c, TO_C)

    spacing, band_start, colatitude = band_geometry(th_dev)
    radius = (inner_radius + (jnp.arange(radii, dtype=jnp.float32) + 0.5) * spacing)[:, None, None]
    inv_radius = 1.0 / radius
    inv_sin = 1.0 / jnp.sin(colatitude)
    cot = spacing * (jnp.cos(colatitude) / jnp.sin(colatitude))[None, :, None]
    sign_c = (1 - 2 * c).astype(jnp.float32)
    row_gain = (sign_c * spacing * 0.5 / ph_dev) * inv_sin[None, :] * inv_radius[:, 0]
    band_counts = lax.dynamic_slice_in_dim(kept_modes, band_start, th_dev).astype(jnp.float32)
    rows = depth * th_dev
    kept_rows = jnp.broadcast_to(band_counts[None, :], (depth, th_dev)).reshape(rows, 1)

    lat_size = lax.axis_size("lat")
    up = [(i, i + 1) for i in range(lat_size - 1)]
    down = [(i + 1, i) for i in range(lat_size - 1)]
    north = lax.ppermute(source[0::2, :, th_dev - 3 :], "lat", up)
    south = lax.ppermute(source[0::2, :, :3], "lat", down)
    current = local_part(magnetic, north, south, radius, inv_radius, cot)

    tables = mode_tables(4 * ph_dev)
    own_half, other_half = [], []
    for k in range(CHUNKS):
        gain_rows = lax.dynamic_slice_in_dim(row_gain, y * half + k * depth, depth).reshape(rows, 1)
        if k == 0:
            (gain_rows,) = after(current, gain_rows)
        mine, to_y, to_c, to_yc = transform(
            place, magnetic, k * depth, across[k], beside, k * depth, diagonal[k], kept_rows, gain_rows, tables
        )
        from_y, from_yc, from_c = send(to_y, TO_Y), send(to_yc, TO_YC), send(to_c, TO_C)
        own_half.append((mine, from_c, True, k * depth))
        other_half.append((from_y, from_yc, False, k * depth))
    current = add_azim(place, current, own_half + other_half[:-1], 2)
    return add_azim(place, current, other_half[-1:], 2)


def solution(mesh):
    placed = (P(None, None, "lat", "azim"), P())

    def run(magnetic, kept_modes):
        radii, ph_dev = magnetic.shape[1], magnetic.shape[3]
        four = lax.axis_size("azim") == 4 and radii % (2 * CHUNKS) == 0 and ph_dev % 256 == 0
        return (on_four if four else on_device)(magnetic, kept_modes)

    return jax.shard_map(
        run,
        mesh=mesh,
        in_specs=placed,
        out_specs=P(None, None, "lat", "azim"),
        check_vma=False,
    )
```

```python
import functools
import math

import jax
import jax.numpy as jnp
import numpy as np
from jax import lax
from jax.experimental import pallas as pl
from jax.experimental.pallas import tpu as pltpu
from jax.sharding import PartitionSpec as P

MB = 128


inner_radius = 0.7
stencil_coeffs = (-1.0 / 60.0, 3.0 / 20.0, -3.0 / 4.0, 0.0, 3.0 / 4.0, -3.0 / 20.0, 1.0 / 60.0)


def extended(value, sides, width):
    for axis, dim in sides:
        size, length = (lax.axis_size(axis), value.shape[dim])
        up = [(i, (i + 1) % size) for i in range(size - 1)]
        down = [(j, i) for i, j in up]
        last = lax.slice_in_dim(value, length - width, length, axis=dim)
        first = lax.slice_in_dim(value, 0, width, axis=dim)
        before = lax.ppermute(last, axis, up)
        after = lax.ppermute(first, axis, down)
        value = jnp.concatenate([before, value, after], axis=dim)
    return value


def stencil_sum(padded, split_axis, length):
    total = jnp.zeros(lax.slice_in_dim(padded, 3, 3 + length, axis=split_axis).shape, jnp.float32)
    for offset in range(-3, 4):
        if offset != 0:
            total = total + stencil_coeffs[offset + 3] * lax.slice_in_dim(
                padded, 3 + offset, 3 + offset + length, axis=split_axis
            )
    return total


def radial_diff(values):
    widths = [(0, 0)] * values.ndim
    widths[0] = (3, 3)
    return stencil_sum(jnp.pad(values, widths), 0, values.shape[0])


def row_counts(band_counts, row_lat):
    lat_ids = jnp.arange(band_counts.shape[0], dtype=jnp.int32)
    match = row_lat[:, None] == lat_ids[None, :]
    return jnp.sum(jnp.where(match, band_counts[None, :], 0), axis=1)


def base_tables(lon_total):
    columns = jnp.arange(lon_total, dtype=jnp.int32)
    mode_ids = jnp.arange(MB, dtype=jnp.int32)
    phase = (mode_ids[:, None] * columns[None, :] % lon_total).astype(jnp.float32) * (
        2.0 * math.pi / lon_total
    )
    return (jnp.cos(phase), jnp.sin(phase))


def spectral(row_data, row_kept, base_cos, base_sin):
    lon_total = row_data.shape[1]
    block_count = (jnp.max(row_kept) + MB - 1) // MB
    columns = jnp.arange(lon_total, dtype=jnp.int32)

    def block_step(block, total):
        mode_ids = block * MB + jnp.arange(MB, dtype=jnp.int32)
        offset_phase = (block * MB * columns % lon_total).astype(jnp.float32) * (
            2.0 * math.pi / lon_total
        )
        offset_cos = jnp.cos(offset_phase)[None, :]
        offset_sin = jnp.sin(offset_phase)[None, :]
        cos_rows = base_cos * offset_cos - base_sin * offset_sin
        sin_rows = base_sin * offset_cos + base_cos * offset_sin
        table = jnp.concatenate([cos_rows, sin_rows], axis=0)
        spectrum = lax.dot_general(
            row_data,
            table,
            (((1,), (1,)), ((), ())),
            precision=lax.Precision.HIGHEST,
            preferred_element_type=jnp.float32,
        )
        weight = jnp.where(mode_ids[None, :] < row_kept[:, None], mode_ids[None, :], 0).astype(
            jnp.float32
        ) * (2.0 / lon_total)
        scaled = jnp.concatenate([spectrum[:, MB:] * weight, -spectrum[:, :MB] * weight], axis=1)
        return total + jnp.dot(
            scaled, table, precision=lax.Precision.HIGHEST, preferred_element_type=jnp.float32
        )

    return lax.fori_loop(0, block_count, block_step, jnp.zeros_like(row_data))


def band_geometry(th_dev):
    lat_total = th_dev * lax.axis_size("lat")
    spacing = math.pi / lat_total
    band_start = lax.axis_index("lat") * th_dev
    colatitude = (
        (band_start + jnp.arange(th_dev, dtype=jnp.int32)).astype(jnp.float32) + 0.5
    ) * spacing
    return spacing, band_start, colatitude


def on_device(magnetic, kept_modes):
    radii_count, th_dev, ph_dev = (magnetic.shape[1], magnetic.shape[2], magnetic.shape[3])
    spacing, band_start, colatitude = band_geometry(th_dev)
    radius = (inner_radius + (jnp.arange(radii_count, dtype=jnp.float32) + 0.5) * spacing)[
        :, None, None
    ]
    inv_sin = (1.0 / jnp.sin(colatitude))[None, :, None]
    cotangent = (jnp.cos(colatitude) / jnp.sin(colatitude))[None, :, None]
    band_counts = lax.dynamic_slice_in_dim(kept_modes, band_start, th_dev)
    theta_pair = jnp.stack([magnetic[0], magnetic[2]])
    padded = extended(theta_pair, (("lat", 2),), 3)
    theta_diff = stencil_sum(padded, 2, th_dev)
    row_data = magnetic[:2].reshape(2 * radii_count * th_dev, ph_dev)
    lined = lax.all_to_all(row_data, "azim", split_axis=0, concat_axis=1, tiled=True)
    base_cos, base_sin = base_tables(lined.shape[1])
    rows_here = lined.shape[0]
    row_start = lax.axis_index("azim") * rows_here
    row_lat = (row_start + jnp.arange(rows_here, dtype=jnp.int32)) % th_dev
    row_kept = row_counts(band_counts, row_lat)
    azimuthal = spectral(lined, row_kept, base_cos, base_sin)
    flat_rows = lax.all_to_all(azimuthal, "azim", split_axis=1, concat_axis=0, tiled=True)
    azim_diff = flat_rows.reshape(2, radii_count, th_dev, ph_dev)
    b_polar = magnetic[1]
    b_azim = magnetic[2]
    j_radial = (
        theta_diff[1] + spacing * cotangent * b_azim - spacing * inv_sin * azim_diff[1]
    ) / radius
    j_polar = (spacing * inv_sin * azim_diff[0] - radial_diff(radius * b_azim)) / radius
    j_azim = (radial_diff(radius * b_polar) - theta_diff[0]) / radius
    return jnp.stack([j_radial, j_polar, j_azim])


CHUNKS = (8, 8)
TO_Y = [(0, 2), (2, 0), (1, 3), (3, 1)]
TO_C = [(0, 1), (1, 0), (2, 3), (3, 2)]
TO_YC = [(0, 3), (3, 0), (1, 2), (2, 1)]
VMEM = 60 * 1024 * 1024
SHORT = pl.CostEstimate(flops=1, bytes_accessed=1, transcendentals=0)


def halves(table):
    high = table.astype(jnp.bfloat16)
    low = (table - high.astype(np.float64)).astype(jnp.bfloat16)
    return np.stack([high, low])


def mode_tables(lon_total):
    quarter = lon_total // 4

    def pair(modes, length):
        phase = (np.arange(length)[:, None] * modes[None, :] % lon_total) * (2.0 * np.pi / lon_total)
        forward = np.concatenate([np.cos(phase), np.sin(phase)], axis=1)
        inverse = np.concatenate([-np.sin(phase), np.cos(phase)], axis=1).T
        return halves(forward), halves(inverse)

    zero = 4 * np.arange(quarter // 2)
    two = zero + 2
    odd = 2 * np.arange(quarter) + 1
    mode_ids = np.concatenate([zero, zero, two, two, odd, odd]).astype(np.float32)[None, :]
    return pair(zero, quarter), pair(two, quarter), pair(odd, 2 * quarter), mode_ids


def triple_dot(value, table):
    high = value.astype(jnp.bfloat16)
    low = (value - high.astype(jnp.float32)).astype(jnp.bfloat16)
    dot = functools.partial(jnp.dot, preferred_element_type=jnp.float32)
    return dot(high, table[0]) + dot(high, table[1]) + dot(low, table[0])


def transform_kernel(place, own, across, beside, diagonal, kept, gain, modes, *refs):
    tables, out_own, out_beside, outs, held, sems = refs[:6], refs[6], refs[7], refs[8:-7], refs[-7:-1], refs[-1]
    copies = [pltpu.make_async_copy(table, ref, sems.at[i]) for i, (table, ref) in enumerate(zip(tables, held))]
    for copy in copies:
        copy.start()
    quarter = own.shape[-1]
    rows = diagonal.shape[0] * diagonal.shape[1]
    sign_y = (1 - 2 * place[0]).astype(jnp.float32)
    sign_c = (1 - 2 * place[1]).astype(jnp.float32)
    first = place[1] == 0
    a, b, c, d = (ref[...].reshape(rows, quarter) for ref in (own, across, beside, diagonal))
    near, far = a + b, c + d
    near_odd, far_odd = sign_y * (a - b), sign_y * (c - d)
    odd = jnp.concatenate([jnp.where(first, near_odd, far_odd), jnp.where(first, far_odd, near_odd)], axis=1)
    limit = kept[...]
    ids = modes[...]
    weight = jnp.where(ids < limit, ids, 0.0) * gain[...]

    def filtered(value, which, start):
        copies[2 * which].wait()
        spectrum = triple_dot(value, held[2 * which])
        copies[2 * which + 1].wait()
        return triple_dot(spectrum * weight[:, start : start + spectrum.shape[1]], held[2 * which + 1])

    even0 = filtered(near + far, 0, 0)
    even2 = sign_c * filtered(sign_c * (near - far), 1, quarter)
    odd_out = sign_y * filtered(odd, 2, 2 * quarter)
    left, right = odd_out[:, :quarter], odd_out[:, quarter:]
    odd_near, odd_far = jnp.where(first, left, right), jnp.where(first, right, left)
    even_near, even_far = even0 + even2, even0 - even2
    shape = out_own.shape
    out_own[...] = (even_near + odd_near).reshape(shape)
    out_beside[...] = (even_far + odd_far).reshape(shape)
    across, diagonal = (even_near - odd_near).reshape(shape), (even_far - odd_far).reshape(shape)
    if len(outs) == 1:
        outs[0][0], outs[0][1] = across, diagonal
    else:
        outs[0][...], outs[1][...] = across, diagonal


def transform(place, magnetic, start, both, beside, diagonal, row_kept, row_gain, tables, paired):
    depth, th_dev, quarter = diagonal.shape
    zero, two, odd, mode_ids = tables
    whole = pl.BlockSpec(memory_space=pltpu.VMEM)
    rows = depth * th_dev
    half = magnetic.shape[1] // 2
    part = (pl.Element(1), pl.Element(depth), pl.Element(th_dev), pl.Element(quarter))
    row_block = pl.BlockSpec((pl.Element(rows), pl.Element(1)), lambda i, p: (start * th_dev, 0))
    grid_spec = pltpu.PrefetchScalarGridSpec(
        num_scalar_prefetch=1,
        grid=(1,),
        in_specs=[
            pl.BlockSpec(part, lambda i, p: (p[1], p[0] * half + start, 0, 0)),
            pl.BlockSpec((None, depth, th_dev, quarter), lambda i, p: (p[1], 0, 0, 0)),
            pl.BlockSpec(part[1:], lambda i, p: (start, 0, 0)),
            whole,
            row_block,
            row_block,
            whole,
        ]
        + [pl.BlockSpec(memory_space=pl.ANY)] * 6,
        out_specs=[whole] * (3 if paired else 4),
        scratch_shapes=[pltpu.VMEM(t.shape, jnp.bfloat16) for t in (*zero, *two, *odd)] + [pltpu.SemaphoreType.DMA((6,))],
    )
    shape = (depth, th_dev, quarter)
    shapes = [shape, shape, (2,) + shape] if paired else [shape] * 4
    outs = pl.pallas_call(
        transform_kernel,
        grid_spec=grid_spec,
        out_shape=[jax.ShapeDtypeStruct(shape, jnp.float32) for shape in shapes],
        compiler_params=pltpu.CompilerParams(vmem_limit_bytes=VMEM),
        cost_estimate=SHORT,
    )(place, magnetic, both, beside, diagonal, row_kept, row_gain, mode_ids, *zero, *two, *odd)
    return (*outs, None) if paired else outs


def diff_along(padded, axis, length):
    total = None
    for offset in range(-3, 4):
        if offset != 0:
            term = stencil_coeffs[offset + 3] * lax.slice_in_dim(padded, 3 + offset, 3 + offset + length, axis=axis)
            total = term if total is None else total + term
    return total


def local_part(place, magnetic, before, after, radius, inv_radius, cot, groups):
    width = 128
    radii, th_dev, ph_dev = magnetic.shape[1:]
    fixed = lambda *shape: pl.BlockSpec(shape, lambda i, p: (0, 0, 0))
    wide = lambda *lead: pl.BlockSpec(lead + (width,), lambda i, p: (0,) * len(lead) + (i,))

    def kernel(place, field, before, after, radius, inv_radius, cot, *refs):
        out, azims = refs[-1], refs[:-1]
        rad, inv = radius[...], inv_radius[...]
        edge = jnp.zeros((3, th_dev, width), jnp.float32)

        def theta(value, which):
            return diff_along(jnp.concatenate([before[which], value, after[which]], axis=1), 1, th_dev)

        def radial(value):
            return diff_along(jnp.concatenate([edge, rad * value, edge], axis=0), 0, radii)

        b_azim = field[2]
        out[0] = (theta(b_azim, 1) + cot[...] * b_azim) * inv
        out[1] = -radial(b_azim) * inv
        out[2] = (radial(field[1]) - theta(field[0], 0)) * inv
        for k, (_, _, own_half, start) in enumerate(groups):
            half = place[0] if own_half else 1 - place[0]
            here = pl.ds(half * (radii // 2) + start, azims[2 * k].shape[0])
            out[1 - place[1], here] += azims[2 * k][...]
            out[place[1], here] += azims[2 * k + 1][...]

    azims = [azim for own, crossed, _, _ in groups for azim in (own, crossed)]
    return pl.pallas_call(
        kernel,
        grid_spec=pltpu.PrefetchScalarGridSpec(
            num_scalar_prefetch=1,
            grid=(ph_dev // width,),
            in_specs=[
                wide(3, radii, th_dev),
                wide(2, radii, 3),
                wide(2, radii, 3),
                fixed(radii, 1, 1),
                fixed(radii, 1, 1),
                fixed(1, th_dev, 1),
            ]
            + [wide(*azim.shape[:-1]) for azim in azims],
            out_specs=wide(3, radii, th_dev),
        ),
        out_shape=jax.ShapeDtypeStruct(magnetic.shape, jnp.float32),
        compiler_params=pltpu.CompilerParams(vmem_limit_bytes=VMEM),
        cost_estimate=SHORT,
    )(place, magnetic, before, after, radius, inv_radius, cot, *azims)


def add_pair(place, current, from_y, from_yc, start):
    depth, th_dev, ph_dev = from_y.shape
    half = current.shape[1] // 2
    whole = pl.BlockSpec(memory_space=pltpu.VMEM)
    block = pl.BlockSpec(
        (pl.Element(2), pl.Element(depth), pl.Element(th_dev), pl.Element(ph_dev)),
        lambda i, p: (0, (1 - p[0]) * half + start, 0, 0),
    )

    def kernel(place, base, own, other, out):
        part = 1 - place[1]
        out[part] = base[part] + own[...]
        out[1 - part] = base[1 - part] + other[...]

    return pl.pallas_call(
        kernel,
        grid_spec=pltpu.PrefetchScalarGridSpec(
            num_scalar_prefetch=1, grid=(1,), in_specs=[block, whole, whole], out_specs=block
        ),
        out_shape=jax.ShapeDtypeStruct(current.shape, jnp.float32),
        input_output_aliases={1: 0},
        compiler_params=pltpu.CompilerParams(vmem_limit_bytes=VMEM // 6),
        cost_estimate=SHORT,
    )(place, current, from_y, from_yc)


def after(first, *then):
    return lax.optimization_barrier((first, then))[1]


def on_four(magnetic, kept_modes):
    radii, th_dev, ph_dev = (magnetic.shape[1], magnetic.shape[2], magnetic.shape[3])
    half = radii // 2
    total = sum(CHUNKS)
    depths = [half * part // total for part in CHUNKS]
    starts = [sum(depths[:k]) for k in range(len(depths))]
    index = lax.axis_index("azim")
    y, c = index // 2, index % 2
    place = jnp.stack([y, c]).astype(jnp.int32)
    send = lambda value, pairs: lax.ppermute(value, "azim", pairs)

    def cut(source, field, start, length):
        return lax.dynamic_slice(source, (field, start, 0, 0), (1, length, th_dev, ph_dev))[0]

    arrived = []
    source = magnetic
    for k, depth in enumerate(depths):
        both = lax.dynamic_slice(source, (0, (1 - y) * half + starts[k], 0, 0), (2, depth, th_dev, ph_dev))
        (source,) = after(both, source)
        arrived.append(send(both, TO_Y))
        if k == 0:
            lat_size = lax.axis_size("lat")
            up = [(i, i + 1) for i in range(lat_size - 1)]
            down = [(i + 1, i) for i in range(lat_size - 1)]
            last, first = source[0::2, :, th_dev - 3 :], source[0::2, :, :3]
            (source,) = after((last, first), source)
            north, south = lax.ppermute(last, "lat", up), lax.ppermute(first, "lat", down)
            to_c = cut(source, 1 - c, y * half, half)
            (source,) = after(to_c, source)
            beside = send(to_c, TO_C)

    spacing, band_start, colatitude = band_geometry(th_dev)
    radius = (inner_radius + (jnp.arange(radii, dtype=jnp.float32) + 0.5) * spacing)[:, None, None]
    inv_radius = 1.0 / radius
    inv_sin = 1.0 / jnp.sin(colatitude)
    cot = spacing * (jnp.cos(colatitude) / jnp.sin(colatitude))[None, :, None]
    sign_c = (1 - 2 * c).astype(jnp.float32)
    row_gain = (sign_c * spacing * 0.5 / ph_dev) * inv_sin[None, :] * inv_radius[:, 0]
    row_gain = lax.dynamic_slice_in_dim(row_gain, y * half, half).reshape(half * th_dev, 1)
    band_counts = lax.dynamic_slice_in_dim(kept_modes, band_start, th_dev).astype(jnp.float32)
    row_kept = jnp.broadcast_to(band_counts[None, :], (half, th_dev)).reshape(half * th_dev, 1)

    tables = mode_tables(4 * ph_dev)
    mine, from_c, returned = [], [], []
    for k, (start, depth) in enumerate(zip(starts, depths)):
        both = arrived[k]
        if k > 0:
            (both,) = after((mine[-1], north, south), both)
            (row_gain,) = after(from_c[-1], row_gain)
        diagonal = send(cut(both, 1 - c, 0, depth), TO_C)
        out, to_c, to_y, to_yc = transform(
            place, magnetic, start, both, beside, diagonal, row_kept, row_gain, tables, k + 1 < len(depths)
        )
        mine.append(out)
        from_c.append(send(to_c, TO_C))
        returned.append(send(to_y, TO_Y))
    final = returned.pop(), send(to_yc, TO_YC)

    groups = [(own, crossed, True, start) for own, crossed, start in zip(mine, from_c, starts)]
    for value, start in zip(returned, starts):
        groups.append((value[0], send(value[1], TO_C), False, start))
    north, south = after(mine[-1], north, south)
    current = local_part(place, magnetic, north, south, radius, inv_radius, cot, groups)
    return add_pair(place, current, *final, starts[-1])


def solution(mesh):
    placed = (P(None, None, "lat", "azim"), P())

    def run(magnetic, kept_modes):
        radii, ph_dev = magnetic.shape[1], magnetic.shape[3]
        four = lax.axis_size("azim") == 4 and radii % (2 * sum(CHUNKS)) == 0 and ph_dev % 256 == 0
        return (on_four if four else on_device)(magnetic, kept_modes)

    return jax.shard_map(
        run,
        mesh=mesh,
        in_specs=placed,
        out_specs=P(None, None, "lat", "azim"),
        check_vma=False,
    )
```

```python
import functools
import math

import jax
import jax.numpy as jnp
import numpy as np
from jax import lax
from jax.experimental import pallas as pl
from jax.experimental.pallas import tpu as pltpu
from jax.sharding import PartitionSpec as P

MB = 128


inner_radius = 0.7
stencil_coeffs = (-1.0 / 60.0, 3.0 / 20.0, -3.0 / 4.0, 0.0, 3.0 / 4.0, -3.0 / 20.0, 1.0 / 60.0)


def extended(value, sides, width):
    for axis, dim in sides:
        size, length = (lax.axis_size(axis), value.shape[dim])
        up = [(i, (i + 1) % size) for i in range(size - 1)]
        down = [(j, i) for i, j in up]
        last = lax.slice_in_dim(value, length - width, length, axis=dim)
        first = lax.slice_in_dim(value, 0, width, axis=dim)
        before = lax.ppermute(last, axis, up)
        after = lax.ppermute(first, axis, down)
        value = jnp.concatenate([before, value, after], axis=dim)
    return value


def stencil_sum(padded, split_axis, length):
    total = jnp.zeros(lax.slice_in_dim(padded, 3, 3 + length, axis=split_axis).shape, jnp.float32)
    for offset in range(-3, 4):
        if offset != 0:
            total = total + stencil_coeffs[offset + 3] * lax.slice_in_dim(
                padded, 3 + offset, 3 + offset + length, axis=split_axis
            )
    return total


def radial_diff(values):
    widths = [(0, 0)] * values.ndim
    widths[0] = (3, 3)
    return stencil_sum(jnp.pad(values, widths), 0, values.shape[0])


def row_counts(band_counts, row_lat):
    lat_ids = jnp.arange(band_counts.shape[0], dtype=jnp.int32)
    match = row_lat[:, None] == lat_ids[None, :]
    return jnp.sum(jnp.where(match, band_counts[None, :], 0), axis=1)


def base_tables(lon_total):
    columns = jnp.arange(lon_total, dtype=jnp.int32)
    mode_ids = jnp.arange(MB, dtype=jnp.int32)
    phase = (mode_ids[:, None] * columns[None, :] % lon_total).astype(jnp.float32) * (
        2.0 * math.pi / lon_total
    )
    return (jnp.cos(phase), jnp.sin(phase))


def spectral(row_data, row_kept, base_cos, base_sin):
    lon_total = row_data.shape[1]
    block_count = (jnp.max(row_kept) + MB - 1) // MB
    columns = jnp.arange(lon_total, dtype=jnp.int32)

    def block_step(block, total):
        mode_ids = block * MB + jnp.arange(MB, dtype=jnp.int32)
        offset_phase = (block * MB * columns % lon_total).astype(jnp.float32) * (
            2.0 * math.pi / lon_total
        )
        offset_cos = jnp.cos(offset_phase)[None, :]
        offset_sin = jnp.sin(offset_phase)[None, :]
        cos_rows = base_cos * offset_cos - base_sin * offset_sin
        sin_rows = base_sin * offset_cos + base_cos * offset_sin
        table = jnp.concatenate([cos_rows, sin_rows], axis=0)
        spectrum = lax.dot_general(
            row_data,
            table,
            (((1,), (1,)), ((), ())),
            precision=lax.Precision.HIGHEST,
            preferred_element_type=jnp.float32,
        )
        weight = jnp.where(mode_ids[None, :] < row_kept[:, None], mode_ids[None, :], 0).astype(
            jnp.float32
        ) * (2.0 / lon_total)
        scaled = jnp.concatenate([spectrum[:, MB:] * weight, -spectrum[:, :MB] * weight], axis=1)
        return total + jnp.dot(
            scaled, table, precision=lax.Precision.HIGHEST, preferred_element_type=jnp.float32
        )

    return lax.fori_loop(0, block_count, block_step, jnp.zeros_like(row_data))


def band_geometry(th_dev):
    lat_total = th_dev * lax.axis_size("lat")
    spacing = math.pi / lat_total
    band_start = lax.axis_index("lat") * th_dev
    colatitude = (
        (band_start + jnp.arange(th_dev, dtype=jnp.int32)).astype(jnp.float32) + 0.5
    ) * spacing
    return spacing, band_start, colatitude


def on_device(magnetic, kept_modes):
    radii_count, th_dev, ph_dev = (magnetic.shape[1], magnetic.shape[2], magnetic.shape[3])
    spacing, band_start, colatitude = band_geometry(th_dev)
    radius = (inner_radius + (jnp.arange(radii_count, dtype=jnp.float32) + 0.5) * spacing)[
        :, None, None
    ]
    inv_sin = (1.0 / jnp.sin(colatitude))[None, :, None]
    cotangent = (jnp.cos(colatitude) / jnp.sin(colatitude))[None, :, None]
    band_counts = lax.dynamic_slice_in_dim(kept_modes, band_start, th_dev)
    theta_pair = jnp.stack([magnetic[0], magnetic[2]])
    padded = extended(theta_pair, (("lat", 2),), 3)
    theta_diff = stencil_sum(padded, 2, th_dev)
    row_data = magnetic[:2].reshape(2 * radii_count * th_dev, ph_dev)
    lined = lax.all_to_all(row_data, "azim", split_axis=0, concat_axis=1, tiled=True)
    base_cos, base_sin = base_tables(lined.shape[1])
    rows_here = lined.shape[0]
    row_start = lax.axis_index("azim") * rows_here
    row_lat = (row_start + jnp.arange(rows_here, dtype=jnp.int32)) % th_dev
    row_kept = row_counts(band_counts, row_lat)
    azimuthal = spectral(lined, row_kept, base_cos, base_sin)
    flat_rows = lax.all_to_all(azimuthal, "azim", split_axis=1, concat_axis=0, tiled=True)
    azim_diff = flat_rows.reshape(2, radii_count, th_dev, ph_dev)
    b_polar = magnetic[1]
    b_azim = magnetic[2]
    j_radial = (
        theta_diff[1] + spacing * cotangent * b_azim - spacing * inv_sin * azim_diff[1]
    ) / radius
    j_polar = (spacing * inv_sin * azim_diff[0] - radial_diff(radius * b_azim)) / radius
    j_azim = (radial_diff(radius * b_polar) - theta_diff[0]) / radius
    return jnp.stack([j_radial, j_polar, j_azim])


CHUNKS = (7, 9)
TO_Y = [(0, 2), (2, 0), (1, 3), (3, 1)]
TO_C = [(0, 1), (1, 0), (2, 3), (3, 2)]
TO_YC = [(0, 3), (3, 0), (1, 2), (2, 1)]
VMEM = 60 * 1024 * 1024
SHORT = pl.CostEstimate(flops=1, bytes_accessed=1, transcendentals=0)


def halves(table):
    high = table.astype(jnp.bfloat16)
    low = (table - high.astype(np.float64)).astype(jnp.bfloat16)
    return np.stack([high, low])


def mode_tables(lon_total):
    quarter = lon_total // 4

    def pair(modes, length):
        phase = (np.arange(length)[:, None] * modes[None, :] % lon_total) * (2.0 * np.pi / lon_total)
        forward = np.concatenate([np.cos(phase), np.sin(phase)], axis=1)
        inverse = np.concatenate([-np.sin(phase), np.cos(phase)], axis=1).T
        return halves(forward), halves(inverse)

    zero = 4 * np.arange(quarter // 2)
    two = zero + 2
    odd = 2 * np.arange(quarter) + 1
    mode_ids = np.concatenate([zero, zero, two, two, odd, odd]).astype(np.float32)[None, :]
    return pair(zero, quarter), pair(two, quarter), pair(odd, 2 * quarter), mode_ids


def triple_dot(value, table):
    high = value.astype(jnp.bfloat16)
    low = (value - high.astype(jnp.float32)).astype(jnp.bfloat16)
    dot = functools.partial(jnp.dot, preferred_element_type=jnp.float32)
    return dot(high, table[0]) + dot(high, table[1]) + dot(low, table[0])


def transform_kernel(place, own, across, beside, diagonal, kept, gain, modes, *refs):
    tables, out_own, out_beside, outs, held, sems = refs[:6], refs[6], refs[7], refs[8:-7], refs[-7:-1], refs[-1]
    copies = [pltpu.make_async_copy(table, ref, sems.at[i]) for i, (table, ref) in enumerate(zip(tables, held))]
    for copy in copies:
        copy.start()
    quarter = own.shape[-1]
    rows = diagonal.shape[0] * diagonal.shape[1]
    sign_y = (1 - 2 * place[0]).astype(jnp.float32)
    sign_c = (1 - 2 * place[1]).astype(jnp.float32)
    first = place[1] == 0
    a, b, c, d = (ref[...].reshape(rows, quarter) for ref in (own, across, beside, diagonal))
    near, far = a + b, c + d
    near_odd, far_odd = sign_y * (a - b), sign_y * (c - d)
    odd = jnp.concatenate([jnp.where(first, near_odd, far_odd), jnp.where(first, far_odd, near_odd)], axis=1)
    limit = kept[...]
    ids = modes[...]
    weight = jnp.where(ids < limit, ids, 0.0) * gain[...]

    def filtered(value, which, start):
        copies[2 * which].wait()
        spectrum = triple_dot(value, held[2 * which])
        copies[2 * which + 1].wait()
        return triple_dot(spectrum * weight[:, start : start + spectrum.shape[1]], held[2 * which + 1])

    even0 = filtered(near + far, 0, 0)
    even2 = sign_c * filtered(sign_c * (near - far), 1, quarter)
    odd_out = sign_y * filtered(odd, 2, 2 * quarter)
    left, right = odd_out[:, :quarter], odd_out[:, quarter:]
    odd_near, odd_far = jnp.where(first, left, right), jnp.where(first, right, left)
    even_near, even_far = even0 + even2, even0 - even2
    shape = out_own.shape
    out_own[...] = (even_near + odd_near).reshape(shape)
    out_beside[...] = (even_far + odd_far).reshape(shape)
    across, diagonal = (even_near - odd_near).reshape(shape), (even_far - odd_far).reshape(shape)
    if len(outs) == 1:
        outs[0][0], outs[0][1] = across, diagonal
    else:
        outs[0][...], outs[1][...] = across, diagonal


def transform(place, magnetic, start, both, beside, diagonal, row_kept, row_gain, tables, paired):
    depth, th_dev, quarter = diagonal.shape
    zero, two, odd, mode_ids = tables
    whole = pl.BlockSpec(memory_space=pltpu.VMEM)
    rows = depth * th_dev
    half = magnetic.shape[1] // 2
    part = (pl.Element(1), pl.Element(depth), pl.Element(th_dev), pl.Element(quarter))
    row_block = pl.BlockSpec((pl.Element(rows), pl.Element(1)), lambda i, p: (start * th_dev, 0))
    grid_spec = pltpu.PrefetchScalarGridSpec(
        num_scalar_prefetch=1,
        grid=(1,),
        in_specs=[
            pl.BlockSpec(part, lambda i, p: (p[1], p[0] * half + start, 0, 0)),
            pl.BlockSpec((None, depth, th_dev, quarter), lambda i, p: (p[1], 0, 0, 0)),
            pl.BlockSpec(part[1:], lambda i, p: (start, 0, 0)),
            whole,
            row_block,
            row_block,
            whole,
        ]
        + [pl.BlockSpec(memory_space=pl.ANY)] * 6,
        out_specs=[whole] * (3 if paired else 4),
        scratch_shapes=[pltpu.VMEM(t.shape, jnp.bfloat16) for t in (*zero, *two, *odd)] + [pltpu.SemaphoreType.DMA((6,))],
    )
    shape = (depth, th_dev, quarter)
    shapes = [shape, shape, (2,) + shape] if paired else [shape] * 4
    outs = pl.pallas_call(
        transform_kernel,
        grid_spec=grid_spec,
        out_shape=[jax.ShapeDtypeStruct(shape, jnp.float32) for shape in shapes],
        compiler_params=pltpu.CompilerParams(vmem_limit_bytes=VMEM),
        cost_estimate=SHORT,
    )(place, magnetic, both, beside, diagonal, row_kept, row_gain, mode_ids, *zero, *two, *odd)
    return (*outs, None) if paired else outs


def edge_rows(magnetic):
    radii, th_dev, ph_dev = magnetic.shape[1:]
    edge = lambda at: pl.BlockSpec((None, radii, 8, ph_dev), lambda i: (2 * i, 0, at, 0))
    rows = pl.BlockSpec((None, 3, radii, ph_dev), lambda i: (i, 0, 0, 0))

    def kernel(top, bottom, last, first):
        for i in range(3):
            last[i] = bottom[:, 5 + i, :]
            first[i] = top[:, i, :]

    return pl.pallas_call(
        kernel,
        grid=(2,),
        in_specs=[edge(0), edge(th_dev // 8 - 1)],
        out_specs=[rows, rows],
        out_shape=[jax.ShapeDtypeStruct((2, 3, radii, ph_dev), jnp.float32)] * 2,
        compiler_params=pltpu.CompilerParams(vmem_limit_bytes=VMEM),
        cost_estimate=SHORT,
    )(magnetic, magnetic)


def local_part(place, magnetic, before, after, radius, inv_radius, cot, groups):
    width = 128
    radii, th_dev, ph_dev = magnetic.shape[1:]
    fixed = lambda *shape: pl.BlockSpec(shape, lambda i, p: (0, 0, 0))
    wide = lambda *lead: pl.BlockSpec(lead + (width,), lambda i, p: (0,) * len(lead) + (i,))
    weights = [stencil_coeffs[3 + offset] for offset in (1, 2, 3)]

    def kernel(place, field, before, after, radius, inv_radius, cot, *refs):
        azims, out, rows, layers = refs[:-3], *refs[-3:]
        inv = inv_radius[...]

        def theta(value, which):
            rows[:, 8 : 8 + th_dev, :] = value
            for i in range(3):
                rows[:, 5 + i, :] = before[which, i]
                rows[:, 8 + th_dev + i, :] = after[which, i]
            shifted = lambda offset: rows[:, 8 + offset : 8 + offset + th_dev, :]
            return sum(w * (shifted(o) - shifted(-o)) for o, w in enumerate(weights, 1))

        def radial(value):
            layers[3 : 3 + radii] = radius[...] * value
            shifted = lambda offset: layers[3 + offset : 3 + offset + radii]
            return sum(w * (shifted(o) - shifted(-o)) for o, w in enumerate(weights, 1))

        layers[:3] = jnp.zeros((3, th_dev, width), jnp.float32)
        layers[3 + radii :] = jnp.zeros((3, th_dev, width), jnp.float32)
        out[0] = (theta(field[2], 1) + cot[...] * field[2]) * inv
        out[1] = -radial(field[2]) * inv
        out[2] = (radial(field[1]) - theta(field[0], 0)) * inv
        for k, (_, _, own_half, start) in enumerate(groups):
            half = place[0] if own_half else 1 - place[0]
            here = pl.ds(half * (radii // 2) + start, azims[2 * k].shape[0])
            out[1 - place[1], here] += azims[2 * k][...]
            out[place[1], here] += azims[2 * k + 1][...]

    azims = [azim for own, crossed, _, _ in groups for azim in (own, crossed)]
    return pl.pallas_call(
        kernel,
        grid_spec=pltpu.PrefetchScalarGridSpec(
            num_scalar_prefetch=1,
            grid=(ph_dev // width,),
            in_specs=[
                wide(3, radii, th_dev),
                wide(2, 3, radii),
                wide(2, 3, radii),
                fixed(radii, 1, 1),
                fixed(radii, 1, 1),
                fixed(1, th_dev, 1),
            ]
            + [wide(*azim.shape[:-1]) for azim in azims],
            out_specs=wide(3, radii, th_dev),
            scratch_shapes=[
                pltpu.VMEM((radii, th_dev + 16, width), jnp.float32),
                pltpu.VMEM((radii + 6, th_dev, width), jnp.float32),
            ],
        ),
        out_shape=jax.ShapeDtypeStruct(magnetic.shape, jnp.float32),
        compiler_params=pltpu.CompilerParams(vmem_limit_bytes=VMEM),
        cost_estimate=SHORT,
    )(place, magnetic, before, after, radius, inv_radius, cot, *azims)


def add_pair(place, current, from_y, from_yc, start):
    depth, th_dev, ph_dev = from_y.shape
    half = current.shape[1] // 2
    whole = pl.BlockSpec(memory_space=pltpu.VMEM)
    block = pl.BlockSpec(
        (pl.Element(2), pl.Element(depth), pl.Element(th_dev), pl.Element(ph_dev)),
        lambda i, p: (0, (1 - p[0]) * half + start, 0, 0),
    )

    def kernel(place, base, own, other, out):
        part = 1 - place[1]
        out[part] = base[part] + own[...]
        out[1 - part] = base[1 - part] + other[...]

    return pl.pallas_call(
        kernel,
        grid_spec=pltpu.PrefetchScalarGridSpec(
            num_scalar_prefetch=1, grid=(1,), in_specs=[block, whole, whole], out_specs=block
        ),
        out_shape=jax.ShapeDtypeStruct(current.shape, jnp.float32),
        input_output_aliases={1: 0},
        compiler_params=pltpu.CompilerParams(vmem_limit_bytes=VMEM // 6),
        cost_estimate=SHORT,
    )(place, current, from_y, from_yc)


def after(first, *then):
    return lax.optimization_barrier((first, then))[1]


def on_four(magnetic, kept_modes):
    radii, th_dev, ph_dev = (magnetic.shape[1], magnetic.shape[2], magnetic.shape[3])
    half = radii // 2
    total = sum(CHUNKS)
    depths = [half * part // total for part in CHUNKS]
    starts = [sum(depths[:k]) for k in range(len(depths))]
    index = lax.axis_index("azim")
    y, c = index // 2, index % 2
    place = jnp.stack([y, c]).astype(jnp.int32)
    send = lambda value, pairs: lax.ppermute(value, "azim", pairs)

    def cut(source, field, start, length):
        return lax.dynamic_slice(source, (field, start, 0, 0), (1, length, th_dev, ph_dev))[0]

    arrived = []
    source = magnetic
    for k, depth in enumerate(depths):
        both = lax.dynamic_slice(source, (0, (1 - y) * half + starts[k], 0, 0), (2, depth, th_dev, ph_dev))
        (source,) = after(both, source)
        arrived.append(send(both, TO_Y))
        if k == 0:
            lat_size = lax.axis_size("lat")
            up = [(i, i + 1) for i in range(lat_size - 1)]
            down = [(i + 1, i) for i in range(lat_size - 1)]
            last, first = edge_rows(source)
            (source,) = after((last, first), source)
            north, south = lax.ppermute(last, "lat", up), lax.ppermute(first, "lat", down)
            to_c = cut(source, 1 - c, y * half, half)
            (source,) = after(to_c, source)
            beside = send(to_c, TO_C)

    spacing, band_start, colatitude = band_geometry(th_dev)
    radius = (inner_radius + (jnp.arange(radii, dtype=jnp.float32) + 0.5) * spacing)[:, None, None]
    inv_radius = 1.0 / radius
    inv_sin = 1.0 / jnp.sin(colatitude)
    cot = spacing * (jnp.cos(colatitude) / jnp.sin(colatitude))[None, :, None]
    sign_c = (1 - 2 * c).astype(jnp.float32)
    row_gain = (sign_c * spacing * 0.5 / ph_dev) * inv_sin[None, :] * inv_radius[:, 0]
    row_gain = lax.dynamic_slice_in_dim(row_gain, y * half, half).reshape(half * th_dev, 1)
    band_counts = lax.dynamic_slice_in_dim(kept_modes, band_start, th_dev).astype(jnp.float32)
    row_kept = jnp.broadcast_to(band_counts[None, :], (half, th_dev)).reshape(half * th_dev, 1)

    tables = mode_tables(4 * ph_dev)
    mine, from_c, returned = [], [], []
    for k, (start, depth) in enumerate(zip(starts, depths)):
        both = arrived[k]
        if k > 0:
            (both,) = after(mine[-1], both)
        (row_gain,) = after(from_c[-1] if k > 0 else (north, south), row_gain)
        diagonal = send(cut(both, 1 - c, 0, depth), TO_C)
        out, to_c, to_y, to_yc = transform(
            place, magnetic, start, both, beside, diagonal, row_kept, row_gain, tables, k + 1 < len(depths)
        )
        mine.append(out)
        from_c.append(send(to_c, TO_C))
        returned.append(send(to_y, TO_Y))
    final = returned.pop(), send(to_yc, TO_YC)

    groups = [(own, crossed, True, start) for own, crossed, start in zip(mine, from_c, starts)]
    for value, start in zip(returned, starts):
        groups.append((value[0], send(value[1], TO_C), False, start))
    north, south = after(mine[-1], north, south)
    current = local_part(place, magnetic, north, south, radius, inv_radius, cot, groups)
    return add_pair(place, current, *final, starts[-1])


def solution(mesh):
    placed = (P(None, None, "lat", "azim"), P())

    def run(magnetic, kept_modes):
        radii, ph_dev = magnetic.shape[1], magnetic.shape[3]
        four = lax.axis_size("azim") == 4 and radii % (2 * sum(CHUNKS)) == 0 and ph_dev % 256 == 0
        return (on_four if four else on_device)(magnetic, kept_modes)

    return jax.shard_map(
        run,
        mesh=mesh,
        in_specs=placed,
        out_specs=P(None, None, "lat", "azim"),
        check_vma=False,
    )
```

```python
import functools
import math

import jax
import jax.numpy as jnp
import numpy as np
from jax import lax
from jax.experimental import pallas as pl
from jax.experimental.pallas import tpu as pltpu
from jax.sharding import PartitionSpec as P

MB = 128


inner_radius = 0.7
stencil_coeffs = (-1.0 / 60.0, 3.0 / 20.0, -3.0 / 4.0, 0.0, 3.0 / 4.0, -3.0 / 20.0, 1.0 / 60.0)


def extended(value, sides, width):
    for axis, dim in sides:
        size, length = (lax.axis_size(axis), value.shape[dim])
        up = [(i, (i + 1) % size) for i in range(size - 1)]
        down = [(j, i) for i, j in up]
        last = lax.slice_in_dim(value, length - width, length, axis=dim)
        first = lax.slice_in_dim(value, 0, width, axis=dim)
        before = lax.ppermute(last, axis, up)
        after = lax.ppermute(first, axis, down)
        value = jnp.concatenate([before, value, after], axis=dim)
    return value


def stencil_sum(padded, split_axis, length):
    total = jnp.zeros(lax.slice_in_dim(padded, 3, 3 + length, axis=split_axis).shape, jnp.float32)
    for offset in range(-3, 4):
        if offset != 0:
            total = total + stencil_coeffs[offset + 3] * lax.slice_in_dim(
                padded, 3 + offset, 3 + offset + length, axis=split_axis
            )
    return total


def radial_diff(values):
    widths = [(0, 0)] * values.ndim
    widths[0] = (3, 3)
    return stencil_sum(jnp.pad(values, widths), 0, values.shape[0])


def row_counts(band_counts, row_lat):
    lat_ids = jnp.arange(band_counts.shape[0], dtype=jnp.int32)
    match = row_lat[:, None] == lat_ids[None, :]
    return jnp.sum(jnp.where(match, band_counts[None, :], 0), axis=1)


def base_tables(lon_total):
    columns = jnp.arange(lon_total, dtype=jnp.int32)
    mode_ids = jnp.arange(MB, dtype=jnp.int32)
    phase = (mode_ids[:, None] * columns[None, :] % lon_total).astype(jnp.float32) * (
        2.0 * math.pi / lon_total
    )
    return (jnp.cos(phase), jnp.sin(phase))


def spectral(row_data, row_kept, base_cos, base_sin):
    lon_total = row_data.shape[1]
    block_count = (jnp.max(row_kept) + MB - 1) // MB
    columns = jnp.arange(lon_total, dtype=jnp.int32)

    def block_step(block, total):
        mode_ids = block * MB + jnp.arange(MB, dtype=jnp.int32)
        offset_phase = (block * MB * columns % lon_total).astype(jnp.float32) * (
            2.0 * math.pi / lon_total
        )
        offset_cos = jnp.cos(offset_phase)[None, :]
        offset_sin = jnp.sin(offset_phase)[None, :]
        cos_rows = base_cos * offset_cos - base_sin * offset_sin
        sin_rows = base_sin * offset_cos + base_cos * offset_sin
        table = jnp.concatenate([cos_rows, sin_rows], axis=0)
        spectrum = lax.dot_general(
            row_data,
            table,
            (((1,), (1,)), ((), ())),
            precision=lax.Precision.HIGHEST,
            preferred_element_type=jnp.float32,
        )
        weight = jnp.where(mode_ids[None, :] < row_kept[:, None], mode_ids[None, :], 0).astype(
            jnp.float32
        ) * (2.0 / lon_total)
        scaled = jnp.concatenate([spectrum[:, MB:] * weight, -spectrum[:, :MB] * weight], axis=1)
        return total + jnp.dot(
            scaled, table, precision=lax.Precision.HIGHEST, preferred_element_type=jnp.float32
        )

    return lax.fori_loop(0, block_count, block_step, jnp.zeros_like(row_data))


def band_geometry(th_dev):
    lat_total = th_dev * lax.axis_size("lat")
    spacing = math.pi / lat_total
    band_start = lax.axis_index("lat") * th_dev
    colatitude = (
        (band_start + jnp.arange(th_dev, dtype=jnp.int32)).astype(jnp.float32) + 0.5
    ) * spacing
    return spacing, band_start, colatitude


def on_device(magnetic, kept_modes):
    radii_count, th_dev, ph_dev = (magnetic.shape[1], magnetic.shape[2], magnetic.shape[3])
    spacing, band_start, colatitude = band_geometry(th_dev)
    radius = (inner_radius + (jnp.arange(radii_count, dtype=jnp.float32) + 0.5) * spacing)[
        :, None, None
    ]
    inv_sin = (1.0 / jnp.sin(colatitude))[None, :, None]
    cotangent = (jnp.cos(colatitude) / jnp.sin(colatitude))[None, :, None]
    band_counts = lax.dynamic_slice_in_dim(kept_modes, band_start, th_dev)
    theta_pair = jnp.stack([magnetic[0], magnetic[2]])
    padded = extended(theta_pair, (("lat", 2),), 3)
    theta_diff = stencil_sum(padded, 2, th_dev)
    row_data = magnetic[:2].reshape(2 * radii_count * th_dev, ph_dev)
    lined = lax.all_to_all(row_data, "azim", split_axis=0, concat_axis=1, tiled=True)
    base_cos, base_sin = base_tables(lined.shape[1])
    rows_here = lined.shape[0]
    row_start = lax.axis_index("azim") * rows_here
    row_lat = (row_start + jnp.arange(rows_here, dtype=jnp.int32)) % th_dev
    row_kept = row_counts(band_counts, row_lat)
    azimuthal = spectral(lined, row_kept, base_cos, base_sin)
    flat_rows = lax.all_to_all(azimuthal, "azim", split_axis=1, concat_axis=0, tiled=True)
    azim_diff = flat_rows.reshape(2, radii_count, th_dev, ph_dev)
    b_polar = magnetic[1]
    b_azim = magnetic[2]
    j_radial = (
        theta_diff[1] + spacing * cotangent * b_azim - spacing * inv_sin * azim_diff[1]
    ) / radius
    j_polar = (spacing * inv_sin * azim_diff[0] - radial_diff(radius * b_azim)) / radius
    j_azim = (radial_diff(radius * b_polar) - theta_diff[0]) / radius
    return jnp.stack([j_radial, j_polar, j_azim])


CHUNKS = ((7,), (9,))
LAST = (7, 2)
TO_Y = [(0, 2), (2, 0), (1, 3), (3, 1)]
TO_C = [(0, 1), (1, 0), (2, 3), (3, 2)]
TO_YC = [(0, 3), (3, 0), (1, 2), (2, 1)]
VMEM = 52 * 1024 * 1024
SHORT = pl.CostEstimate(flops=1, bytes_accessed=1, transcendentals=0)


def halves(table):
    high = table.astype(jnp.bfloat16)
    low = (table - high.astype(np.float64)).astype(jnp.bfloat16)
    return np.stack([high, low])


def mode_tables(lon_total):
    quarter = lon_total // 4

    def pair(modes, length):
        phase = (np.arange(length)[:, None] * modes[None, :] % lon_total) * (2.0 * np.pi / lon_total)
        forward = np.concatenate([np.cos(phase), np.sin(phase)], axis=1)
        inverse = np.concatenate([-np.sin(phase), np.cos(phase)], axis=1).T
        return halves(forward), halves(inverse)

    zero = 4 * np.arange(quarter // 2)
    two = zero + 2
    odd = 2 * np.arange(quarter) + 1
    mode_ids = np.concatenate([zero, zero, two, two, odd, odd]).astype(np.float32)[None, :]
    return pair(zero, quarter), pair(two, quarter), pair(odd, 2 * quarter), mode_ids


def triple_dot(value, table):
    high = value.astype(jnp.bfloat16)
    low = (value - high.astype(jnp.float32)).astype(jnp.bfloat16)
    dot = functools.partial(jnp.dot, preferred_element_type=jnp.float32)
    return dot(high, table[0]) + dot(high, table[1]) + dot(low, table[0])


def transform_kernel(count, outputs, place, own, beside, diagonal, kept, gain, modes, *refs):
    across, tables, refs = refs[:count], refs[count : count + 6], refs[count + 6 :]
    (out_own, out_beside, *outs), held, sems = refs[:outputs], refs[outputs:-1], refs[-1]
    copies = [pltpu.make_async_copy(table, ref, sems.at[i]) for i, (table, ref) in enumerate(zip(tables, held))]
    for copy in copies:
        copy.start()
    quarter = own.shape[-1]
    rows = diagonal.shape[0] * diagonal.shape[1]
    sign_y = (1 - 2 * place[0]).astype(jnp.float32)
    sign_c = (1 - 2 * place[1]).astype(jnp.float32)
    first = place[1] == 0
    a, c, d = (ref[...].reshape(rows, quarter) for ref in (own, beside, diagonal))
    b = jnp.concatenate([ref[...].reshape(-1, quarter) for ref in across], axis=0)
    near, far = a + b, c + d
    near_odd, far_odd = sign_y * (a - b), sign_y * (c - d)
    odd = jnp.concatenate([jnp.where(first, near_odd, far_odd), jnp.where(first, far_odd, near_odd)], axis=1)
    limit = kept[...]
    ids = modes[...]
    weight = jnp.where(ids < limit, ids, 0.0) * gain[...]

    def filtered(value, which, start):
        copies[2 * which].wait()
        spectrum = triple_dot(value, held[2 * which])
        copies[2 * which + 1].wait()
        return triple_dot(spectrum * weight[:, start : start + spectrum.shape[1]], held[2 * which + 1])

    even0 = filtered(near + far, 0, 0)
    even2 = sign_c * filtered(sign_c * (near - far), 1, quarter)
    odd_out = sign_y * filtered(odd, 2, 2 * quarter)
    left, right = odd_out[:, :quarter], odd_out[:, quarter:]
    odd_near, odd_far = jnp.where(first, left, right), jnp.where(first, right, left)
    even_near, even_far = even0 + even2, even0 - even2
    shape = out_own.shape
    out_own[...] = (even_near + odd_near).reshape(shape)
    out_beside[...] = (even_far + odd_far).reshape(shape)
    across, diagonal = (even_near - odd_near).reshape(shape), (even_far - odd_far).reshape(shape)
    if len(outs) == 1:
        outs[0][0], outs[0][1] = across, diagonal
    else:
        outs[0][...] = across
        at = 0
        for out in outs[1:]:
            out[...] = diagonal[at : at + out.shape[0]]
            at += out.shape[0]


def transform(place, magnetic, start, parts, beside, diagonal, row_kept, row_gain, tables, cuts):
    depth, th_dev, quarter = diagonal.shape
    zero, two, odd, mode_ids = tables
    whole = pl.BlockSpec(memory_space=pltpu.VMEM)
    rows = depth * th_dev
    half = magnetic.shape[1] // 2
    part = (pl.Element(1), pl.Element(depth), pl.Element(th_dev), pl.Element(quarter))
    row_block = pl.BlockSpec((pl.Element(rows), pl.Element(1)), lambda i, p: (start * th_dev, 0))
    shape = (depth, th_dev, quarter)
    shapes = [shape, shape, (2,) + shape] if cuts is None else [shape] * 3 + [(cut, th_dev, quarter) for cut in cuts]
    grid_spec = pltpu.PrefetchScalarGridSpec(
        num_scalar_prefetch=1,
        grid=(1,),
        in_specs=[
            pl.BlockSpec(part, lambda i, p: (p[1], p[0] * half + start, 0, 0)),
            pl.BlockSpec(part[1:], lambda i, p: (start, 0, 0)),
            whole,
            row_block,
            row_block,
            whole,
        ]
        + [pl.BlockSpec((None,) + value.shape[1:], lambda i, p: (p[1], 0, 0, 0)) for value in parts]
        + [pl.BlockSpec(memory_space=pl.ANY)] * 6,
        out_specs=[whole] * len(shapes),
        scratch_shapes=[pltpu.VMEM(t.shape, jnp.bfloat16) for t in (*zero, *two, *odd)] + [pltpu.SemaphoreType.DMA((6,))],
    )
    return pl.pallas_call(
        functools.partial(transform_kernel, len(parts), len(shapes)),
        grid_spec=grid_spec,
        out_shape=[jax.ShapeDtypeStruct(shape, jnp.float32) for shape in shapes],
        compiler_params=pltpu.CompilerParams(vmem_limit_bytes=VMEM),
        cost_estimate=SHORT,
    )(place, magnetic, beside, diagonal, row_kept, row_gain, mode_ids, *parts, *zero, *two, *odd)


def edge_rows(magnetic):
    radii, th_dev, ph_dev = magnetic.shape[1:]
    edge = lambda at: pl.BlockSpec((None, radii, 8, ph_dev), lambda i: (2 * i, 0, at, 0))
    rows = pl.BlockSpec((None, 3, radii, ph_dev), lambda i: (i, 0, 0, 0))

    def kernel(top, bottom, last, first):
        for i in range(3):
            last[i] = bottom[:, 5 + i, :]
            first[i] = top[:, i, :]

    return pl.pallas_call(
        kernel,
        grid=(2,),
        in_specs=[edge(0), edge(th_dev // 8 - 1)],
        out_specs=[rows, rows],
        out_shape=[jax.ShapeDtypeStruct((2, 3, radii, ph_dev), jnp.float32)] * 2,
        compiler_params=pltpu.CompilerParams(vmem_limit_bytes=VMEM),
        cost_estimate=SHORT,
    )(magnetic, magnetic)


def copy_part(place, magnetic, start, depth):
    radii, th_dev, ph_dev = magnetic.shape[1:]

    def kernel(place, magnetic, out, sems):
        first = (1 - place[0]) * (radii // 2) + start
        copies = [
            pltpu.make_async_copy(magnetic.at[field, pl.ds(first, depth)], out.at[field], sems.at[field])
            for field in range(2)
        ]
        for copy in copies:
            copy.start()
        for copy in copies:
            copy.wait()

    return pl.pallas_call(
        kernel,
        grid_spec=pltpu.PrefetchScalarGridSpec(
            num_scalar_prefetch=1,
            grid=(1,),
            in_specs=[pl.BlockSpec(memory_space=pl.ANY)],
            out_specs=pl.BlockSpec(memory_space=pltpu.VMEM),
            scratch_shapes=[pltpu.SemaphoreType.DMA((2,))],
        ),
        out_shape=jax.ShapeDtypeStruct((2, depth, th_dev, ph_dev), jnp.float32),
        compiler_params=pltpu.CompilerParams(vmem_limit_bytes=VMEM),
        cost_estimate=SHORT,
    )(place, magnetic)


def local_part(place, magnetic, before, after, radius, inv_radius, cot, groups):
    width = 128
    radii, th_dev, ph_dev = magnetic.shape[1:]
    fixed = lambda *shape: pl.BlockSpec(shape, lambda i, p: (0, 0, 0))
    wide = lambda *lead: pl.BlockSpec(lead + (width,), lambda i, p: (0,) * len(lead) + (i,))
    weights = [stencil_coeffs[3 + offset] for offset in (1, 2, 3)]

    def kernel(place, field, before, after, radius, inv_radius, cot, *refs):
        azims, out, rows, layers = refs[:-3], *refs[-3:]
        inv = inv_radius[...]

        def theta(value, which):
            rows[:, 8 : 8 + th_dev, :] = value
            for i in range(3):
                rows[:, 5 + i, :] = before[which, i]
                rows[:, 8 + th_dev + i, :] = after[which, i]
            shifted = lambda offset: rows[:, 8 + offset : 8 + offset + th_dev, :]
            return sum(w * (shifted(o) - shifted(-o)) for o, w in enumerate(weights, 1))

        def radial(value):
            layers[3 : 3 + radii] = radius[...] * value
            shifted = lambda offset: layers[3 + offset : 3 + offset + radii]
            return sum(w * (shifted(o) - shifted(-o)) for o, w in enumerate(weights, 1))

        layers[:3] = jnp.zeros((3, th_dev, width), jnp.float32)
        layers[3 + radii :] = jnp.zeros((3, th_dev, width), jnp.float32)
        out[0] = (theta(field[2], 1) + cot[...] * field[2]) * inv
        out[1] = -radial(field[2]) * inv
        out[2] = (radial(field[1]) - theta(field[0], 0)) * inv
        for k, (_, _, own_half, start) in enumerate(groups):
            half = place[0] if own_half else 1 - place[0]
            here = pl.ds(half * (radii // 2) + start, azims[2 * k].shape[0])
            out[1 - place[1], here] += azims[2 * k][...]
            out[place[1], here] += azims[2 * k + 1][...]

    azims = [azim for own, crossed, _, _ in groups for azim in (own, crossed)]
    return pl.pallas_call(
        kernel,
        grid_spec=pltpu.PrefetchScalarGridSpec(
            num_scalar_prefetch=1,
            grid=(ph_dev // width,),
            in_specs=[
                wide(3, radii, th_dev),
                wide(2, 3, radii),
                wide(2, 3, radii),
                fixed(radii, 1, 1),
                fixed(radii, 1, 1),
                fixed(1, th_dev, 1),
            ]
            + [wide(*azim.shape[:-1]) for azim in azims],
            out_specs=wide(3, radii, th_dev),
            scratch_shapes=[
                pltpu.VMEM((radii, th_dev + 16, width), jnp.float32),
                pltpu.VMEM((radii + 6, th_dev, width), jnp.float32),
            ],
        ),
        out_shape=jax.ShapeDtypeStruct(magnetic.shape, jnp.float32),
        compiler_params=pltpu.CompilerParams(vmem_limit_bytes=VMEM),
        cost_estimate=SHORT,
    )(place, magnetic, before, after, radius, inv_radius, cot, *azims)


def add_one(place, current, azim, own_field, start):
    depth, th_dev, ph_dev = azim.shape
    half = current.shape[1] // 2
    part = lambda p: 1 - p[1] if own_field else p[1]
    block = pl.BlockSpec(
        (pl.Element(1), pl.Element(depth), pl.Element(th_dev), pl.Element(ph_dev)),
        lambda i, p: (part(p), (1 - p[0]) * half + start, 0, 0),
    )

    def kernel(place, base, azim, out):
        out[0] = base[0] + azim[...]

    return pl.pallas_call(
        kernel,
        grid_spec=pltpu.PrefetchScalarGridSpec(
            num_scalar_prefetch=1,
            grid=(1,),
            in_specs=[block, pl.BlockSpec(memory_space=pltpu.VMEM)],
            out_specs=block,
        ),
        out_shape=jax.ShapeDtypeStruct(current.shape, jnp.float32),
        input_output_aliases={1: 0},
        compiler_params=pltpu.CompilerParams(vmem_limit_bytes=VMEM // 6),
        cost_estimate=SHORT,
    )(place, current, azim)


def put_sum(place, current, base, azim, start):
    depth = azim.shape[0]
    half = current.shape[1] // 2
    whole = pl.BlockSpec(memory_space=pltpu.VMEM)

    def kernel(place, current, base, azim, out, total, sem):
        total[...] = base[...] + azim[...]
        copy = pltpu.make_async_copy(total, out.at[place[1], pl.ds((1 - place[0]) * half + start, depth)], sem)
        copy.start()
        copy.wait()

    return pl.pallas_call(
        kernel,
        grid_spec=pltpu.PrefetchScalarGridSpec(
            num_scalar_prefetch=1,
            grid=(1,),
            in_specs=[pl.BlockSpec(memory_space=pl.ANY), whole, whole],
            out_specs=pl.BlockSpec(memory_space=pl.ANY),
            scratch_shapes=[pltpu.VMEM(azim.shape, jnp.float32), pltpu.SemaphoreType.DMA],
        ),
        out_shape=jax.ShapeDtypeStruct(current.shape, jnp.float32),
        input_output_aliases={1: 0},
        compiler_params=pltpu.CompilerParams(vmem_limit_bytes=VMEM // 6),
        cost_estimate=SHORT,
    )(place, current, base, azim)


def after(first, *then):
    return lax.optimization_barrier((first, then))[1]


def on_four(magnetic, kept_modes):
    radii, th_dev, ph_dev = (magnetic.shape[1], magnetic.shape[2], magnetic.shape[3])
    half = radii // 2
    unit = half // sum(map(sum, CHUNKS))
    pieces = [[unit * piece for piece in chunk] for chunk in CHUNKS]
    depths = [sum(chunk) for chunk in pieces]
    last_cuts = [unit * piece for piece in LAST]
    starts = [sum(depths[:k]) for k in range(len(depths))]
    index = lax.axis_index("azim")
    y, c = index // 2, index % 2
    place = jnp.stack([y, c]).astype(jnp.int32)
    send = lambda value, pairs: lax.ppermute(value, "azim", pairs)

    def cut(source, field, start, length):
        return lax.dynamic_slice(source, (field, start, 0, 0), (1, length, th_dev, ph_dev))[0]

    arrived = []
    source = magnetic
    for k, chunk in enumerate(pieces):
        arrived.append([])
        for i, depth in enumerate(chunk):
            at = (1 - y) * half + starts[k] + sum(chunk[:i])
            if k == 0:
                both = copy_part(place, source, starts[k] + sum(chunk[:i]), depth)
            else:
                both = lax.dynamic_slice(source, (0, at, 0, 0), (2, depth, th_dev, ph_dev))
            (source,) = after(both, source)
            arrived[k].append(send(both, TO_Y))
        if k == 0:
            lat_size = lax.axis_size("lat")
            up = [(i, i + 1) for i in range(lat_size - 1)]
            down = [(i + 1, i) for i in range(lat_size - 1)]
            last, first = edge_rows(source)
            (source,) = after((last, first), source)
            north, south = lax.ppermute(last, "lat", up), lax.ppermute(first, "lat", down)
            to_c = cut(source, 1 - c, y * half, half)
            (source,) = after(to_c, source)
            beside = send(to_c, TO_C)

    spacing, band_start, colatitude = band_geometry(th_dev)
    radius = (inner_radius + (jnp.arange(radii, dtype=jnp.float32) + 0.5) * spacing)[:, None, None]
    inv_radius = 1.0 / radius
    inv_sin = 1.0 / jnp.sin(colatitude)
    cot = spacing * (jnp.cos(colatitude) / jnp.sin(colatitude))[None, :, None]
    sign_c = (1 - 2 * c).astype(jnp.float32)
    row_gain = (sign_c * spacing * 0.5 / ph_dev) * inv_sin[None, :] * inv_radius[:, 0]
    row_gain = lax.dynamic_slice_in_dim(row_gain, y * half, half).reshape(half * th_dev, 1)
    band_counts = lax.dynamic_slice_in_dim(kept_modes, band_start, th_dev).astype(jnp.float32)
    row_kept = jnp.broadcast_to(band_counts[None, :], (half, th_dev)).reshape(half * th_dev, 1)

    tables = mode_tables(4 * ph_dev)
    mine, from_c, returned = [], [], []
    for k, start in enumerate(starts):
        parts = arrived[k]
        if k > 0:
            parts = after(mine[-1], *parts)
        (row_gain,) = after(from_c[-1] if k > 0 else (north, south), row_gain)
        diagonal = send(jnp.concatenate([cut(part, 1 - c, 0, part.shape[1]) for part in parts]), TO_C)
        cuts = None if k + 1 < len(starts) else last_cuts
        out, to_c, to_y, *to_yc = transform(
            place, magnetic, start, parts, beside, diagonal, row_kept, row_gain, tables, cuts
        )
        mine.append(out)
        from_c.append(send(to_c, TO_C))
        returned.append(send(to_y, TO_Y))
    final = [(returned.pop(), True, starts[-1])]
    for i, value in enumerate(to_yc):
        final.append((send(value, TO_YC), False, starts[-1] + sum(last_cuts[:i])))

    groups = [(own, crossed, True, start) for own, crossed, start in zip(mine, from_c, starts)]
    for value, start in zip(returned, starts):
        groups.append((value[0], send(value[1], TO_C), False, start))
    north, south = after(mine[-1], north, south)
    current = local_part(place, magnetic, north, south, radius, inv_radius, cot, groups)
    azim, _, start = final[-1]
    base = cut(current, c, (1 - y) * half + start, azim.shape[0])
    (current,) = after(base, current)
    for value, own_field, at in final[:-1]:
        current = add_one(place, current, value, own_field, at)
    return put_sum(place, current, base, azim, start)


def solution(mesh):
    placed = (P(None, None, "lat", "azim"), P())

    def run(magnetic, kept_modes):
        radii, ph_dev = magnetic.shape[1], magnetic.shape[3]
        four = lax.axis_size("azim") == 4 and radii % (2 * sum(map(sum, CHUNKS))) == 0 and ph_dev % 256 == 0
        return (on_four if four else on_device)(magnetic, kept_modes)

    return jax.shard_map(
        run,
        mesh=mesh,
        in_specs=placed,
        out_specs=P(None, None, "lat", "azim"),
        check_vma=False,
    )
```

```python
import functools
import math

import jax
import jax.numpy as jnp
import numpy as np
from jax import lax
from jax.experimental import pallas as pl
from jax.experimental.pallas import tpu as pltpu
from jax.sharding import PartitionSpec as P

MB = 128


inner_radius = 0.7
stencil_coeffs = (-1.0 / 60.0, 3.0 / 20.0, -3.0 / 4.0, 0.0, 3.0 / 4.0, -3.0 / 20.0, 1.0 / 60.0)


def extended(value, sides, width):
    for axis, dim in sides:
        size, length = (lax.axis_size(axis), value.shape[dim])
        up = [(i, (i + 1) % size) for i in range(size - 1)]
        down = [(j, i) for i, j in up]
        last = lax.slice_in_dim(value, length - width, length, axis=dim)
        first = lax.slice_in_dim(value, 0, width, axis=dim)
        before = lax.ppermute(last, axis, up)
        after = lax.ppermute(first, axis, down)
        value = jnp.concatenate([before, value, after], axis=dim)
    return value


def stencil_sum(padded, split_axis, length):
    total = jnp.zeros(lax.slice_in_dim(padded, 3, 3 + length, axis=split_axis).shape, jnp.float32)
    for offset in range(-3, 4):
        if offset != 0:
            total = total + stencil_coeffs[offset + 3] * lax.slice_in_dim(
                padded, 3 + offset, 3 + offset + length, axis=split_axis
            )
    return total


def radial_diff(values):
    widths = [(0, 0)] * values.ndim
    widths[0] = (3, 3)
    return stencil_sum(jnp.pad(values, widths), 0, values.shape[0])


def row_counts(band_counts, row_lat):
    lat_ids = jnp.arange(band_counts.shape[0], dtype=jnp.int32)
    match = row_lat[:, None] == lat_ids[None, :]
    return jnp.sum(jnp.where(match, band_counts[None, :], 0), axis=1)


def base_tables(lon_total):
    columns = jnp.arange(lon_total, dtype=jnp.int32)
    mode_ids = jnp.arange(MB, dtype=jnp.int32)
    phase = (mode_ids[:, None] * columns[None, :] % lon_total).astype(jnp.float32) * (
        2.0 * math.pi / lon_total
    )
    return (jnp.cos(phase), jnp.sin(phase))


def spectral(row_data, row_kept, base_cos, base_sin):
    lon_total = row_data.shape[1]
    block_count = (jnp.max(row_kept) + MB - 1) // MB
    columns = jnp.arange(lon_total, dtype=jnp.int32)

    def block_step(block, total):
        mode_ids = block * MB + jnp.arange(MB, dtype=jnp.int32)
        offset_phase = (block * MB * columns % lon_total).astype(jnp.float32) * (
            2.0 * math.pi / lon_total
        )
        offset_cos = jnp.cos(offset_phase)[None, :]
        offset_sin = jnp.sin(offset_phase)[None, :]
        cos_rows = base_cos * offset_cos - base_sin * offset_sin
        sin_rows = base_sin * offset_cos + base_cos * offset_sin
        table = jnp.concatenate([cos_rows, sin_rows], axis=0)
        spectrum = lax.dot_general(
            row_data,
            table,
            (((1,), (1,)), ((), ())),
            precision=lax.Precision.HIGHEST,
            preferred_element_type=jnp.float32,
        )
        weight = jnp.where(mode_ids[None, :] < row_kept[:, None], mode_ids[None, :], 0).astype(
            jnp.float32
        ) * (2.0 / lon_total)
        scaled = jnp.concatenate([spectrum[:, MB:] * weight, -spectrum[:, :MB] * weight], axis=1)
        return total + jnp.dot(
            scaled, table, precision=lax.Precision.HIGHEST, preferred_element_type=jnp.float32
        )

    return lax.fori_loop(0, block_count, block_step, jnp.zeros_like(row_data))


def band_geometry(th_dev):
    lat_total = th_dev * lax.axis_size("lat")
    spacing = math.pi / lat_total
    band_start = lax.axis_index("lat") * th_dev
    colatitude = (
        (band_start + jnp.arange(th_dev, dtype=jnp.int32)).astype(jnp.float32) + 0.5
    ) * spacing
    return spacing, band_start, colatitude


def on_device(magnetic, kept_modes):
    radii_count, th_dev, ph_dev = (magnetic.shape[1], magnetic.shape[2], magnetic.shape[3])
    spacing, band_start, colatitude = band_geometry(th_dev)
    radius = (inner_radius + (jnp.arange(radii_count, dtype=jnp.float32) + 0.5) * spacing)[
        :, None, None
    ]
    inv_sin = (1.0 / jnp.sin(colatitude))[None, :, None]
    cotangent = (jnp.cos(colatitude) / jnp.sin(colatitude))[None, :, None]
    band_counts = lax.dynamic_slice_in_dim(kept_modes, band_start, th_dev)
    theta_pair = jnp.stack([magnetic[0], magnetic[2]])
    padded = extended(theta_pair, (("lat", 2),), 3)
    theta_diff = stencil_sum(padded, 2, th_dev)
    row_data = magnetic[:2].reshape(2 * radii_count * th_dev, ph_dev)
    lined = lax.all_to_all(row_data, "azim", split_axis=0, concat_axis=1, tiled=True)
    base_cos, base_sin = base_tables(lined.shape[1])
    rows_here = lined.shape[0]
    row_start = lax.axis_index("azim") * rows_here
    row_lat = (row_start + jnp.arange(rows_here, dtype=jnp.int32)) % th_dev
    row_kept = row_counts(band_counts, row_lat)
    azimuthal = spectral(lined, row_kept, base_cos, base_sin)
    flat_rows = lax.all_to_all(azimuthal, "azim", split_axis=1, concat_axis=0, tiled=True)
    azim_diff = flat_rows.reshape(2, radii_count, th_dev, ph_dev)
    b_polar = magnetic[1]
    b_azim = magnetic[2]
    j_radial = (
        theta_diff[1] + spacing * cotangent * b_azim - spacing * inv_sin * azim_diff[1]
    ) / radius
    j_polar = (spacing * inv_sin * azim_diff[0] - radial_diff(radius * b_azim)) / radius
    j_azim = (radial_diff(radius * b_polar) - theta_diff[0]) / radius
    return jnp.stack([j_radial, j_polar, j_azim])


CHUNKS = (7, 9)
LAST = (7, 2)
TO_Y = [(0, 2), (2, 0), (1, 3), (3, 1)]
TO_C = [(0, 1), (1, 0), (2, 3), (3, 2)]
TO_YC = [(0, 3), (3, 0), (1, 2), (2, 1)]
VMEM = 52 * 1024 * 1024
SHORT = pl.CostEstimate(flops=1, bytes_accessed=1, transcendentals=0)


def halves(table):
    high = table.astype(jnp.bfloat16)
    low = (table - high.astype(np.float64)).astype(jnp.bfloat16)
    return np.stack([high, low])


def mode_tables(lon_total):
    quarter = lon_total // 4

    def pair(modes, length):
        phase = (np.arange(length)[:, None] * modes[None, :] % lon_total) * (2.0 * np.pi / lon_total)
        forward = np.concatenate([np.cos(phase), np.sin(phase)], axis=1)
        inverse = np.concatenate([-np.sin(phase), np.cos(phase)], axis=1).T
        return halves(forward), halves(inverse)

    zero = 4 * np.arange(quarter // 2)
    two = zero + 2
    odd = 2 * np.arange(quarter) + 1
    mode_ids = np.concatenate([zero, zero, two, two, odd, odd]).astype(np.float32)[None, :]
    return pair(zero, quarter), pair(two, quarter), pair(odd, 2 * quarter), mode_ids


def triple_dot(value, table):
    high = value.astype(jnp.bfloat16)
    low = (value - high.astype(jnp.float32)).astype(jnp.bfloat16)
    dot = functools.partial(jnp.dot, preferred_element_type=jnp.float32)
    return dot(high, table[0]) + dot(high, table[1]) + dot(low, table[0])


def transform_kernel(place, own, across, beside, diagonal, kept, gain, modes, *refs):
    tables, (out_own, out_beside, *outs), held, sems = refs[:6], refs[6:-7], refs[-7:-1], refs[-1]
    copies = [pltpu.make_async_copy(table, ref, sems.at[i]) for i, (table, ref) in enumerate(zip(tables, held))]
    for copy in copies:
        copy.start()
    quarter = own.shape[-1]
    rows = across.shape[0] * across.shape[1]
    sign_y = (1 - 2 * place[0]).astype(jnp.float32)
    sign_c = (1 - 2 * place[1]).astype(jnp.float32)
    first = place[1] == 0
    a, b, c, d = (ref[...].reshape(rows, quarter) for ref in (own, across, beside, diagonal))
    near, far = a + b, c + d
    near_odd, far_odd = sign_y * (a - b), sign_y * (c - d)
    odd = jnp.concatenate([jnp.where(first, near_odd, far_odd), jnp.where(first, far_odd, near_odd)], axis=1)
    limit = kept[...]
    ids = modes[...]
    weight = jnp.where(ids < limit, ids, 0.0) * gain[...]

    def filtered(value, which, start):
        copies[2 * which].wait()
        spectrum = triple_dot(value, held[2 * which])
        copies[2 * which + 1].wait()
        return triple_dot(spectrum * weight[:, start : start + spectrum.shape[1]], held[2 * which + 1])

    even0 = filtered(near + far, 0, 0)
    even2 = sign_c * filtered(sign_c * (near - far), 1, quarter)
    odd_out = sign_y * filtered(odd, 2, 2 * quarter)
    left, right = odd_out[:, :quarter], odd_out[:, quarter:]
    odd_near, odd_far = jnp.where(first, left, right), jnp.where(first, right, left)
    even_near, even_far = even0 + even2, even0 - even2
    shape = out_own.shape
    out_own[...] = (even_near + odd_near).reshape(shape)
    out_beside[...] = (even_far + odd_far).reshape(shape)
    across, diagonal = (even_near - odd_near).reshape(shape), (even_far - odd_far).reshape(shape)
    if len(outs) == 1:
        outs[0][0], outs[0][1] = across, diagonal
    else:
        outs[0][...] = across
        at = 0
        for out in outs[1:]:
            out[...] = diagonal[at : at + out.shape[0]]
            at += out.shape[0]


def transform(place, magnetic, start, across, beside, diagonal, row_kept, row_gain, tables, cuts):
    depth, th_dev, quarter = across.shape[1:]
    zero, two, odd, mode_ids = tables
    whole = pl.BlockSpec(memory_space=pltpu.VMEM)
    rows = depth * th_dev
    half = magnetic.shape[1] // 2
    shape = (depth, th_dev, quarter)
    part = tuple(pl.Element(size) for size in shape)
    row_block = pl.BlockSpec((pl.Element(rows), pl.Element(1)), lambda i, p: (start * th_dev, 0))
    shapes = [shape, shape, (2,) + shape] if cuts is None else [shape] * 3 + [(cut, th_dev, quarter) for cut in cuts]
    if diagonal is None:
        diagonal, whole_diagonal = across, pl.BlockSpec((None,) + shape, lambda i, p: (1, 0, 0, 0))
        across_part = pl.BlockSpec((None,) + shape, lambda i, p: (0, 0, 0, 0))
    else:
        whole_diagonal, across_part = whole, pl.BlockSpec((None,) + shape, lambda i, p: (p[1], 0, 0, 0))
    grid_spec = pltpu.PrefetchScalarGridSpec(
        num_scalar_prefetch=1,
        grid=(1,),
        in_specs=[
            pl.BlockSpec((pl.Element(1),) + part, lambda i, p: (p[1], p[0] * half + start, 0, 0)),
            across_part,
            pl.BlockSpec(part, lambda i, p: (start, 0, 0)),
            whole_diagonal,
            row_block,
            row_block,
            whole,
        ]
        + [pl.BlockSpec(memory_space=pl.ANY)] * 6,
        out_specs=[whole] * len(shapes),
        scratch_shapes=[pltpu.VMEM(t.shape, jnp.bfloat16) for t in (*zero, *two, *odd)] + [pltpu.SemaphoreType.DMA((6,))],
    )
    return pl.pallas_call(
        transform_kernel,
        grid_spec=grid_spec,
        out_shape=[jax.ShapeDtypeStruct(shape, jnp.float32) for shape in shapes],
        compiler_params=pltpu.CompilerParams(vmem_limit_bytes=VMEM),
        cost_estimate=SHORT,
    )(place, magnetic, across, beside, diagonal, row_kept, row_gain, mode_ids, *zero, *two, *odd)


def edge_rows(magnetic):
    radii, th_dev, ph_dev = magnetic.shape[1:]
    edge = lambda at: pl.BlockSpec((None, radii, 8, ph_dev), lambda i: (2 * i, 0, at, 0))
    rows = pl.BlockSpec((None, 3, radii, ph_dev), lambda i: (i, 0, 0, 0))

    def kernel(top, bottom, last, first):
        for i in range(3):
            last[i] = bottom[:, 5 + i, :]
            first[i] = top[:, i, :]

    return pl.pallas_call(
        kernel,
        grid=(2,),
        in_specs=[edge(0), edge(th_dev // 8 - 1)],
        out_specs=[rows, rows],
        out_shape=[jax.ShapeDtypeStruct((2, 3, radii, ph_dev), jnp.float32)] * 2,
        compiler_params=pltpu.CompilerParams(vmem_limit_bytes=VMEM),
        cost_estimate=SHORT,
    )(magnetic, magnetic)


def copy_part(place, magnetic, start, depth):
    radii, th_dev, ph_dev = magnetic.shape[1:]

    def kernel(place, magnetic, out, sems):
        first = (1 - place[0]) * (radii // 2) + start
        copies = [
            pltpu.make_async_copy(magnetic.at[field, pl.ds(first, depth)], out.at[field], sems.at[field])
            for field in range(2)
        ]
        for copy in copies:
            copy.start()
        for copy in copies:
            copy.wait()

    return pl.pallas_call(
        kernel,
        grid_spec=pltpu.PrefetchScalarGridSpec(
            num_scalar_prefetch=1,
            grid=(1,),
            in_specs=[pl.BlockSpec(memory_space=pl.ANY)],
            out_specs=pl.BlockSpec(memory_space=pltpu.VMEM),
            scratch_shapes=[pltpu.SemaphoreType.DMA((2,))],
        ),
        out_shape=jax.ShapeDtypeStruct((2, depth, th_dev, ph_dev), jnp.float32),
        compiler_params=pltpu.CompilerParams(vmem_limit_bytes=VMEM),
        cost_estimate=SHORT,
    )(place, magnetic)


def local_part(place, magnetic, before, after, radius, inv_radius, cot, groups):
    width = 128
    radii, th_dev, ph_dev = magnetic.shape[1:]
    fixed = lambda *shape: pl.BlockSpec(shape, lambda i, p: (0, 0, 0))
    wide = lambda *lead: pl.BlockSpec(lead + (width,), lambda i, p: (0,) * len(lead) + (i,))
    weights = [stencil_coeffs[3 + offset] for offset in (1, 2, 3)]

    def kernel(place, field, before, after, radius, inv_radius, cot, *refs):
        azims, out, rows, layers = refs[:-3], *refs[-3:]
        inv = inv_radius[...]

        def theta(value, which):
            rows[:, 8 : 8 + th_dev, :] = value
            for i in range(3):
                rows[:, 5 + i, :] = before[which, i]
                rows[:, 8 + th_dev + i, :] = after[which, i]
            shifted = lambda offset: rows[:, 8 + offset : 8 + offset + th_dev, :]
            return sum(w * (shifted(o) - shifted(-o)) for o, w in enumerate(weights, 1))

        def radial(value):
            layers[3 : 3 + radii] = radius[...] * value
            shifted = lambda offset: layers[3 + offset : 3 + offset + radii]
            return sum(w * (shifted(o) - shifted(-o)) for o, w in enumerate(weights, 1))

        layers[:3] = jnp.zeros((3, th_dev, width), jnp.float32)
        layers[3 + radii :] = jnp.zeros((3, th_dev, width), jnp.float32)
        out[0] = (theta(field[2], 1) + cot[...] * field[2]) * inv
        out[1] = -radial(field[2]) * inv
        out[2] = (radial(field[1]) - theta(field[0], 0)) * inv
        for k, (_, _, own_half, start) in enumerate(groups):
            half = place[0] if own_half else 1 - place[0]
            here = pl.ds(half * (radii // 2) + start, azims[2 * k].shape[0])
            out[1 - place[1], here] += azims[2 * k][...]
            out[place[1], here] += azims[2 * k + 1][...]

    azims = [azim for own, crossed, _, _ in groups for azim in (own, crossed)]
    return pl.pallas_call(
        kernel,
        grid_spec=pltpu.PrefetchScalarGridSpec(
            num_scalar_prefetch=1,
            grid=(ph_dev // width,),
            in_specs=[
                wide(3, radii, th_dev),
                wide(2, 3, radii),
                wide(2, 3, radii),
                fixed(radii, 1, 1),
                fixed(radii, 1, 1),
                fixed(1, th_dev, 1),
            ]
            + [wide(*azim.shape[:-1]) for azim in azims],
            out_specs=wide(3, radii, th_dev),
            scratch_shapes=[
                pltpu.VMEM((radii, th_dev + 16, width), jnp.float32),
                pltpu.VMEM((radii + 6, th_dev, width), jnp.float32),
            ],
        ),
        out_shape=jax.ShapeDtypeStruct(magnetic.shape, jnp.float32),
        compiler_params=pltpu.CompilerParams(vmem_limit_bytes=VMEM),
        cost_estimate=SHORT,
    )(place, magnetic, before, after, radius, inv_radius, cot, *azims)


def add_one(place, current, azim, own_field, start):
    depth, th_dev, ph_dev = azim.shape
    half = current.shape[1] // 2
    part = lambda p: 1 - p[1] if own_field else p[1]
    block = pl.BlockSpec(
        (pl.Element(1), pl.Element(depth), pl.Element(th_dev), pl.Element(ph_dev)),
        lambda i, p: (part(p), (1 - p[0]) * half + start, 0, 0),
    )

    def kernel(place, base, azim, out):
        out[0] = base[0] + azim[...]

    return pl.pallas_call(
        kernel,
        grid_spec=pltpu.PrefetchScalarGridSpec(
            num_scalar_prefetch=1,
            grid=(1,),
            in_specs=[block, pl.BlockSpec(memory_space=pltpu.VMEM)],
            out_specs=block,
        ),
        out_shape=jax.ShapeDtypeStruct(current.shape, jnp.float32),
        input_output_aliases={1: 0},
        compiler_params=pltpu.CompilerParams(vmem_limit_bytes=VMEM // 6),
        cost_estimate=SHORT,
    )(place, current, azim)


def put_sum(place, current, base, azim, start):
    depth = azim.shape[0]
    half = current.shape[1] // 2
    whole = pl.BlockSpec(memory_space=pltpu.VMEM)

    def kernel(place, current, base, azim, out, total, sem):
        total[...] = base[...] + azim[...]
        copy = pltpu.make_async_copy(total, out.at[place[1], pl.ds((1 - place[0]) * half + start, depth)], sem)
        copy.start()
        copy.wait()

    return pl.pallas_call(
        kernel,
        grid_spec=pltpu.PrefetchScalarGridSpec(
            num_scalar_prefetch=1,
            grid=(1,),
            in_specs=[pl.BlockSpec(memory_space=pl.ANY), whole, whole],
            out_specs=pl.BlockSpec(memory_space=pl.ANY),
            scratch_shapes=[pltpu.VMEM(azim.shape, jnp.float32), pltpu.SemaphoreType.DMA],
        ),
        out_shape=jax.ShapeDtypeStruct(current.shape, jnp.float32),
        input_output_aliases={1: 0},
        compiler_params=pltpu.CompilerParams(vmem_limit_bytes=VMEM // 6),
        cost_estimate=SHORT,
    )(place, current, base, azim)


def after(first, *then):
    return lax.optimization_barrier((first, then))[1]


def on_four(magnetic, kept_modes):
    radii, th_dev, ph_dev = (magnetic.shape[1], magnetic.shape[2], magnetic.shape[3])
    half = radii // 2
    unit = half // sum(CHUNKS)
    depths = [unit * part for part in CHUNKS]
    last_cuts = [unit * part for part in LAST]
    starts = [sum(depths[:k]) for k in range(len(depths))]
    index = lax.axis_index("azim")
    y, c = index // 2, index % 2
    place = jnp.stack([y, c]).astype(jnp.int32)
    send = lambda value, pairs: lax.ppermute(value, "azim", pairs)

    def cut(source, field, start, length):
        return lax.dynamic_slice(source, (field, start, 0, 0), (1, length, th_dev, ph_dev))[0]

    both = copy_part(place, magnetic, 0, depths[0])
    (source,) = after(both, magnetic)
    arrived = [send(both, TO_Y)]
    last, first = edge_rows(source)
    (source,) = after((last, first), source)
    crossing = []
    for start, depth in zip(starts[1:], depths[1:]):
        to_c = cut(source, 1 - c, (1 - y) * half + start, depth)
        (source,) = after(to_c, source)
        crossing.append(send(to_c, TO_C))
    to_c = cut(source, 1 - c, y * half, half)
    (source,) = after(to_c, source)
    beside = send(to_c, TO_C)
    for start, depth, crossed in zip(starts[1:], depths[1:], crossing):
        both = jnp.stack([cut(source, c, (1 - y) * half + start, depth), crossed])
        arrived.append(send(both, TO_Y))
    lat_size = lax.axis_size("lat")
    up = [(i, i + 1) for i in range(lat_size - 1)]
    down = [(i + 1, i) for i in range(lat_size - 1)]
    north, south = lax.ppermute(last, "lat", up), lax.ppermute(first, "lat", down)

    spacing, band_start, colatitude = band_geometry(th_dev)
    radius = (inner_radius + (jnp.arange(radii, dtype=jnp.float32) + 0.5) * spacing)[:, None, None]
    inv_radius = 1.0 / radius
    inv_sin = 1.0 / jnp.sin(colatitude)
    cot = spacing * (jnp.cos(colatitude) / jnp.sin(colatitude))[None, :, None]
    sign_c = (1 - 2 * c).astype(jnp.float32)
    row_gain = (sign_c * spacing * 0.5 / ph_dev) * inv_sin[None, :] * inv_radius[:, 0]
    row_gain = lax.dynamic_slice_in_dim(row_gain, y * half, half).reshape(half * th_dev, 1)
    band_counts = lax.dynamic_slice_in_dim(kept_modes, band_start, th_dev).astype(jnp.float32)
    row_kept = jnp.broadcast_to(band_counts[None, :], (half, th_dev)).reshape(half * th_dev, 1)

    tables = mode_tables(4 * ph_dev)
    mine, from_c, returned = [], [], []
    for k, start in enumerate(starts):
        across, diagonal = arrived[k], None
        (row_gain,) = after(from_c[-1] if k > 0 else (north, south), row_gain)
        if k == 0:
            diagonal = send(cut(across, 1 - c, 0, depths[k]), TO_C)
        else:
            (across,) = after(mine[-1], across)
        cuts = None if k + 1 < len(starts) else last_cuts
        out, to_c, to_y, *to_yc = transform(
            place, magnetic, start, across, beside, diagonal, row_kept, row_gain, tables, cuts
        )
        mine.append(out)
        if k + 1 < len(starts):
            (to_c,) = after(arrived[k + 1], to_c)
        from_c.append(send(to_c, TO_C))
        returned.append(send(to_y, TO_Y))
    final = [(returned.pop(), True, starts[-1])]
    for i, value in enumerate(to_yc):
        final.append((send(value, TO_YC), False, starts[-1] + sum(last_cuts[:i])))

    groups = [(own, crossed, True, start) for own, crossed, start in zip(mine, from_c, starts)]
    for value, start in zip(returned, starts):
        groups.append((value[0], send(value[1], TO_C), False, start))
    north, south = after(mine[-1], north, south)
    current = local_part(place, magnetic, north, south, radius, inv_radius, cot, groups)
    azim, _, start = final[-1]
    base = cut(current, c, (1 - y) * half + start, azim.shape[0])
    (current,) = after(base, current)
    for value, own_field, at in final[:-1]:
        current = add_one(place, current, value, own_field, at)
    return put_sum(place, current, base, azim, start)


def solution(mesh):
    placed = (P(None, None, "lat", "azim"), P())

    def run(magnetic, kept_modes):
        radii, ph_dev = magnetic.shape[1], magnetic.shape[3]
        four = lax.axis_size("azim") == 4 and radii % (2 * sum(CHUNKS)) == 0 and ph_dev % 256 == 0
        return (on_four if four else on_device)(magnetic, kept_modes)

    return jax.shard_map(
        run,
        mesh=mesh,
        in_specs=placed,
        out_specs=P(None, None, "lat", "azim"),
        check_vma=False,
    )
```

```python
import functools
import math

import jax
import jax.numpy as jnp
import numpy as np
from jax import lax
from jax.experimental import pallas as pl
from jax.experimental.pallas import tpu as pltpu
from jax.sharding import PartitionSpec as P

MB = 128


inner_radius = 0.7
stencil_coeffs = (-1.0 / 60.0, 3.0 / 20.0, -3.0 / 4.0, 0.0, 3.0 / 4.0, -3.0 / 20.0, 1.0 / 60.0)


def extended(value, sides, width):
    for axis, dim in sides:
        size, length = (lax.axis_size(axis), value.shape[dim])
        up = [(i, (i + 1) % size) for i in range(size - 1)]
        down = [(j, i) for i, j in up]
        last = lax.slice_in_dim(value, length - width, length, axis=dim)
        first = lax.slice_in_dim(value, 0, width, axis=dim)
        before = lax.ppermute(last, axis, up)
        after = lax.ppermute(first, axis, down)
        value = jnp.concatenate([before, value, after], axis=dim)
    return value


def stencil_sum(padded, split_axis, length):
    total = jnp.zeros(lax.slice_in_dim(padded, 3, 3 + length, axis=split_axis).shape, jnp.float32)
    for offset in range(-3, 4):
        if offset != 0:
            total = total + stencil_coeffs[offset + 3] * lax.slice_in_dim(
                padded, 3 + offset, 3 + offset + length, axis=split_axis
            )
    return total


def radial_diff(values):
    widths = [(0, 0)] * values.ndim
    widths[0] = (3, 3)
    return stencil_sum(jnp.pad(values, widths), 0, values.shape[0])


def row_counts(band_counts, row_lat):
    lat_ids = jnp.arange(band_counts.shape[0], dtype=jnp.int32)
    match = row_lat[:, None] == lat_ids[None, :]
    return jnp.sum(jnp.where(match, band_counts[None, :], 0), axis=1)


def base_tables(lon_total):
    columns = jnp.arange(lon_total, dtype=jnp.int32)
    mode_ids = jnp.arange(MB, dtype=jnp.int32)
    phase = (mode_ids[:, None] * columns[None, :] % lon_total).astype(jnp.float32) * (
        2.0 * math.pi / lon_total
    )
    return (jnp.cos(phase), jnp.sin(phase))


def spectral(row_data, row_kept, base_cos, base_sin):
    lon_total = row_data.shape[1]
    block_count = (jnp.max(row_kept) + MB - 1) // MB
    columns = jnp.arange(lon_total, dtype=jnp.int32)

    def block_step(block, total):
        mode_ids = block * MB + jnp.arange(MB, dtype=jnp.int32)
        offset_phase = (block * MB * columns % lon_total).astype(jnp.float32) * (
            2.0 * math.pi / lon_total
        )
        offset_cos = jnp.cos(offset_phase)[None, :]
        offset_sin = jnp.sin(offset_phase)[None, :]
        cos_rows = base_cos * offset_cos - base_sin * offset_sin
        sin_rows = base_sin * offset_cos + base_cos * offset_sin
        table = jnp.concatenate([cos_rows, sin_rows], axis=0)
        spectrum = lax.dot_general(
            row_data,
            table,
            (((1,), (1,)), ((), ())),
            precision=lax.Precision.HIGHEST,
            preferred_element_type=jnp.float32,
        )
        weight = jnp.where(mode_ids[None, :] < row_kept[:, None], mode_ids[None, :], 0).astype(
            jnp.float32
        ) * (2.0 / lon_total)
        scaled = jnp.concatenate([spectrum[:, MB:] * weight, -spectrum[:, :MB] * weight], axis=1)
        return total + jnp.dot(
            scaled, table, precision=lax.Precision.HIGHEST, preferred_element_type=jnp.float32
        )

    return lax.fori_loop(0, block_count, block_step, jnp.zeros_like(row_data))


def band_geometry(th_dev):
    lat_total = th_dev * lax.axis_size("lat")
    spacing = math.pi / lat_total
    band_start = lax.axis_index("lat") * th_dev
    colatitude = (
        (band_start + jnp.arange(th_dev, dtype=jnp.int32)).astype(jnp.float32) + 0.5
    ) * spacing
    return spacing, band_start, colatitude


def on_device(magnetic, kept_modes):
    radii_count, th_dev, ph_dev = (magnetic.shape[1], magnetic.shape[2], magnetic.shape[3])
    spacing, band_start, colatitude = band_geometry(th_dev)
    radius = (inner_radius + (jnp.arange(radii_count, dtype=jnp.float32) + 0.5) * spacing)[
        :, None, None
    ]
    inv_sin = (1.0 / jnp.sin(colatitude))[None, :, None]
    cotangent = (jnp.cos(colatitude) / jnp.sin(colatitude))[None, :, None]
    band_counts = lax.dynamic_slice_in_dim(kept_modes, band_start, th_dev)
    theta_pair = jnp.stack([magnetic[0], magnetic[2]])
    padded = extended(theta_pair, (("lat", 2),), 3)
    theta_diff = stencil_sum(padded, 2, th_dev)
    row_data = magnetic[:2].reshape(2 * radii_count * th_dev, ph_dev)
    lined = lax.all_to_all(row_data, "azim", split_axis=0, concat_axis=1, tiled=True)
    base_cos, base_sin = base_tables(lined.shape[1])
    rows_here = lined.shape[0]
    row_start = lax.axis_index("azim") * rows_here
    row_lat = (row_start + jnp.arange(rows_here, dtype=jnp.int32)) % th_dev
    row_kept = row_counts(band_counts, row_lat)
    azimuthal = spectral(lined, row_kept, base_cos, base_sin)
    flat_rows = lax.all_to_all(azimuthal, "azim", split_axis=1, concat_axis=0, tiled=True)
    azim_diff = flat_rows.reshape(2, radii_count, th_dev, ph_dev)
    b_polar = magnetic[1]
    b_azim = magnetic[2]
    j_radial = (
        theta_diff[1] + spacing * cotangent * b_azim - spacing * inv_sin * azim_diff[1]
    ) / radius
    j_polar = (spacing * inv_sin * azim_diff[0] - radial_diff(radius * b_azim)) / radius
    j_azim = (radial_diff(radius * b_polar) - theta_diff[0]) / radius
    return jnp.stack([j_radial, j_polar, j_azim])


CHUNKS = (7, 9)
LAST = (6, 3)
TO_Y = [(0, 2), (2, 0), (1, 3), (3, 1)]
TO_C = [(0, 1), (1, 0), (2, 3), (3, 2)]
TO_YC = [(0, 3), (3, 0), (1, 2), (2, 1)]
VMEM = 52 * 1024 * 1024
SHORT = pl.CostEstimate(flops=1, bytes_accessed=1, transcendentals=0)


def halves(table):
    high = table.astype(jnp.bfloat16)
    low = (table - high.astype(np.float64)).astype(jnp.bfloat16)
    return np.stack([high, low])


def mode_tables(lon_total):
    quarter = lon_total // 4

    def pair(modes, length):
        phase = (np.arange(length)[:, None] * modes[None, :] % lon_total) * (2.0 * np.pi / lon_total)
        forward = np.concatenate([np.cos(phase), np.sin(phase)], axis=1)
        inverse = np.concatenate([-np.sin(phase), np.cos(phase)], axis=1).T
        return halves(forward), halves(inverse)

    zero = 4 * np.arange(quarter // 2)
    two = zero + 2
    odd = 2 * np.arange(quarter) + 1
    mode_ids = np.concatenate([zero, zero, two, two, odd, odd]).astype(np.float32)[None, :]
    return pair(zero, quarter), pair(two, quarter), pair(odd, 2 * quarter), mode_ids


def triple_dot(value, table):
    high = value.astype(jnp.bfloat16)
    low = (value - high.astype(jnp.float32)).astype(jnp.bfloat16)
    dot = functools.partial(jnp.dot, preferred_element_type=jnp.float32)
    return dot(high, table[0]) + dot(high, table[1]) + dot(low, table[0])


def transform_kernel(place, own, across, beside, diagonal, kept, gain, modes, *refs):
    tables, (out_own, out_beside, *outs), held, sems = refs[:6], refs[6:-7], refs[-7:-1], refs[-1]
    copies = [pltpu.make_async_copy(table, ref, sems.at[i]) for i, (table, ref) in enumerate(zip(tables, held))]
    for copy in copies:
        copy.start()
    quarter = own.shape[-1]
    rows = across.shape[0] * across.shape[1]
    sign_y = (1 - 2 * place[0]).astype(jnp.float32)
    sign_c = (1 - 2 * place[1]).astype(jnp.float32)
    first = place[1] == 0
    a, b, c, d = (ref[...].reshape(rows, quarter) for ref in (own, across, beside, diagonal))
    near, far = a + b, c + d
    near_odd, far_odd = sign_y * (a - b), sign_y * (c - d)
    odd = jnp.concatenate([jnp.where(first, near_odd, far_odd), jnp.where(first, far_odd, near_odd)], axis=1)
    limit = kept[...]
    ids = modes[...]
    weight = jnp.where(ids < limit, ids, 0.0) * gain[...]

    def filtered(value, which, start):
        copies[2 * which].wait()
        spectrum = triple_dot(value, held[2 * which])
        copies[2 * which + 1].wait()
        return triple_dot(spectrum * weight[:, start : start + spectrum.shape[1]], held[2 * which + 1])

    even0 = filtered(near + far, 0, 0)
    even2 = sign_c * filtered(sign_c * (near - far), 1, quarter)
    odd_out = sign_y * filtered(odd, 2, 2 * quarter)
    left, right = odd_out[:, :quarter], odd_out[:, quarter:]
    odd_near, odd_far = jnp.where(first, left, right), jnp.where(first, right, left)
    even_near, even_far = even0 + even2, even0 - even2
    shape = out_own.shape
    out_own[...] = (even_near + odd_near).reshape(shape)
    out_beside[...] = (even_far + odd_far).reshape(shape)
    across, diagonal = (even_near - odd_near).reshape(shape), (even_far - odd_far).reshape(shape)
    if len(outs) == 1:
        outs[0][0], outs[0][1] = across, diagonal
    else:
        outs[0][...] = across
        at = 0
        for out in outs[1:]:
            out[...] = diagonal[at : at + out.shape[0]]
            at += out.shape[0]


def transform(place, magnetic, start, across, beside, diagonal, row_kept, row_gain, tables, cuts):
    depth, th_dev, quarter = across.shape[1:]
    zero, two, odd, mode_ids = tables
    whole = pl.BlockSpec(memory_space=pltpu.VMEM)
    rows = depth * th_dev
    half = magnetic.shape[1] // 2
    shape = (depth, th_dev, quarter)
    part = tuple(pl.Element(size) for size in shape)
    row_block = pl.BlockSpec((pl.Element(rows), pl.Element(1)), lambda i, p: (start * th_dev, 0))
    shapes = [shape, shape, (2,) + shape] if cuts is None else [shape] * 3 + [(cut, th_dev, quarter) for cut in cuts]
    if diagonal is None:
        diagonal, whole_diagonal = across, pl.BlockSpec((None,) + shape, lambda i, p: (1, 0, 0, 0))
        across_part = pl.BlockSpec((None,) + shape, lambda i, p: (0, 0, 0, 0))
    else:
        whole_diagonal, across_part = whole, pl.BlockSpec((None,) + shape, lambda i, p: (p[1], 0, 0, 0))
    grid_spec = pltpu.PrefetchScalarGridSpec(
        num_scalar_prefetch=1,
        grid=(1,),
        in_specs=[
            pl.BlockSpec((pl.Element(1),) + part, lambda i, p: (p[1], p[0] * half + start, 0, 0)),
            across_part,
            pl.BlockSpec(part, lambda i, p: (start, 0, 0)),
            whole_diagonal,
            row_block,
            row_block,
            whole,
        ]
        + [pl.BlockSpec(memory_space=pl.ANY)] * 6,
        out_specs=[whole] * len(shapes),
        scratch_shapes=[pltpu.VMEM(t.shape, jnp.bfloat16) for t in (*zero, *two, *odd)] + [pltpu.SemaphoreType.DMA((6,))],
    )
    return pl.pallas_call(
        transform_kernel,
        grid_spec=grid_spec,
        out_shape=[jax.ShapeDtypeStruct(shape, jnp.float32) for shape in shapes],
        compiler_params=pltpu.CompilerParams(vmem_limit_bytes=VMEM),
        cost_estimate=SHORT,
    )(place, magnetic, across, beside, diagonal, row_kept, row_gain, mode_ids, *zero, *two, *odd)


def edge_rows(magnetic):
    radii, th_dev, ph_dev = magnetic.shape[1:]
    edge = lambda at: pl.BlockSpec((None, radii, 8, ph_dev), lambda i: (2 * i, 0, at, 0))
    rows = pl.BlockSpec((None, 3, radii, ph_dev), lambda i: (i, 0, 0, 0))

    def kernel(top, bottom, last, first):
        for i in range(3):
            last[i] = bottom[:, 5 + i, :]
            first[i] = top[:, i, :]

    return pl.pallas_call(
        kernel,
        grid=(2,),
        in_specs=[edge(0), edge(th_dev // 8 - 1)],
        out_specs=[rows, rows],
        out_shape=[jax.ShapeDtypeStruct((2, 3, radii, ph_dev), jnp.float32)] * 2,
        compiler_params=pltpu.CompilerParams(vmem_limit_bytes=VMEM),
        cost_estimate=SHORT,
    )(magnetic, magnetic)


def copy_part(place, magnetic, start, depth):
    radii, th_dev, ph_dev = magnetic.shape[1:]

    def kernel(place, magnetic, out, sems):
        first = (1 - place[0]) * (radii // 2) + start
        copies = [
            pltpu.make_async_copy(magnetic.at[field, pl.ds(first, depth)], out.at[field], sems.at[field])
            for field in range(2)
        ]
        for copy in copies:
            copy.start()
        for copy in copies:
            copy.wait()

    return pl.pallas_call(
        kernel,
        grid_spec=pltpu.PrefetchScalarGridSpec(
            num_scalar_prefetch=1,
            grid=(1,),
            in_specs=[pl.BlockSpec(memory_space=pl.ANY)],
            out_specs=pl.BlockSpec(memory_space=pltpu.VMEM),
            scratch_shapes=[pltpu.SemaphoreType.DMA((2,))],
        ),
        out_shape=jax.ShapeDtypeStruct((2, depth, th_dev, ph_dev), jnp.float32),
        compiler_params=pltpu.CompilerParams(vmem_limit_bytes=VMEM),
        cost_estimate=SHORT,
    )(place, magnetic)


def local_part(place, magnetic, before, after, radius, inv_radius, cot, groups):
    width = 128
    radii, th_dev, ph_dev = magnetic.shape[1:]
    fixed = lambda *shape: pl.BlockSpec(shape, lambda i, p: (0, 0, 0))
    wide = lambda *lead: pl.BlockSpec(lead + (width,), lambda i, p: (0,) * len(lead) + (i,))
    weights = [stencil_coeffs[3 + offset] for offset in (1, 2, 3)]

    def kernel(place, field, before, after, radius, inv_radius, cot, *refs):
        azims, out, rows, layers = refs[:-3], *refs[-3:]
        inv = inv_radius[...]

        def theta(value, which):
            rows[:, 8 : 8 + th_dev, :] = value
            for i in range(3):
                rows[:, 5 + i, :] = before[which, i]
                rows[:, 8 + th_dev + i, :] = after[which, i]
            shifted = lambda offset: rows[:, 8 + offset : 8 + offset + th_dev, :]
            return sum(w * (shifted(o) - shifted(-o)) for o, w in enumerate(weights, 1))

        def radial(value):
            layers[3 : 3 + radii] = radius[...] * value
            shifted = lambda offset: layers[3 + offset : 3 + offset + radii]
            return sum(w * (shifted(o) - shifted(-o)) for o, w in enumerate(weights, 1))

        layers[:3] = jnp.zeros((3, th_dev, width), jnp.float32)
        layers[3 + radii :] = jnp.zeros((3, th_dev, width), jnp.float32)
        out[0] = (theta(field[2], 1) + cot[...] * field[2]) * inv
        out[1] = -radial(field[2]) * inv
        out[2] = (radial(field[1]) - theta(field[0], 0)) * inv
        for k, (_, _, own_half, start) in enumerate(groups):
            half = place[0] if own_half else 1 - place[0]
            here = pl.ds(half * (radii // 2) + start, azims[2 * k].shape[0])
            out[1 - place[1], here] += azims[2 * k][...]
            out[place[1], here] += azims[2 * k + 1][...]

    azims = [azim for own, crossed, _, _ in groups for azim in (own, crossed)]
    return pl.pallas_call(
        kernel,
        grid_spec=pltpu.PrefetchScalarGridSpec(
            num_scalar_prefetch=1,
            grid=(ph_dev // width,),
            in_specs=[
                wide(3, radii, th_dev),
                wide(2, 3, radii),
                wide(2, 3, radii),
                fixed(radii, 1, 1),
                fixed(radii, 1, 1),
                fixed(1, th_dev, 1),
            ]
            + [wide(*azim.shape[:-1]) for azim in azims],
            out_specs=wide(3, radii, th_dev),
            scratch_shapes=[
                pltpu.VMEM((radii, th_dev + 16, width), jnp.float32),
                pltpu.VMEM((radii + 6, th_dev, width), jnp.float32),
            ],
        ),
        out_shape=jax.ShapeDtypeStruct(magnetic.shape, jnp.float32),
        compiler_params=pltpu.CompilerParams(vmem_limit_bytes=VMEM),
        cost_estimate=SHORT,
    )(place, magnetic, before, after, radius, inv_radius, cot, *azims)


def add_one(place, current, azim, own_field, start):
    depth, th_dev, ph_dev = azim.shape
    half = current.shape[1] // 2
    part = lambda p: 1 - p[1] if own_field else p[1]
    block = pl.BlockSpec(
        (pl.Element(1), pl.Element(depth), pl.Element(th_dev), pl.Element(ph_dev)),
        lambda i, p: (part(p), (1 - p[0]) * half + start, 0, 0),
    )

    def kernel(place, base, azim, out):
        out[0] = base[0] + azim[...]

    return pl.pallas_call(
        kernel,
        grid_spec=pltpu.PrefetchScalarGridSpec(
            num_scalar_prefetch=1,
            grid=(1,),
            in_specs=[block, pl.BlockSpec(memory_space=pltpu.VMEM)],
            out_specs=block,
        ),
        out_shape=jax.ShapeDtypeStruct(current.shape, jnp.float32),
        input_output_aliases={1: 0},
        compiler_params=pltpu.CompilerParams(vmem_limit_bytes=VMEM // 6),
        cost_estimate=SHORT,
    )(place, current, azim)


def put_sum(place, current, base, azim, start):
    depth = azim.shape[0]
    half = current.shape[1] // 2
    whole = pl.BlockSpec(memory_space=pltpu.VMEM)

    def kernel(place, current, base, azim, out, total, sem):
        total[...] = base[...] + azim[...]
        copy = pltpu.make_async_copy(total, out.at[place[1], pl.ds((1 - place[0]) * half + start, depth)], sem)
        copy.start()
        copy.wait()

    return pl.pallas_call(
        kernel,
        grid_spec=pltpu.PrefetchScalarGridSpec(
            num_scalar_prefetch=1,
            grid=(1,),
            in_specs=[pl.BlockSpec(memory_space=pl.ANY), whole, whole],
            out_specs=pl.BlockSpec(memory_space=pl.ANY),
            scratch_shapes=[pltpu.VMEM(azim.shape, jnp.float32), pltpu.SemaphoreType.DMA],
        ),
        out_shape=jax.ShapeDtypeStruct(current.shape, jnp.float32),
        input_output_aliases={1: 0},
        compiler_params=pltpu.CompilerParams(vmem_limit_bytes=VMEM // 6),
        cost_estimate=SHORT,
    )(place, current, base, azim)


def after(first, *then):
    return lax.optimization_barrier((first, then))[1]


def on_four(magnetic, kept_modes):
    radii, th_dev, ph_dev = (magnetic.shape[1], magnetic.shape[2], magnetic.shape[3])
    half = radii // 2
    unit = half // sum(CHUNKS)
    depths = [unit * part for part in CHUNKS]
    last_cuts = [unit * part for part in LAST]
    starts = [sum(depths[:k]) for k in range(len(depths))]
    index = lax.axis_index("azim")
    y, c = index // 2, index % 2
    place = jnp.stack([y, c]).astype(jnp.int32)
    send = lambda value, pairs: lax.ppermute(value, "azim", pairs)

    def cut(source, field, start, length):
        return lax.dynamic_slice(source, (field, start, 0, 0), (1, length, th_dev, ph_dev))[0]

    both = copy_part(place, magnetic, 0, depths[0])
    (source,) = after(both, magnetic)
    arrived = [send(both, TO_Y)]
    last, first = edge_rows(source)
    (source,) = after((last, first), source)
    crossing = []
    for start, depth in zip(starts[1:], depths[1:]):
        to_c = cut(source, 1 - c, (1 - y) * half + start, depth)
        (source,) = after(to_c, source)
        crossing.append(send(to_c, TO_C))
    to_c = cut(source, 1 - c, y * half, half)
    (source,) = after(to_c, source)
    beside = send(to_c, TO_C)
    for start, depth, crossed in zip(starts[1:], depths[1:], crossing):
        both = jnp.stack([cut(source, c, (1 - y) * half + start, depth), crossed])
        arrived.append(send(both, TO_Y))
    lat_size = lax.axis_size("lat")
    up = [(i, i + 1) for i in range(lat_size - 1)]
    down = [(i + 1, i) for i in range(lat_size - 1)]
    north, south = lax.ppermute(last, "lat", up), lax.ppermute(first, "lat", down)

    spacing, band_start, colatitude = band_geometry(th_dev)
    radius = (inner_radius + (jnp.arange(radii, dtype=jnp.float32) + 0.5) * spacing)[:, None, None]
    inv_radius = 1.0 / radius
    inv_sin = 1.0 / jnp.sin(colatitude)
    cot = spacing * (jnp.cos(colatitude) / jnp.sin(colatitude))[None, :, None]
    sign_c = (1 - 2 * c).astype(jnp.float32)
    row_gain = (sign_c * spacing * 0.5 / ph_dev) * inv_sin[None, :] * inv_radius[:, 0]
    row_gain = lax.dynamic_slice_in_dim(row_gain, y * half, half).reshape(half * th_dev, 1)
    band_counts = lax.dynamic_slice_in_dim(kept_modes, band_start, th_dev).astype(jnp.float32)
    row_kept = jnp.broadcast_to(band_counts[None, :], (half, th_dev)).reshape(half * th_dev, 1)

    tables = mode_tables(4 * ph_dev)
    mine, from_c, returned = [], [], []
    for k, start in enumerate(starts):
        across, diagonal = arrived[k], None
        (row_gain,) = after(from_c[-1] if k > 0 else (north, south), row_gain)
        if k == 0:
            diagonal = send(cut(across, 1 - c, 0, depths[k]), TO_C)
        else:
            (across,) = after(mine[-1], across)
        cuts = None if k + 1 < len(starts) else last_cuts
        out, to_c, to_y, *to_yc = transform(
            place, magnetic, start, across, beside, diagonal, row_kept, row_gain, tables, cuts
        )
        mine.append(out)
        if k + 1 < len(starts):
            (to_c,) = after(arrived[k + 1], to_c)
        from_c.append(send(to_c, TO_C))
        returned.append(send(to_y, TO_Y))
    final = [(returned.pop(), True, starts[-1])]
    for i, value in enumerate(to_yc):
        final.append((send(value, TO_YC), False, starts[-1] + sum(last_cuts[:i])))

    groups = [(own, crossed, True, start) for own, crossed, start in zip(mine, from_c, starts)]
    for value, start in zip(returned, starts):
        groups.append((value[0], send(value[1], TO_C), False, start))
    north, south = after(mine[-1], north, south)
    current = local_part(place, magnetic, north, south, radius, inv_radius, cot, groups)
    azim, _, start = final[-1]
    base = cut(current, c, (1 - y) * half + start, azim.shape[0])
    (current,) = after(base, current)
    for value, own_field, at in final[:-1]:
        current = add_one(place, current, value, own_field, at)
    return put_sum(place, current, base, azim, start)


def solution(mesh):
    placed = (P(None, None, "lat", "azim"), P())

    def run(magnetic, kept_modes):
        radii, th_dev, ph_dev = magnetic.shape[1:]
        four = lax.axis_size("azim") == 4 and radii % (2 * sum(CHUNKS)) == 0 and ph_dev % 256 == 0
        four = four and th_dev % 8 == 0
        return (on_four if four else on_device)(magnetic, kept_modes)

    return jax.shard_map(
        run,
        mesh=mesh,
        in_specs=placed,
        out_specs=P(None, None, "lat", "azim"),
        check_vma=False,
    )
```

```python
import functools
import math

import jax
import jax.numpy as jnp
import numpy as np
from jax import lax
from jax.experimental import pallas as pl
from jax.experimental.pallas import tpu as pltpu
from jax.sharding import PartitionSpec as P

MB = 128


inner_radius = 0.7
stencil_coeffs = (-1.0 / 60.0, 3.0 / 20.0, -3.0 / 4.0, 0.0, 3.0 / 4.0, -3.0 / 20.0, 1.0 / 60.0)


def extended(value, sides, width):
    for axis, dim in sides:
        size, length = (lax.axis_size(axis), value.shape[dim])
        up = [(i, (i + 1) % size) for i in range(size - 1)]
        down = [(j, i) for i, j in up]
        last = lax.slice_in_dim(value, length - width, length, axis=dim)
        first = lax.slice_in_dim(value, 0, width, axis=dim)
        before = lax.ppermute(last, axis, up)
        after = lax.ppermute(first, axis, down)
        value = jnp.concatenate([before, value, after], axis=dim)
    return value


def stencil_sum(padded, split_axis, length):
    total = jnp.zeros(lax.slice_in_dim(padded, 3, 3 + length, axis=split_axis).shape, jnp.float32)
    for offset in range(-3, 4):
        if offset != 0:
            total = total + stencil_coeffs[offset + 3] * lax.slice_in_dim(
                padded, 3 + offset, 3 + offset + length, axis=split_axis
            )
    return total


def radial_diff(values):
    widths = [(0, 0)] * values.ndim
    widths[0] = (3, 3)
    return stencil_sum(jnp.pad(values, widths), 0, values.shape[0])


def row_counts(band_counts, row_lat):
    lat_ids = jnp.arange(band_counts.shape[0], dtype=jnp.int32)
    match = row_lat[:, None] == lat_ids[None, :]
    return jnp.sum(jnp.where(match, band_counts[None, :], 0), axis=1)


def base_tables(lon_total):
    columns = jnp.arange(lon_total, dtype=jnp.int32)
    mode_ids = jnp.arange(MB, dtype=jnp.int32)
    phase = (mode_ids[:, None] * columns[None, :] % lon_total).astype(jnp.float32) * (
        2.0 * math.pi / lon_total
    )
    return (jnp.cos(phase), jnp.sin(phase))


def spectral(row_data, row_kept, base_cos, base_sin):
    lon_total = row_data.shape[1]
    block_count = (jnp.max(row_kept) + MB - 1) // MB
    columns = jnp.arange(lon_total, dtype=jnp.int32)

    def block_step(block, total):
        mode_ids = block * MB + jnp.arange(MB, dtype=jnp.int32)
        offset_phase = (block * MB * columns % lon_total).astype(jnp.float32) * (
            2.0 * math.pi / lon_total
        )
        offset_cos = jnp.cos(offset_phase)[None, :]
        offset_sin = jnp.sin(offset_phase)[None, :]
        cos_rows = base_cos * offset_cos - base_sin * offset_sin
        sin_rows = base_sin * offset_cos + base_cos * offset_sin
        table = jnp.concatenate([cos_rows, sin_rows], axis=0)
        spectrum = lax.dot_general(
            row_data,
            table,
            (((1,), (1,)), ((), ())),
            precision=lax.Precision.HIGHEST,
            preferred_element_type=jnp.float32,
        )
        weight = jnp.where(mode_ids[None, :] < row_kept[:, None], mode_ids[None, :], 0).astype(
            jnp.float32
        ) * (2.0 / lon_total)
        scaled = jnp.concatenate([spectrum[:, MB:] * weight, -spectrum[:, :MB] * weight], axis=1)
        return total + jnp.dot(
            scaled, table, precision=lax.Precision.HIGHEST, preferred_element_type=jnp.float32
        )

    return lax.fori_loop(0, block_count, block_step, jnp.zeros_like(row_data))


def band_geometry(th_dev):
    lat_total = th_dev * lax.axis_size("lat")
    spacing = math.pi / lat_total
    band_start = lax.axis_index("lat") * th_dev
    colatitude = (
        (band_start + jnp.arange(th_dev, dtype=jnp.int32)).astype(jnp.float32) + 0.5
    ) * spacing
    return spacing, band_start, colatitude


def on_device(magnetic, kept_modes):
    radii_count, th_dev, ph_dev = (magnetic.shape[1], magnetic.shape[2], magnetic.shape[3])
    spacing, band_start, colatitude = band_geometry(th_dev)
    radius = (inner_radius + (jnp.arange(radii_count, dtype=jnp.float32) + 0.5) * spacing)[
        :, None, None
    ]
    inv_sin = (1.0 / jnp.sin(colatitude))[None, :, None]
    cotangent = (jnp.cos(colatitude) / jnp.sin(colatitude))[None, :, None]
    band_counts = lax.dynamic_slice_in_dim(kept_modes, band_start, th_dev)
    theta_pair = jnp.stack([magnetic[0], magnetic[2]])
    padded = extended(theta_pair, (("lat", 2),), 3)
    theta_diff = stencil_sum(padded, 2, th_dev)
    row_data = magnetic[:2].reshape(2 * radii_count * th_dev, ph_dev)
    lined = lax.all_to_all(row_data, "azim", split_axis=0, concat_axis=1, tiled=True)
    base_cos, base_sin = base_tables(lined.shape[1])
    rows_here = lined.shape[0]
    row_start = lax.axis_index("azim") * rows_here
    row_lat = (row_start + jnp.arange(rows_here, dtype=jnp.int32)) % th_dev
    row_kept = row_counts(band_counts, row_lat)
    azimuthal = spectral(lined, row_kept, base_cos, base_sin)
    flat_rows = lax.all_to_all(azimuthal, "azim", split_axis=1, concat_axis=0, tiled=True)
    azim_diff = flat_rows.reshape(2, radii_count, th_dev, ph_dev)
    b_polar = magnetic[1]
    b_azim = magnetic[2]
    j_radial = (
        theta_diff[1] + spacing * cotangent * b_azim - spacing * inv_sin * azim_diff[1]
    ) / radius
    j_polar = (spacing * inv_sin * azim_diff[0] - radial_diff(radius * b_azim)) / radius
    j_azim = (radial_diff(radius * b_polar) - theta_diff[0]) / radius
    return jnp.stack([j_radial, j_polar, j_azim])


CHUNKS = (7, 9)
LAST = (6, 3)
TO_Y = [(0, 2), (2, 0), (1, 3), (3, 1)]
TO_C = [(0, 1), (1, 0), (2, 3), (3, 2)]
TO_YC = [(0, 3), (3, 0), (1, 2), (2, 1)]
VMEM = 52 * 1024 * 1024
SHORT = pl.CostEstimate(flops=1, bytes_accessed=1, transcendentals=0)


def split_table(table, count):
    parts = []
    for _ in range(count):
        parts.append(table.astype(jnp.bfloat16))
        table = table - parts[-1].astype(np.float64)
    return np.stack(parts)


def mode_tables(lon_total):
    quarter = lon_total // 4

    def pair(modes, length):
        phase = (np.arange(length)[:, None] * modes[None, :] % lon_total) * (2.0 * np.pi / lon_total)
        forward = np.concatenate([np.cos(phase), np.sin(phase)], axis=1)
        inverse = np.concatenate([-np.sin(phase), np.cos(phase)], axis=1).T
        return split_table(forward, 3), split_table(inverse, 2)

    zero = 4 * np.arange(quarter // 2)
    two = zero + 2
    odd = 2 * np.arange(quarter) + 1
    mode_ids = np.concatenate([zero, zero, two, two, odd, odd]).astype(np.float32)[None, :]
    return pair(zero, quarter), pair(two, quarter), pair(odd, 2 * quarter), mode_ids


def split_dot(value, table):
    count = table.shape[0]
    parts = []
    for _ in range(count):
        parts.append(value.astype(jnp.bfloat16))
        value = value - parts[-1].astype(jnp.float32)
    total = None
    for order in reversed(range(count)):
        for i in range(order + 1):
            term = jnp.dot(parts[i], table[order - i], preferred_element_type=jnp.float32)
            total = term if total is None else total + term
    return total


def transform_kernel(place, own, across, beside, diagonal, kept, gain, modes, *refs):
    tables, (out_own, out_beside, *outs), held, sems = refs[:6], refs[6:-7], refs[-7:-1], refs[-1]
    copies = [pltpu.make_async_copy(table, ref, sems.at[i]) for i, (table, ref) in enumerate(zip(tables, held))]
    for copy in copies:
        copy.start()
    quarter = own.shape[-1]
    rows = across.shape[0] * across.shape[1]
    sign_y = (1 - 2 * place[0]).astype(jnp.float32)
    sign_c = (1 - 2 * place[1]).astype(jnp.float32)
    first = place[1] == 0
    a, b, c, d = (ref[...].reshape(rows, quarter) for ref in (own, across, beside, diagonal))
    near, far = a + b, c + d
    near_odd, far_odd = sign_y * (a - b), sign_y * (c - d)
    odd = jnp.concatenate([jnp.where(first, near_odd, far_odd), jnp.where(first, far_odd, near_odd)], axis=1)
    limit = kept[...]
    ids = modes[...]
    weight = jnp.where(ids < limit, ids, 0.0) * gain[...]

    def filtered(value, which, start):
        copies[2 * which].wait()
        spectrum = split_dot(value, held[2 * which])
        copies[2 * which + 1].wait()
        return split_dot(spectrum * weight[:, start : start + spectrum.shape[1]], held[2 * which + 1])

    even0 = filtered(near + far, 0, 0)
    even2 = sign_c * filtered(sign_c * (near - far), 1, quarter)
    odd_out = sign_y * filtered(odd, 2, 2 * quarter)
    left, right = odd_out[:, :quarter], odd_out[:, quarter:]
    odd_near, odd_far = jnp.where(first, left, right), jnp.where(first, right, left)
    even_near, even_far = even0 + even2, even0 - even2
    shape = out_own.shape
    out_own[...] = (even_near + odd_near).reshape(shape)
    out_beside[...] = (even_far + odd_far).reshape(shape)
    across, diagonal = (even_near - odd_near).reshape(shape), (even_far - odd_far).reshape(shape)
    if len(outs) == 1:
        outs[0][0], outs[0][1] = across, diagonal
    else:
        outs[0][...] = across
        at = 0
        for out in outs[1:]:
            out[...] = diagonal[at : at + out.shape[0]]
            at += out.shape[0]


def transform(place, magnetic, start, across, beside, diagonal, row_kept, row_gain, tables, cuts):
    depth, th_dev, quarter = across.shape[1:]
    zero, two, odd, mode_ids = tables
    whole = pl.BlockSpec(memory_space=pltpu.VMEM)
    rows = depth * th_dev
    half = magnetic.shape[1] // 2
    shape = (depth, th_dev, quarter)
    part = tuple(pl.Element(size) for size in shape)
    row_block = pl.BlockSpec((pl.Element(rows), pl.Element(1)), lambda i, p: (start * th_dev, 0))
    shapes = [shape, shape, (2,) + shape] if cuts is None else [shape] * 3 + [(cut, th_dev, quarter) for cut in cuts]
    if diagonal is None:
        diagonal, whole_diagonal = across, pl.BlockSpec((None,) + shape, lambda i, p: (1, 0, 0, 0))
        across_part = pl.BlockSpec((None,) + shape, lambda i, p: (0, 0, 0, 0))
    else:
        whole_diagonal, across_part = whole, pl.BlockSpec((None,) + shape, lambda i, p: (p[1], 0, 0, 0))
    grid_spec = pltpu.PrefetchScalarGridSpec(
        num_scalar_prefetch=1,
        grid=(1,),
        in_specs=[
            pl.BlockSpec((pl.Element(1),) + part, lambda i, p: (p[1], p[0] * half + start, 0, 0)),
            across_part,
            pl.BlockSpec(part, lambda i, p: (start, 0, 0)),
            whole_diagonal,
            row_block,
            row_block,
            whole,
        ]
        + [pl.BlockSpec(memory_space=pl.ANY)] * 6,
        out_specs=[whole] * len(shapes),
        scratch_shapes=[pltpu.VMEM(t.shape, jnp.bfloat16) for t in (*zero, *two, *odd)] + [pltpu.SemaphoreType.DMA((6,))],
    )
    return pl.pallas_call(
        transform_kernel,
        grid_spec=grid_spec,
        out_shape=[jax.ShapeDtypeStruct(shape, jnp.float32) for shape in shapes],
        compiler_params=pltpu.CompilerParams(vmem_limit_bytes=VMEM),
        cost_estimate=SHORT,
    )(place, magnetic, across, beside, diagonal, row_kept, row_gain, mode_ids, *zero, *two, *odd)


def edge_rows(magnetic):
    radii, th_dev, ph_dev = magnetic.shape[1:]
    edge = lambda at: pl.BlockSpec((None, radii, 8, ph_dev), lambda i: (2 * i, 0, at, 0))
    rows = pl.BlockSpec((None, 3, radii, ph_dev), lambda i: (i, 0, 0, 0))

    def kernel(top, bottom, last, first):
        for i in range(3):
            last[i] = bottom[:, 5 + i, :]
            first[i] = top[:, i, :]

    return pl.pallas_call(
        kernel,
        grid=(2,),
        in_specs=[edge(0), edge(th_dev // 8 - 1)],
        out_specs=[rows, rows],
        out_shape=[jax.ShapeDtypeStruct((2, 3, radii, ph_dev), jnp.float32)] * 2,
        compiler_params=pltpu.CompilerParams(vmem_limit_bytes=VMEM),
        cost_estimate=SHORT,
    )(magnetic, magnetic)


def copy_part(place, magnetic, start, depth):
    radii, th_dev, ph_dev = magnetic.shape[1:]

    def kernel(place, magnetic, out, sems):
        first = (1 - place[0]) * (radii // 2) + start
        copies = [
            pltpu.make_async_copy(magnetic.at[field, pl.ds(first, depth)], out.at[field], sems.at[field])
            for field in range(2)
        ]
        for copy in copies:
            copy.start()
        for copy in copies:
            copy.wait()

    return pl.pallas_call(
        kernel,
        grid_spec=pltpu.PrefetchScalarGridSpec(
            num_scalar_prefetch=1,
            grid=(1,),
            in_specs=[pl.BlockSpec(memory_space=pl.ANY)],
            out_specs=pl.BlockSpec(memory_space=pltpu.VMEM),
            scratch_shapes=[pltpu.SemaphoreType.DMA((2,))],
        ),
        out_shape=jax.ShapeDtypeStruct((2, depth, th_dev, ph_dev), jnp.float32),
        compiler_params=pltpu.CompilerParams(vmem_limit_bytes=VMEM),
        cost_estimate=SHORT,
    )(place, magnetic)


def local_part(place, magnetic, before, after, radius, inv_radius, cot, groups):
    width = 128
    radii, th_dev, ph_dev = magnetic.shape[1:]
    fixed = lambda *shape: pl.BlockSpec(shape, lambda i, p: (0, 0, 0))
    wide = lambda *lead: pl.BlockSpec(lead + (width,), lambda i, p: (0,) * len(lead) + (i,))
    weights = [stencil_coeffs[3 + offset] for offset in (1, 2, 3)]

    def kernel(place, field, before, after, radius, inv_radius, cot, *refs):
        azims, out, rows, layers = refs[:-3], *refs[-3:]
        inv = inv_radius[...]

        def theta(value, which):
            rows[:, 8 : 8 + th_dev, :] = value
            for i in range(3):
                rows[:, 5 + i, :] = before[which, i]
                rows[:, 8 + th_dev + i, :] = after[which, i]
            shifted = lambda offset: rows[:, 8 + offset : 8 + offset + th_dev, :]
            return sum(w * (shifted(o) - shifted(-o)) for o, w in enumerate(weights, 1))

        def radial(value):
            layers[3 : 3 + radii] = radius[...] * value
            shifted = lambda offset: layers[3 + offset : 3 + offset + radii]
            return sum(w * (shifted(o) - shifted(-o)) for o, w in enumerate(weights, 1))

        layers[:3] = jnp.zeros((3, th_dev, width), jnp.float32)
        layers[3 + radii :] = jnp.zeros((3, th_dev, width), jnp.float32)
        out[0] = (theta(field[2], 1) + cot[...] * field[2]) * inv
        out[1] = -radial(field[2]) * inv
        out[2] = (radial(field[1]) - theta(field[0], 0)) * inv
        for k, (_, _, own_half, start) in enumerate(groups):
            half = place[0] if own_half else 1 - place[0]
            here = pl.ds(half * (radii // 2) + start, azims[2 * k].shape[0])
            out[1 - place[1], here] += azims[2 * k][...]
            out[place[1], here] += azims[2 * k + 1][...]

    azims = [azim for own, crossed, _, _ in groups for azim in (own, crossed)]
    return pl.pallas_call(
        kernel,
        grid_spec=pltpu.PrefetchScalarGridSpec(
            num_scalar_prefetch=1,
            grid=(ph_dev // width,),
            in_specs=[
                wide(3, radii, th_dev),
                wide(2, 3, radii),
                wide(2, 3, radii),
                fixed(radii, 1, 1),
                fixed(radii, 1, 1),
                fixed(1, th_dev, 1),
            ]
            + [wide(*azim.shape[:-1]) for azim in azims],
            out_specs=wide(3, radii, th_dev),
            scratch_shapes=[
                pltpu.VMEM((radii, th_dev + 16, width), jnp.float32),
                pltpu.VMEM((radii + 6, th_dev, width), jnp.float32),
            ],
        ),
        out_shape=jax.ShapeDtypeStruct(magnetic.shape, jnp.float32),
        compiler_params=pltpu.CompilerParams(vmem_limit_bytes=VMEM),
        cost_estimate=SHORT,
    )(place, magnetic, before, after, radius, inv_radius, cot, *azims)


def add_one(place, current, azim, own_field, start):
    depth, th_dev, ph_dev = azim.shape
    half = current.shape[1] // 2
    part = lambda p: 1 - p[1] if own_field else p[1]
    block = pl.BlockSpec(
        (pl.Element(1), pl.Element(depth), pl.Element(th_dev), pl.Element(ph_dev)),
        lambda i, p: (part(p), (1 - p[0]) * half + start, 0, 0),
    )

    def kernel(place, base, azim, out):
        out[0] = base[0] + azim[...]

    return pl.pallas_call(
        kernel,
        grid_spec=pltpu.PrefetchScalarGridSpec(
            num_scalar_prefetch=1,
            grid=(1,),
            in_specs=[block, pl.BlockSpec(memory_space=pltpu.VMEM)],
            out_specs=block,
        ),
        out_shape=jax.ShapeDtypeStruct(current.shape, jnp.float32),
        input_output_aliases={1: 0},
        compiler_params=pltpu.CompilerParams(vmem_limit_bytes=VMEM // 6),
        cost_estimate=SHORT,
    )(place, current, azim)


def put_sum(place, current, base, azim, start):
    depth = azim.shape[0]
    half = current.shape[1] // 2
    whole = pl.BlockSpec(memory_space=pltpu.VMEM)

    def kernel(place, current, base, azim, out, total, sem):
        total[...] = base[...] + azim[...]
        copy = pltpu.make_async_copy(total, out.at[place[1], pl.ds((1 - place[0]) * half + start, depth)], sem)
        copy.start()
        copy.wait()

    return pl.pallas_call(
        kernel,
        grid_spec=pltpu.PrefetchScalarGridSpec(
            num_scalar_prefetch=1,
            grid=(1,),
            in_specs=[pl.BlockSpec(memory_space=pl.ANY), whole, whole],
            out_specs=pl.BlockSpec(memory_space=pl.ANY),
            scratch_shapes=[pltpu.VMEM(azim.shape, jnp.float32), pltpu.SemaphoreType.DMA],
        ),
        out_shape=jax.ShapeDtypeStruct(current.shape, jnp.float32),
        input_output_aliases={1: 0},
        compiler_params=pltpu.CompilerParams(vmem_limit_bytes=VMEM // 6),
        cost_estimate=SHORT,
    )(place, current, base, azim)


def after(first, *then):
    return lax.optimization_barrier((first, then))[1]


def on_four(magnetic, kept_modes):
    radii, th_dev, ph_dev = (magnetic.shape[1], magnetic.shape[2], magnetic.shape[3])
    half = radii // 2
    unit = half // sum(CHUNKS)
    depths = [unit * part for part in CHUNKS]
    last_cuts = [unit * part for part in LAST]
    starts = [sum(depths[:k]) for k in range(len(depths))]
    index = lax.axis_index("azim")
    y, c = index // 2, index % 2
    place = jnp.stack([y, c]).astype(jnp.int32)
    send = lambda value, pairs: lax.ppermute(value, "azim", pairs)

    def cut(source, field, start, length):
        return lax.dynamic_slice(source, (field, start, 0, 0), (1, length, th_dev, ph_dev))[0]

    both = copy_part(place, magnetic, 0, depths[0])
    (source,) = after(both, magnetic)
    arrived = [send(both, TO_Y)]
    last, first = edge_rows(source)
    (source,) = after((last, first), source)
    crossing = []
    for start, depth in zip(starts[1:], depths[1:]):
        to_c = cut(source, 1 - c, (1 - y) * half + start, depth)
        (source,) = after(to_c, source)
        crossing.append(send(to_c, TO_C))
    to_c = cut(source, 1 - c, y * half, half)
    (source,) = after(to_c, source)
    beside = send(to_c, TO_C)
    for start, depth, crossed in zip(starts[1:], depths[1:], crossing):
        both = jnp.stack([cut(source, c, (1 - y) * half + start, depth), crossed])
        arrived.append(send(both, TO_Y))
    lat_size = lax.axis_size("lat")
    up = [(i, i + 1) for i in range(lat_size - 1)]
    down = [(i + 1, i) for i in range(lat_size - 1)]
    north, south = lax.ppermute(last, "lat", up), lax.ppermute(first, "lat", down)

    spacing, band_start, colatitude = band_geometry(th_dev)
    radius = (inner_radius + (jnp.arange(radii, dtype=jnp.float32) + 0.5) * spacing)[:, None, None]
    inv_radius = 1.0 / radius
    inv_sin = 1.0 / jnp.sin(colatitude)
    cot = spacing * (jnp.cos(colatitude) / jnp.sin(colatitude))[None, :, None]
    sign_c = (1 - 2 * c).astype(jnp.float32)
    row_gain = (sign_c * spacing * 0.5 / ph_dev) * inv_sin[None, :] * inv_radius[:, 0]
    row_gain = lax.dynamic_slice_in_dim(row_gain, y * half, half).reshape(half * th_dev, 1)
    band_counts = lax.dynamic_slice_in_dim(kept_modes, band_start, th_dev).astype(jnp.float32)
    row_kept = jnp.broadcast_to(band_counts[None, :], (half, th_dev)).reshape(half * th_dev, 1)

    tables = mode_tables(4 * ph_dev)
    mine, from_c, returned = [], [], []
    for k, start in enumerate(starts):
        across, diagonal = arrived[k], None
        (row_gain,) = after(from_c[-1] if k > 0 else (north, south), row_gain)
        if k == 0:
            diagonal = send(cut(across, 1 - c, 0, depths[k]), TO_C)
        else:
            (across,) = after(mine[-1], across)
        cuts = None if k + 1 < len(starts) else last_cuts
        out, to_c, to_y, *to_yc = transform(
            place, magnetic, start, across, beside, diagonal, row_kept, row_gain, tables, cuts
        )
        mine.append(out)
        if k + 1 < len(starts):
            (to_c,) = after(arrived[k + 1], to_c)
        from_c.append(send(to_c, TO_C))
        returned.append(send(to_y, TO_Y))
    final = [(returned.pop(), True, starts[-1])]
    for i, value in enumerate(to_yc):
        final.append((send(value, TO_YC), False, starts[-1] + sum(last_cuts[:i])))

    groups = [(own, crossed, True, start) for own, crossed, start in zip(mine, from_c, starts)]
    for value, start in zip(returned, starts):
        groups.append((value[0], send(value[1], TO_C), False, start))
    north, south = after(mine[-1], north, south)
    current = local_part(place, magnetic, north, south, radius, inv_radius, cot, groups)
    azim, _, start = final[-1]
    base = cut(current, c, (1 - y) * half + start, azim.shape[0])
    (current,) = after(base, current)
    for value, own_field, at in final[:-1]:
        current = add_one(place, current, value, own_field, at)
    return put_sum(place, current, base, azim, start)


def solution(mesh):
    placed = (P(None, None, "lat", "azim"), P())

    def run(magnetic, kept_modes):
        radii, th_dev, ph_dev = magnetic.shape[1:]
        four = lax.axis_size("azim") == 4 and radii % (2 * sum(CHUNKS)) == 0 and ph_dev % 256 == 0
        four = four and th_dev % 8 == 0
        return (on_four if four else on_device)(magnetic, kept_modes)

    return jax.shard_map(
        run,
        mesh=mesh,
        in_specs=placed,
        out_specs=P(None, None, "lat", "azim"),
        check_vma=False,
    )
```

```python
import functools
import math

import jax
import jax.numpy as jnp
import numpy as np
from jax import lax
from jax.experimental import pallas as pl
from jax.experimental.pallas import tpu as pltpu
from jax.sharding import PartitionSpec as P

MB = 128


inner_radius = 0.7
stencil_coeffs = (-1.0 / 60.0, 3.0 / 20.0, -3.0 / 4.0, 0.0, 3.0 / 4.0, -3.0 / 20.0, 1.0 / 60.0)


def extended(value, sides, width):
    for axis, dim in sides:
        size, length = (lax.axis_size(axis), value.shape[dim])
        up = [(i, (i + 1) % size) for i in range(size - 1)]
        down = [(j, i) for i, j in up]
        last = lax.slice_in_dim(value, length - width, length, axis=dim)
        first = lax.slice_in_dim(value, 0, width, axis=dim)
        before = lax.ppermute(last, axis, up)
        after = lax.ppermute(first, axis, down)
        value = jnp.concatenate([before, value, after], axis=dim)
    return value


def stencil_sum(padded, split_axis, length):
    total = jnp.zeros(lax.slice_in_dim(padded, 3, 3 + length, axis=split_axis).shape, jnp.float32)
    for offset in range(-3, 4):
        if offset != 0:
            total = total + stencil_coeffs[offset + 3] * lax.slice_in_dim(
                padded, 3 + offset, 3 + offset + length, axis=split_axis
            )
    return total


def radial_diff(values):
    widths = [(0, 0)] * values.ndim
    widths[0] = (3, 3)
    return stencil_sum(jnp.pad(values, widths), 0, values.shape[0])


def row_counts(band_counts, row_lat):
    lat_ids = jnp.arange(band_counts.shape[0], dtype=jnp.int32)
    match = row_lat[:, None] == lat_ids[None, :]
    return jnp.sum(jnp.where(match, band_counts[None, :], 0), axis=1)


def base_tables(lon_total):
    columns = jnp.arange(lon_total, dtype=jnp.int32)
    mode_ids = jnp.arange(MB, dtype=jnp.int32)
    phase = (mode_ids[:, None] * columns[None, :] % lon_total).astype(jnp.float32) * (
        2.0 * math.pi / lon_total
    )
    return (jnp.cos(phase), jnp.sin(phase))


def spectral(row_data, row_kept, base_cos, base_sin):
    lon_total = row_data.shape[1]
    block_count = (jnp.max(row_kept) + MB - 1) // MB
    columns = jnp.arange(lon_total, dtype=jnp.int32)

    def block_step(block, total):
        mode_ids = block * MB + jnp.arange(MB, dtype=jnp.int32)
        offset_phase = (block * MB * columns % lon_total).astype(jnp.float32) * (
            2.0 * math.pi / lon_total
        )
        offset_cos = jnp.cos(offset_phase)[None, :]
        offset_sin = jnp.sin(offset_phase)[None, :]
        cos_rows = base_cos * offset_cos - base_sin * offset_sin
        sin_rows = base_sin * offset_cos + base_cos * offset_sin
        table = jnp.concatenate([cos_rows, sin_rows], axis=0)
        spectrum = lax.dot_general(
            row_data,
            table,
            (((1,), (1,)), ((), ())),
            precision=lax.Precision.HIGHEST,
            preferred_element_type=jnp.float32,
        )
        weight = jnp.where(mode_ids[None, :] < row_kept[:, None], mode_ids[None, :], 0).astype(
            jnp.float32
        ) * (2.0 / lon_total)
        scaled = jnp.concatenate([spectrum[:, MB:] * weight, -spectrum[:, :MB] * weight], axis=1)
        return total + jnp.dot(
            scaled, table, precision=lax.Precision.HIGHEST, preferred_element_type=jnp.float32
        )

    return lax.fori_loop(0, block_count, block_step, jnp.zeros_like(row_data))


def band_geometry(th_dev):
    lat_total = th_dev * lax.axis_size("lat")
    spacing = math.pi / lat_total
    band_start = lax.axis_index("lat") * th_dev
    colatitude = (
        (band_start + jnp.arange(th_dev, dtype=jnp.int32)).astype(jnp.float32) + 0.5
    ) * spacing
    return spacing, band_start, colatitude


def on_device(magnetic, kept_modes):
    radii_count, th_dev, ph_dev = (magnetic.shape[1], magnetic.shape[2], magnetic.shape[3])
    spacing, band_start, colatitude = band_geometry(th_dev)
    radius = (inner_radius + (jnp.arange(radii_count, dtype=jnp.float32) + 0.5) * spacing)[
        :, None, None
    ]
    inv_sin = (1.0 / jnp.sin(colatitude))[None, :, None]
    cotangent = (jnp.cos(colatitude) / jnp.sin(colatitude))[None, :, None]
    band_counts = lax.dynamic_slice_in_dim(kept_modes, band_start, th_dev)
    theta_pair = jnp.stack([magnetic[0], magnetic[2]])
    padded = extended(theta_pair, (("lat", 2),), 3)
    theta_diff = stencil_sum(padded, 2, th_dev)
    row_data = magnetic[:2].reshape(2 * radii_count * th_dev, ph_dev)
    lined = lax.all_to_all(row_data, "azim", split_axis=0, concat_axis=1, tiled=True)
    base_cos, base_sin = base_tables(lined.shape[1])
    rows_here = lined.shape[0]
    row_start = lax.axis_index("azim") * rows_here
    row_lat = (row_start + jnp.arange(rows_here, dtype=jnp.int32)) % th_dev
    row_kept = row_counts(band_counts, row_lat)
    azimuthal = spectral(lined, row_kept, base_cos, base_sin)
    flat_rows = lax.all_to_all(azimuthal, "azim", split_axis=1, concat_axis=0, tiled=True)
    azim_diff = flat_rows.reshape(2, radii_count, th_dev, ph_dev)
    b_polar = magnetic[1]
    b_azim = magnetic[2]
    j_radial = (
        theta_diff[1] + spacing * cotangent * b_azim - spacing * inv_sin * azim_diff[1]
    ) / radius
    j_polar = (spacing * inv_sin * azim_diff[0] - radial_diff(radius * b_azim)) / radius
    j_azim = (radial_diff(radius * b_polar) - theta_diff[0]) / radius
    return jnp.stack([j_radial, j_polar, j_azim])


CHUNKS = (7, 9)
LAST = (6, 3)
TO_Y = [(0, 2), (2, 0), (1, 3), (3, 1)]
TO_C = [(0, 1), (1, 0), (2, 3), (3, 2)]
TO_YC = [(0, 3), (3, 0), (1, 2), (2, 1)]
VMEM = 50 * 1024 * 1024
SHORT = pl.CostEstimate(flops=1, bytes_accessed=1, transcendentals=0)


def split_table(table, count):
    parts = []
    for _ in range(count):
        parts.append(table.astype(jnp.bfloat16))
        table = table - parts[-1].astype(np.float64)
    return np.concatenate(parts)


def mode_tables(lon_total):
    quarter = lon_total // 4

    def pair(modes, length):
        phase = (np.arange(length)[:, None] * modes[None, :] % lon_total) * (2.0 * np.pi / lon_total)
        forward = np.concatenate([np.cos(phase), np.sin(phase)], axis=1)
        inverse = np.concatenate([-np.sin(phase), np.cos(phase)], axis=1).T
        return split_table(forward, 3), split_table(inverse, 2)

    zero = 8 * np.arange(quarter // 4)
    four = zero + 4
    two = 4 * np.arange(quarter // 2) + 2
    odd = 2 * np.arange(quarter) + 1
    mode_ids = np.concatenate([zero, zero, four, four, two, two, odd, odd]).astype(np.float32)[None, :]
    return pair(zero, quarter // 2), pair(four, quarter // 2), pair(two, quarter), pair(odd, 2 * quarter), mode_ids


def split_dot(value, table):
    depth = value.shape[1]
    count = table.shape[0] // depth
    parts = []
    for _ in range(count):
        parts.append(value.astype(jnp.bfloat16))
        value = value - parts[-1].astype(jnp.float32)
    total = None
    for order in reversed(range(count)):
        row = jnp.concatenate(parts[order::-1], axis=1)
        term = jnp.dot(row, table[: (order + 1) * depth], preferred_element_type=jnp.float32)
        total = term if total is None else total + term
    return total


def transform_kernel(place, own, across, beside, diagonal, kept, gain, modes, *refs):
    tables, (out_own, out_beside, *outs), held, sems = refs[:8], refs[8:-9], refs[-9:-1], refs[-1]
    copies = [pltpu.make_async_copy(table, ref, sems.at[i]) for i, (table, ref) in enumerate(zip(tables, held))]
    for copy in copies:
        copy.start()
    quarter = own.shape[-1]
    rows = across.shape[0] * across.shape[1]
    sign_y = (1 - 2 * place[0]).astype(jnp.float32)
    sign_c = (1 - 2 * place[1]).astype(jnp.float32)
    first = place[1] == 0
    a, b, c, d = (ref[...].reshape(rows, quarter) for ref in (own, across, beside, diagonal))
    near, far = a + b, c + d
    near_odd, far_odd = sign_y * (a - b), sign_y * (c - d)
    odd = jnp.concatenate([jnp.where(first, near_odd, far_odd), jnp.where(first, far_odd, near_odd)], axis=1)
    limit = kept[...]
    ids = modes[...]
    weight = jnp.where(ids < limit, ids, 0.0) * gain[...]

    def filtered(value, which, start):
        copies[2 * which].wait()
        spectrum = split_dot(value, held[2 * which])
        copies[2 * which + 1].wait()
        return split_dot(spectrum * weight[:, start : start + spectrum.shape[1]], held[2 * which + 1])

    lower, upper = (near + far)[:, : quarter // 2], (near + far)[:, quarter // 2 :]
    zero, four = filtered(lower + upper, 0, 0), filtered(lower - upper, 1, quarter // 2)
    even0 = jnp.concatenate([zero + four, zero - four], axis=1)
    even2 = sign_c * filtered(sign_c * (near - far), 2, quarter)
    odd_out = sign_y * filtered(odd, 3, 2 * quarter)
    left, right = odd_out[:, :quarter], odd_out[:, quarter:]
    odd_near, odd_far = jnp.where(first, left, right), jnp.where(first, right, left)
    even_near, even_far = even0 + even2, even0 - even2
    shape = out_own.shape
    out_own[...] = (even_near + odd_near).reshape(shape)
    out_beside[...] = (even_far + odd_far).reshape(shape)
    across, diagonal = (even_near - odd_near).reshape(shape), (even_far - odd_far).reshape(shape)
    if len(outs) == 1:
        outs[0][0], outs[0][1] = across, diagonal
    else:
        outs[0][...] = across
        at = 0
        for out in outs[1:]:
            out[...] = diagonal[at : at + out.shape[0]]
            at += out.shape[0]


def transform(place, magnetic, start, across, beside, diagonal, row_kept, row_gain, tables, cuts):
    depth, th_dev, quarter = across.shape[1:]
    *pairs, mode_ids = tables
    flat = [table for pair in pairs for table in pair]
    whole = pl.BlockSpec(memory_space=pltpu.VMEM)
    rows = depth * th_dev
    half = magnetic.shape[1] // 2
    shape = (depth, th_dev, quarter)
    part = tuple(pl.Element(size) for size in shape)
    row_block = pl.BlockSpec((pl.Element(rows), pl.Element(1)), lambda i, p: (start * th_dev, 0))
    shapes = [shape, shape, (2,) + shape] if cuts is None else [shape] * 3 + [(cut, th_dev, quarter) for cut in cuts]
    if diagonal is None:
        diagonal, whole_diagonal = across, pl.BlockSpec((None,) + shape, lambda i, p: (1, 0, 0, 0))
        across_part = pl.BlockSpec((None,) + shape, lambda i, p: (0, 0, 0, 0))
    else:
        whole_diagonal, across_part = whole, pl.BlockSpec((None,) + shape, lambda i, p: (p[1], 0, 0, 0))
    grid_spec = pltpu.PrefetchScalarGridSpec(
        num_scalar_prefetch=1,
        grid=(1,),
        in_specs=[
            pl.BlockSpec((pl.Element(1),) + part, lambda i, p: (p[1], p[0] * half + start, 0, 0)),
            across_part,
            pl.BlockSpec(part, lambda i, p: (start, 0, 0)),
            whole_diagonal,
            row_block,
            row_block,
            whole,
        ]
        + [pl.BlockSpec(memory_space=pl.ANY)] * len(flat),
        out_specs=[whole] * len(shapes),
        scratch_shapes=[pltpu.VMEM(t.shape, jnp.bfloat16) for t in flat] + [pltpu.SemaphoreType.DMA((len(flat),))],
    )
    return pl.pallas_call(
        transform_kernel,
        grid_spec=grid_spec,
        out_shape=[jax.ShapeDtypeStruct(shape, jnp.float32) for shape in shapes],
        compiler_params=pltpu.CompilerParams(vmem_limit_bytes=VMEM),
        cost_estimate=SHORT,
    )(place, magnetic, across, beside, diagonal, row_kept, row_gain, mode_ids, *flat)


def edge_rows(magnetic):
    radii, th_dev, ph_dev = magnetic.shape[1:]
    edge = lambda at: pl.BlockSpec((None, radii, 8, ph_dev), lambda i: (2 * i, 0, at, 0))
    rows = pl.BlockSpec((None, 3, radii, ph_dev), lambda i: (i, 0, 0, 0))

    def kernel(top, bottom, last, first):
        for i in range(3):
            last[i] = bottom[:, 5 + i, :]
            first[i] = top[:, i, :]

    return pl.pallas_call(
        kernel,
        grid=(2,),
        in_specs=[edge(0), edge(th_dev // 8 - 1)],
        out_specs=[rows, rows],
        out_shape=[jax.ShapeDtypeStruct((2, 3, radii, ph_dev), jnp.float32)] * 2,
        compiler_params=pltpu.CompilerParams(vmem_limit_bytes=VMEM),
        cost_estimate=SHORT,
    )(magnetic, magnetic)


def copy_part(place, magnetic, start, depth):
    radii, th_dev, ph_dev = magnetic.shape[1:]

    def kernel(place, magnetic, out, sems):
        first = (1 - place[0]) * (radii // 2) + start
        copies = [
            pltpu.make_async_copy(magnetic.at[field, pl.ds(first, depth)], out.at[field], sems.at[field])
            for field in range(2)
        ]
        for copy in copies:
            copy.start()
        for copy in copies:
            copy.wait()

    return pl.pallas_call(
        kernel,
        grid_spec=pltpu.PrefetchScalarGridSpec(
            num_scalar_prefetch=1,
            grid=(1,),
            in_specs=[pl.BlockSpec(memory_space=pl.ANY)],
            out_specs=pl.BlockSpec(memory_space=pltpu.VMEM),
            scratch_shapes=[pltpu.SemaphoreType.DMA((2,))],
        ),
        out_shape=jax.ShapeDtypeStruct((2, depth, th_dev, ph_dev), jnp.float32),
        compiler_params=pltpu.CompilerParams(vmem_limit_bytes=VMEM),
        cost_estimate=SHORT,
    )(place, magnetic)


def local_part(place, magnetic, before, after, radius, inv_radius, cot, groups):
    width = 128
    radii, th_dev, ph_dev = magnetic.shape[1:]
    fixed = lambda *shape: pl.BlockSpec(shape, lambda i, p: (0, 0, 0))
    wide = lambda *lead: pl.BlockSpec(lead + (width,), lambda i, p: (0,) * len(lead) + (i,))
    weights = [stencil_coeffs[3 + offset] for offset in (1, 2, 3)]

    def kernel(place, field, before, after, radius, inv_radius, cot, *refs):
        azims, out, rows, layers = refs[:-3], *refs[-3:]
        inv = inv_radius[...]

        def theta(value, which):
            rows[:, 8 : 8 + th_dev, :] = value
            for i in range(3):
                rows[:, 5 + i, :] = before[which, i]
                rows[:, 8 + th_dev + i, :] = after[which, i]
            shifted = lambda offset: rows[:, 8 + offset : 8 + offset + th_dev, :]
            return sum(w * (shifted(o) - shifted(-o)) for o, w in enumerate(weights, 1))

        def radial(value):
            layers[3 : 3 + radii] = radius[...] * value
            shifted = lambda offset: layers[3 + offset : 3 + offset + radii]
            return sum(w * (shifted(o) - shifted(-o)) for o, w in enumerate(weights, 1))

        layers[:3] = jnp.zeros((3, th_dev, width), jnp.float32)
        layers[3 + radii :] = jnp.zeros((3, th_dev, width), jnp.float32)
        out[0] = (theta(field[2], 1) + cot[...] * field[2]) * inv
        out[1] = -radial(field[2]) * inv
        out[2] = (radial(field[1]) - theta(field[0], 0)) * inv
        for k, (_, _, own_half, start) in enumerate(groups):
            half = place[0] if own_half else 1 - place[0]
            here = pl.ds(half * (radii // 2) + start, azims[2 * k].shape[0])
            out[1 - place[1], here] += azims[2 * k][...]
            out[place[1], here] += azims[2 * k + 1][...]

    azims = [azim for own, crossed, _, _ in groups for azim in (own, crossed)]
    return pl.pallas_call(
        kernel,
        grid_spec=pltpu.PrefetchScalarGridSpec(
            num_scalar_prefetch=1,
            grid=(ph_dev // width,),
            in_specs=[
                wide(3, radii, th_dev),
                wide(2, 3, radii),
                wide(2, 3, radii),
                fixed(radii, 1, 1),
                fixed(radii, 1, 1),
                fixed(1, th_dev, 1),
            ]
            + [wide(*azim.shape[:-1]) for azim in azims],
            out_specs=wide(3, radii, th_dev),
            scratch_shapes=[
                pltpu.VMEM((radii, th_dev + 16, width), jnp.float32),
                pltpu.VMEM((radii + 6, th_dev, width), jnp.float32),
            ],
        ),
        out_shape=jax.ShapeDtypeStruct(magnetic.shape, jnp.float32),
        compiler_params=pltpu.CompilerParams(vmem_limit_bytes=VMEM),
        cost_estimate=SHORT,
    )(place, magnetic, before, after, radius, inv_radius, cot, *azims)


def add_one(place, current, azim, own_field, start):
    depth, th_dev, ph_dev = azim.shape
    half = current.shape[1] // 2
    part = lambda p: 1 - p[1] if own_field else p[1]
    block = pl.BlockSpec(
        (pl.Element(1), pl.Element(depth), pl.Element(th_dev), pl.Element(ph_dev)),
        lambda i, p: (part(p), (1 - p[0]) * half + start, 0, 0),
    )

    def kernel(place, base, azim, out):
        out[0] = base[0] + azim[...]

    return pl.pallas_call(
        kernel,
        grid_spec=pltpu.PrefetchScalarGridSpec(
            num_scalar_prefetch=1,
            grid=(1,),
            in_specs=[block, pl.BlockSpec(memory_space=pltpu.VMEM)],
            out_specs=block,
        ),
        out_shape=jax.ShapeDtypeStruct(current.shape, jnp.float32),
        input_output_aliases={1: 0},
        compiler_params=pltpu.CompilerParams(vmem_limit_bytes=VMEM // 6),
        cost_estimate=SHORT,
    )(place, current, azim)


def put_sum(place, current, base, azim, start):
    depth = azim.shape[0]
    half = current.shape[1] // 2
    whole = pl.BlockSpec(memory_space=pltpu.VMEM)

    def kernel(place, current, base, azim, out, total, sem):
        total[...] = base[...] + azim[...]
        copy = pltpu.make_async_copy(total, out.at[place[1], pl.ds((1 - place[0]) * half + start, depth)], sem)
        copy.start()
        copy.wait()

    return pl.pallas_call(
        kernel,
        grid_spec=pltpu.PrefetchScalarGridSpec(
            num_scalar_prefetch=1,
            grid=(1,),
            in_specs=[pl.BlockSpec(memory_space=pl.ANY), whole, whole],
            out_specs=pl.BlockSpec(memory_space=pl.ANY),
            scratch_shapes=[pltpu.VMEM(azim.shape, jnp.float32), pltpu.SemaphoreType.DMA],
        ),
        out_shape=jax.ShapeDtypeStruct(current.shape, jnp.float32),
        input_output_aliases={1: 0},
        compiler_params=pltpu.CompilerParams(vmem_limit_bytes=VMEM // 6),
        cost_estimate=SHORT,
    )(place, current, base, azim)


def after(first, *then):
    return lax.optimization_barrier((first, then))[1]


def on_four(magnetic, kept_modes):
    radii, th_dev, ph_dev = (magnetic.shape[1], magnetic.shape[2], magnetic.shape[3])
    half = radii // 2
    unit = half // sum(CHUNKS)
    depths = [unit * part for part in CHUNKS]
    last_cuts = [unit * part for part in LAST]
    starts = [sum(depths[:k]) for k in range(len(depths))]
    index = lax.axis_index("azim")
    y, c = index // 2, index % 2
    place = jnp.stack([y, c]).astype(jnp.int32)
    send = lambda value, pairs: lax.ppermute(value, "azim", pairs)

    def cut(source, field, start, length):
        return lax.dynamic_slice(source, (field, start, 0, 0), (1, length, th_dev, ph_dev))[0]

    both = copy_part(place, magnetic, 0, depths[0])
    (source,) = after(both, magnetic)
    arrived = [send(both, TO_Y)]
    last, first = edge_rows(source)
    (source,) = after((last, first), source)
    crossing = []
    for start, depth in zip(starts[1:], depths[1:]):
        to_c = cut(source, 1 - c, (1 - y) * half + start, depth)
        (source,) = after(to_c, source)
        crossing.append(send(to_c, TO_C))
    to_c = cut(source, 1 - c, y * half, half)
    (source,) = after(to_c, source)
    beside = send(to_c, TO_C)
    for start, depth, crossed in zip(starts[1:], depths[1:], crossing):
        both = jnp.stack([cut(source, c, (1 - y) * half + start, depth), crossed])
        arrived.append(send(both, TO_Y))
    lat_size = lax.axis_size("lat")
    up = [(i, i + 1) for i in range(lat_size - 1)]
    down = [(i + 1, i) for i in range(lat_size - 1)]
    north, south = lax.ppermute(last, "lat", up), lax.ppermute(first, "lat", down)

    spacing, band_start, colatitude = band_geometry(th_dev)
    radius = (inner_radius + (jnp.arange(radii, dtype=jnp.float32) + 0.5) * spacing)[:, None, None]
    inv_radius = 1.0 / radius
    inv_sin = 1.0 / jnp.sin(colatitude)
    cot = spacing * (jnp.cos(colatitude) / jnp.sin(colatitude))[None, :, None]
    sign_c = (1 - 2 * c).astype(jnp.float32)
    row_gain = (sign_c * spacing * 0.5 / ph_dev) * inv_sin[None, :] * inv_radius[:, 0]
    row_gain = lax.dynamic_slice_in_dim(row_gain, y * half, half).reshape(half * th_dev, 1)
    band_counts = lax.dynamic_slice_in_dim(kept_modes, band_start, th_dev).astype(jnp.float32)
    row_kept = jnp.broadcast_to(band_counts[None, :], (half, th_dev)).reshape(half * th_dev, 1)

    tables = mode_tables(4 * ph_dev)
    mine, from_c, returned = [], [], []
    for k, start in enumerate(starts):
        across, diagonal = arrived[k], None
        (row_gain,) = after(from_c[-1] if k > 0 else (north, south), row_gain)
        if k == 0:
            diagonal = send(cut(across, 1 - c, 0, depths[k]), TO_C)
        else:
            (across,) = after(mine[-1], across)
        cuts = None if k + 1 < len(starts) else last_cuts
        out, to_c, to_y, *to_yc = transform(
            place, magnetic, start, across, beside, diagonal, row_kept, row_gain, tables, cuts
        )
        mine.append(out)
        if k + 1 < len(starts):
            (to_c,) = after(arrived[k + 1], to_c)
        from_c.append(send(to_c, TO_C))
        returned.append(send(to_y, TO_Y))
    final = [(returned.pop(), True, starts[-1])]
    for i, value in enumerate(to_yc):
        final.append((send(value, TO_YC), False, starts[-1] + sum(last_cuts[:i])))

    groups = [(own, crossed, True, start) for own, crossed, start in zip(mine, from_c, starts)]
    for value, start in zip(returned, starts):
        groups.append((value[0], send(value[1], TO_C), False, start))
    north, south = after(mine[-1], north, south)
    current = local_part(place, magnetic, north, south, radius, inv_radius, cot, groups)
    azim, _, start = final[-1]
    base = cut(current, c, (1 - y) * half + start, azim.shape[0])
    (current,) = after(base, current)
    for value, own_field, at in final[:-1]:
        current = add_one(place, current, value, own_field, at)
    return put_sum(place, current, base, azim, start)


def solution(mesh):
    placed = (P(None, None, "lat", "azim"), P())

    def run(magnetic, kept_modes):
        radii, th_dev, ph_dev = magnetic.shape[1:]
        four = lax.axis_size("azim") == 4 and radii % (2 * sum(CHUNKS)) == 0 and ph_dev % 256 == 0
        four = four and th_dev % 8 == 0
        return (on_four if four else on_device)(magnetic, kept_modes)

    return jax.shard_map(
        run,
        mesh=mesh,
        in_specs=placed,
        out_specs=P(None, None, "lat", "azim"),
        check_vma=False,
    )
```
